32 devices in a mesh: section: 4 (over y, x), dp: 8 (over z, core).
Axes of the slice: x: 2, y: 2, z: 4, core: 2. Of those that a mesh axis runs over, the one named last changes fastest.
Arguments:
- features: bfloat16 [32, 16, 16, 256], P('dp', 'section'), may hold values from -6 to 6
- tower_class: float32 [4, 2304, 256], P('section', 'dp'), may hold values from -0.125 to 0.125
- bias_class: float32 [4, 256], replicated, may hold values from -3 to 3
- tower_boxes: float32 [4, 2304, 256], P('section', 'dp'), may hold values from -0.125 to 0.125
- bias_boxes: float32 [4, 256], replicated, may hold values from -3 to 3
- head_class: float32 [2304, 720], P('dp', 'section'), may hold values from -0.125 to 0.125
- head_class_bias: float32 [720], replicated, may hold values from -4.6 to -3
- head_boxes: float32 [2304, 36], P('dp', 'section'), may hold values from -0.125 to 0.125
- head_boxes_bias: float32 [36], replicated, may hold values from -3 to 3
- anchor_state: int32 [32, 16, 144], P('dp'), may hold values from 0 to 2, as said below
- class_labels: int32 [32, 16, 144], P('dp'), may hold values from 0 to 79
- box_targets: float32 [32, 16, 576], P('dp'), may hold values from -6 to 6
- valid_rows: int32 [32], P('dp'), may hold values from 4 to 16
Outputs:
- grad_features: bfloat16 [32, 16, 16, 256], P('dp', 'section')
- grad_tower_class: float32 [4, 2304, 256], P('section', 'dp')
- grad_bias_class: float32 [4, 256], replicated
- grad_tower_boxes: float32 [4, 2304, 256], P('section', 'dp')
- grad_bias_boxes: float32 [4, 256], replicated
- grad_head_class: float32 [2304, 720], P('dp', 'section')
- grad_head_class_bias: float32 [720], replicated
- grad_head_boxes: float32 [2304, 36], P('dp', 'section')
- grad_head_boxes_bias: float32 [36], replicated
The draws below stay inside these ranges and needn't reach their ends.
Inputs may be any that keep to these rules, and one draw needn't show every extreme that they name: `anchor_state`: 0 marks a negative anchor, 1 a positive one, 2 an ignored one.
All inputs are finite; a program needn't handle non-finite values.
Results may differ from the reference program's by a relative error of at most 0.018.
Values may be sent and summed in bfloat16 or wider, within the bound.
A program may use at most 256 MiB of HBM per device.

```python
import jax
import jax.numpy as jnp
from jax import lax

C = 256
K = 80
A = 9
LAYERS = 4
CLS = 720
BOX = 36
TILE = 16
TILES = 32


def draw_anchor_state(key, part):
    key = jax.random.fold_in(key, 5)
    shape_all = (TILES, TILE, TILE * A)
    ticket = jax.random.randint(key, shape_all, 0, 1000)
    position = lax.broadcasted_iota(jnp.int32, shape_all, 0)
    positive_rate = 40 + 80 * position // TILES
    return jnp.where(ticket < positive_rate, 1, jnp.where(ticket < positive_rate + 100, 2, 0)).astype(jnp.int32)


def place_ends(result, rng, low, largest):
    longest = result.shape.index(max(result.shape))
    spots = []
    for shift in (0, 1):
        where = [jax.random.randint(jax.random.fold_in(rng, axis), (), 0, length) for axis, length in enumerate(result.shape)]
        where[longest] = (where[longest] + shift) % result.shape[longest]
        spots.append(tuple(where))
    return result.at[spots[0]].set(low).at[spots[1]].set(largest)


def block_levels(stream_key, shape, cuts, least, high):
    def one(axis_at, blocks):
        steps = jax.random.uniform(jax.random.fold_in(jax.random.fold_in(stream_key, 6), axis_at), (blocks,), jnp.float32, least / len(cuts), high / len(cuts))
        return jnp.repeat(jnp.exp(steps), shape[axis_at] // blocks).reshape((-1,) + (1,) * (len(shape) - axis_at - 1))

    level = one(*cuts[0])
    for cut in cuts[1:]:
        level = level * one(*cut)
    return level


def bell_draw(own_key, dims, width, limit, cuts=(), held_as=jnp.bfloat16):
    result = width * jax.random.normal(own_key, dims, jnp.float32)
    if cuts:
        result = result * block_levels(own_key, dims, cuts, -0.22, 0.18)
    return jnp.clip(result, -limit, limit).astype(held_as)


def setup_inputs(seed: int = 0) -> dict:
    keys = jax.random.split(jax.random.key(seed), 14)
    return {
        "features": bell_draw(keys[0], (TILES, TILE, TILE, C), 1.0, 6.0, ((0, 8), (1, 4))),
        "tower_class": bell_draw(keys[1], (LAYERS, 9 * C, C), (9 * C) ** -0.5, 0.125, ((0, 4), (1, 8)), jnp.float32),
        "bias_class": bell_draw(keys[2], (LAYERS, C), 0.5, 3.0, (), jnp.float32),
        "tower_boxes": bell_draw(keys[3], (LAYERS, 9 * C, C), (9 * C) ** -0.5, 0.125, ((0, 4), (1, 8)), jnp.float32),
        "bias_boxes": bell_draw(keys[4], (LAYERS, C), 0.5, 3.0, (), jnp.float32),
        "head_class": bell_draw(keys[5], (9 * C, CLS), (9 * C) ** -0.5, 0.125, ((0, 8), (1, 4)), jnp.float32),
        "head_class_bias": jnp.clip(jax.random.uniform(keys[6], (CLS,), jnp.float32, -4.6, -3.0), -4.6, -3.0),
        "head_boxes": bell_draw(keys[7], (9 * C, BOX), (9 * C) ** -0.5, 0.125, ((0, 8), (1, 4)), jnp.float32),
        "head_boxes_bias": bell_draw(keys[8], (BOX,), 0.5, 3.0, (), jnp.float32),
        "anchor_state": draw_anchor_state(jax.random.fold_in(keys[13], 71), 0),
        "class_labels": place_ends(jax.random.randint(keys[10], (TILES, TILE, TILE * A), 0, K), jax.random.fold_in(keys[10], 1), 0, K - 1).astype(jnp.int32),
        "box_targets": bell_draw(keys[11], (TILES, TILE, TILE * BOX), 1.0, 6.0, ((0, 8),), jnp.float32),
        "valid_rows": place_ends(jax.random.randint(keys[12], (TILES,), TILE // 4, TILE + 1), jax.random.fold_in(keys[12], 1), TILE // 4, TILE).astype(jnp.int32),
    }


huber_beta = 1.0 / 9.0

@jax.custom_vjp
def low(v):
    return lax.optimization_barrier(v.astype(jnp.bfloat16)).astype(jnp.float32)

@jax.custom_vjp
def low_back(v):
    return v

def low_keep(v):
    return (low(v), None)

def low_pass(kept, grad):
    return (grad,)

def back_keep(v):
    return (v, None)

def back_low(kept, grad):
    return (low(grad),)
low.defvjp(low_keep, low_pass)
low_back.defvjp(back_keep, back_low)

def convolve(values, weight):
    kernel = weight.reshape(3, 3, values.shape[-1], weight.shape[-1])
    return lax.conv_general_dilated(values, kernel, (1, 1), 'SAME', dimension_numbers=('NHWC', 'HWIO', 'NHWC'), precision=lax.Precision.HIGHEST)

def anchor_masks(anchor_state, valid_rows):
    tile_count = anchor_state.shape[0]
    anchor_kind = anchor_state.reshape(tile_count, TILE, TILE, A)
    row_index = lax.broadcasted_iota(jnp.int32, (tile_count, TILE, 1, 1), 1)
    inside = row_index < valid_rows.reshape(tile_count, 1, 1, 1)
    positive = jnp.logical_and(anchor_kind == 1, inside).astype(jnp.float32)
    counted = jnp.logical_and(anchor_kind != 2, inside).astype(jnp.float32)
    return (positive, counted)

def head_loss(logits, box_values, positive, counted, class_labels, box_targets, normalizer):
    tile_count = logits.shape[0]
    scores = logits.reshape(tile_count, TILE, TILE, A, K)
    labels = class_labels.reshape(tile_count, TILE, TILE, A, 1)
    classes = lax.broadcasted_iota(jnp.int32, (1, 1, 1, 1, K), 4)
    target = (labels == classes).astype(jnp.float32) * positive[..., None]
    chance = jax.nn.sigmoid(scores)
    entropy = jax.nn.softplus(scores) - target * scores
    agreement = chance * target + (1.0 - chance) * (1.0 - target)
    balance = 0.25 * target + 0.75 * (1.0 - target)
    focal_terms = balance * (1.0 - agreement) ** 2 * entropy
    focal_sum = jnp.sum(focal_terms * counted[..., None])
    offsets = box_values.reshape(tile_count, TILE, TILE, A, 4) - box_targets.reshape(tile_count, TILE, TILE, A, 4)
    spread = jnp.abs(offsets)
    huber_terms = jnp.where(spread < huber_beta, 0.5 * offsets * offsets / huber_beta, spread - 0.5 * huber_beta)
    box_sum = jnp.sum(huber_terms * positive[..., None])
    return (focal_sum + box_sum) / normalizer

def reference(features, tower_class, bias_class, tower_boxes, bias_boxes, head_class, head_class_bias, head_boxes, head_boxes_bias, anchor_state, class_labels, box_targets, valid_rows):
    positive, counted = anchor_masks(anchor_state, valid_rows)
    normalizer = jnp.maximum(jnp.sum(positive), 1.0)
    inputs = features.astype(jnp.float32)

    def forward(inputs, tower_class, bias_class, tower_boxes, bias_boxes, head_class, head_class_bias, head_boxes, head_boxes_bias):
        branch_class = inputs
        branch_boxes = inputs
        for layer_index in range(LAYERS):
            if layer_index > 0:
                branch_class = low(low_back(branch_class))
                branch_boxes = low(low_back(branch_boxes))
            branch_class = jax.nn.gelu(low_back(convolve(branch_class, low(tower_class[layer_index])) + bias_class[layer_index]))
            branch_boxes = jax.nn.gelu(low_back(convolve(branch_boxes, low(tower_boxes[layer_index])) + bias_boxes[layer_index]))
        logits = low_back(convolve(low(branch_class), low(head_class)) + head_class_bias)
        box_values = low_back(convolve(low(branch_boxes), low(head_boxes)) + head_boxes_bias)
        return head_loss(logits, box_values, positive, counted, class_labels, box_targets, normalizer)
    total_loss, pullback = jax.vjp(forward, inputs, tower_class, bias_class, tower_boxes, bias_boxes, head_class, head_class_bias, head_boxes, head_boxes_bias)
    gradients = pullback(jnp.ones_like(total_loss))
    return (gradients[0].astype(jnp.bfloat16), gradients[1], gradients[2], gradients[3], gradients[4], gradients[5], gradients[6], gradients[7], gradients[8])
```

```python
import functools
import math
from types import SimpleNamespace

import jax
import jax.numpy as jnp
import numpy as np
from jax import lax
from jax.experimental import pallas as pl
from jax.experimental.pallas import tpu as pltpu
from jax.sharding import PartitionSpec as P

K = 80
A = 9
LAYERS = 4
TILE = 16
MICRO = 4


huber_beta = 1.0 / 9.0

F32 = jnp.float32
BF16 = jnp.bfloat16
MESH = pl.DeviceIdType.MESH
GELU_C = math.sqrt(2.0 / math.pi)

SECTIONS = 4
PLANES = 4
CORES = 2
CH = 256
PX = TILE * TILE
ROWS = 288
HALF = ROWS // 2
PACK = ROWS + HALF
LANES = 128
TAIL = 64
HEAD = SECTIONS * (LANES + TAIL)
LAB = 256
TGT = 640
DEEP = 9 * CH


def head_layout(width):
    per = width // SECTIONS
    columns = np.full((HEAD,), -1)
    for s in range(SECTIONS):
        main = min(per, LANES)
        columns[s * LANES : s * LANES + main] = s * per + np.arange(main)
        rest = per - main
        at = SECTIONS * LANES + s * TAIL
        columns[at : at + rest] = s * per + main + np.arange(rest)
    return columns


def constants(class_width, boxes_width):
    classes, boxes = head_layout(class_width), head_layout(boxes_width)
    spread = np.zeros((2, LAB, HEAD), np.float32)
    targets = np.zeros((TGT, HEAD), np.float32)
    for j in range(TILE):
        for col in range(HEAD):
            if classes[col] >= 0:
                spread[0, j * A + classes[col] // K, col] = 1
            if boxes[col] >= 0:
                spread[1, j * A + boxes[col] // 4, col] = 1
                targets[j * boxes_width + boxes[col], col] = 1
    pixel = np.arange(PX)[:, None] % TILE
    mask_lab = (np.arange(LAB)[None, :] // A == pixel) & (np.arange(LAB)[None, :] < TILE * A)
    mask_tgt = (np.arange(TGT)[None, :] // boxes_width == pixel) & (np.arange(TGT)[None, :] < TILE * boxes_width)
    label = np.where(classes >= 0, classes % K, -9).astype(np.float32)[None, :] + 2.0
    bf = lambda v: jnp.asarray(v.astype(np.float32), BF16)
    return bf(spread), bf(targets), bf(mask_lab), bf(mask_tgt), jnp.asarray(np.repeat(label, 8, 0))


def dot(a, b):
    return jnp.dot(a, b, preferred_element_type=F32)


def dot_nt(a, b):
    return lax.dot_general(a, b, (((1,), (1,)), ((), ())), preferred_element_type=F32)


def put_shifted(ref, t, v, order, width):
    col = lax.broadcasted_iota(jnp.int32, v.shape, 0) % TILE
    before = jnp.where(col == 0, 0.0, pltpu.roll(v, 1, 0))
    after = jnp.where(col == TILE - 1, 0.0, pltpu.roll(v, PX - 1, 0))
    blocks = (before, v, after) if order > 0 else (after, v, before)
    for s, block in enumerate(blocks):
        ref[t, TILE : TILE + PX, s * width : (s + 1) * width] = block.astype(BF16)


def shifted_rows(ref, r, lanes=slice(None)):
    return ref[:, TILE * r : TILE * r + PX, lanes].reshape(2 * PX, -1)


def swap_halves(p, q):
    p, q = p.astype(F32), q.astype(F32)
    low = lax.broadcasted_iota(jnp.int32, p.shape, 1) < TAIL
    p_turned, q_turned = pltpu.roll(p, TAIL, 1), pltpu.roll(q, TAIL, 1)
    return jnp.where(low, p, q_turned), jnp.where(low, p_turned, q)


def forward_layer(m, l):
    z = sum(dot(shifted_rows(m.act3, r), m.w[l, 3 * CH * r : 3 * CH * (r + 1), :]) for r in range(3))
    z = z + m.bias[m.role, l : l + 1, 0:CH]
    for t in range(2):
        zt = z[t * PX : (t + 1) * PX]
        square = zt * zt
        th = jnp.tanh(GELU_C * (zt + 0.044715 * zt * square))
        half = 0.5 * (1.0 + th)
        a = zt * half
        m.slope[l, t * PX : (t + 1) * PX, :] = half + (0.5 * GELU_C) * zt * (1.0 - th * th) * (
            1.0 + (3 * 0.044715) * square
        )
        put_shifted(m.act3, t, a, 1, CH)
        m.act_t[l + 1, :, t * PX : (t + 1) * PX] = a.T.astype(BF16)


def head_forward(m):
    for n in range(0, HEAD, 256):
        m.logits[:, n : n + 256] = sum(
            dot(shifted_rows(m.act3, r), m.wh[3 * CH * r : 3 * CH * (r + 1), n : n + 256]) for r in range(3)
        )


def expand(row, mask):
    lanes = row.shape[-1]
    return jnp.broadcast_to(row[:, None, :], (TILE, TILE, lanes)).reshape(PX, lanes) * mask[...].astype(F32)


def prepare_loss(m):
    for t, lab in enumerate((m.lab, m.lab_in)):
        codes = expand(lab[:, 0:LAB], m.mask_lab).astype(BF16)
        m.code[t * PX : (t + 1) * PX, :] = dot(codes, m.spread[m.role])

    @pl.when(m.role == 1)
    def _():
        for t, lab in enumerate((m.lab, m.lab_in)):
            values = expand(lab[:, LAB : LAB + TGT], m.mask_tgt)
            m.target[t * PX : (t + 1) * PX, :] = jnp.dot(
                values, m.targets[...].astype(F32), precision=lax.Precision.HIGHEST, preferred_element_type=F32
            )


def loss_gradient(m):
    total = m.count_sum[0:1, :] + m.count_in[1, 0:1, :] + m.count_in[2, 0:1, :] + m.count_in[3, 0:1, :]
    scale = jnp.concatenate([1.0 / jnp.maximum(total, 1.0)] * (HEAD // LANES), axis=1)
    bias = m.bias[m.role, 4:5, :]

    def keep(t, g):
        g = g.astype(BF16).astype(F32)
        m.grad_bias[4:5, :] += jnp.sum(g, axis=0, keepdims=True)
        put_shifted(m.g3h, t, g, -1, HEAD)

    @pl.when(m.role == 0)
    def _():
        for t in range(2):
            at = slice(t * PX, (t + 1) * PX)
            x = m.logits[at, :] + bias
            code = m.code[at, :]
            labeled = code == m.label[0:1, :]
            y = jnp.where(labeled, -x, x)
            e = jnp.exp(-jnp.abs(y))
            q = jnp.where(y >= 0, 1.0, e) / (1.0 + e)
            softplus = jnp.maximum(y, 0.0) + jnp.log1p(e)
            slope = q * q * (2.0 * (1.0 - q) * softplus + q)
            keep(t, slope * jnp.where(labeled, -0.25, jnp.where(code > 0.5, 0.75, 0.0)) * scale)

    @pl.when(m.role == 1)
    def _():
        for t in range(2):
            at = slice(t * PX, (t + 1) * PX)
            offset = m.logits[at, :] + bias - m.target[at, :]
            keep(t, jnp.where(m.code[at, :] > 1.5, jnp.clip(offset / huber_beta, -1.0, 1.0), 0.0) * scale)


def head_kernel_gradient(m, r):
    for s in range(3):
        at = (3 * r + s) * CH
        m.gh[at : at + CH, :] = dot(
            m.act_t[LAYERS], shifted_rows(m.g3h, 2 - r, slice(s * HEAD, (s + 1) * HEAD))
        ).astype(BF16)


def input_gradient(m, g3, width, kernel):
    acc = None
    for r in range(3):
        for s in range(3):
            at = (3 * r + s) * CH
            part = dot_nt(shifted_rows(g3, 2 - r, slice(s * width, (s + 1) * width)), kernel[at : at + CH, :])
            acc = part if acc is None else acc + part
    return acc


def layer_upstream(m, l):
    g = (m.da[...] * m.slope[l]).astype(BF16).astype(F32)
    m.grad_bias[l : l + 1, 0:CH] = jnp.sum(g, axis=0, keepdims=True)
    for t in range(2):
        put_shifted(m.g3, t, g[t * PX : (t + 1) * PX], -1, CH)


def layer_kernel_gradient(m, l, r):
    part = dot(m.act_t[l], shifted_rows(m.g3, 2 - r))
    for s in range(3):
        at = (3 * r + s) * CH
        m.g[l, at : at + CH, :] = part[:, s * CH : (s + 1) * CH].astype(BF16)


class Traffic:
    def __init__(self, send_sem, recv_sem):
        self.send_sem, self.recv_sem = send_sem, recv_sem
        self.names, self.used, self.sent = {}, 0, []

    def copy(self, name, src, dst, peer, span=1, offset=0):
        if name not in self.names:
            self.names[name] = self.used
            self.used += span
        i = self.names[name] + offset
        return pltpu.make_async_remote_copy(
            src, dst, self.send_sem.at[i], self.recv_sem.at[i], device_id=peer, device_id_type=MESH
        )

    def send(self, name, src, dst, peer, when=None, **at):
        copy = self.copy(name, src, dst, peer, **at)
        if when is None:
            copy.start()
        else:
            pl.when(when)(copy.start)
        self.sent.append((when, copy))

    def arrived(self, name, dst, peer, **at):
        self.copy(name, dst, dst, peer, **at).wait_recv()

    def finish(self):
        for when, copy in self.sent:
            if when is None:
                copy.wait_send()
            else:
                pl.when(when)(copy.wait_send)


SEMAPHORES = 192
GATHER_ORDER = (
    ("T", 0, "A"), ("H", 0, "B"), ("T", 1, "B"), ("T", 3, "A"), ("T", 2, "B"), ("H", 1, "A"), ("H", 3, "B"), ("H", 2, "A"),
)


def head_kernel(
    features, tower_class, tower_boxes, head_class, head_boxes, bias, state, labels, targets_in, valid,
    spread, targets, mask_lab, mask_tgt, label,
    out_features, out_class, out_boxes, out_head_class, out_head_boxes, out_bias,
    own, own_h, w, wh, hp, g, gh, rc, rch, sh, r1, r1h, r2, r2h, rz, rzh,
    act3, g3, g3h, act_t, slope, logits, code, target, da,
    x, lab, lab_in, count_mine, count_sum, count_in, grad_bias, bias_in, bias_z, dx, dx_in, tile_out, features_in,
    send_sem, recv_sem,
):
    s, dp = lax.axis_index("section"), lax.axis_index("dp")
    my_y, my_x, my_z, my_c = s // 2, s % 2, dp // 2, dp % 2
    sx, sy, sg = 2 * my_y + (1 - my_x), 2 * (1 - my_y) + my_x, 2 * (1 - my_y) + (1 - my_x)
    to_x, to_y, to_g, to_c = (sx, dp), (sy, dp), (sg, dp), (s, 2 * my_z + 1 - my_c)
    plane = lambda k: (my_z + k) % PLANES
    to_z = lambda k: (s, 2 * plane(k) + my_c)
    to_pair = (s, 2 * (my_z + 1 - 2 * (my_z % 2)) + my_c)
    role = my_z % 2
    net = Traffic(send_sem, recv_sem)
    m = SimpleNamespace(
        w=w, wh=wh, g=g, gh=gh, act3=act3, g3=g3, g3h=g3h, act_t=act_t, slope=slope, logits=logits, code=code,
        target=target, da=da, lab=lab, lab_in=lab_in, count_sum=count_sum, count_in=count_in, grad_bias=grad_bias,
        bias=bias, spread=spread, targets=targets, mask_lab=mask_lab, mask_tgt=mask_tgt, label=label, role=role,
    )

    def shard(z, c):
        return pl.ds(pl.multiple_of(ROWS * (2 * z + c), 16), ROWS)

    barrier = pltpu.get_barrier_semaphore()
    peers = (to_x, to_y, to_g, to_c, to_z(1), to_z(2), to_z(3))
    for peer in peers:
        pl.semaphore_signal(barrier, inc=1, device_id=peer, device_id_type=MESH)

    for role_at, (tower, head) in enumerate(((tower_class, head_class), (tower_boxes, head_boxes))):
        own[role_at] = tower[0].astype(BF16)
        width = head.shape[1]
        main = min(width, LANES)
        own_h[role_at] = jnp.zeros((PACK, LANES), BF16)
        own_h[role_at, 0:ROWS, 0:main] = head[:, 0:main].astype(BF16)
        if width > LANES:
            logits[0:ROWS, 0:LANES] = jnp.zeros((ROWS, LANES), F32)
            logits[0:ROWS, 0 : width - LANES] = head[:, LANES:width]
            own_h[role_at, ROWS:PACK, :] = (
                logits[0:HALF, 0:LANES] + pltpu.roll(logits[HALF:ROWS, 0:LANES], TAIL, 1)
            ).astype(BF16)

    row = lax.broadcasted_iota(jnp.int32, (TILE, TILE * A), 0)
    found = jnp.zeros((TILE, TILE * A), F32)
    for t in range(SECTIONS):
        found += jnp.where(jnp.logical_and(state[t] == 1, row < valid[t]), 1.0, 0.0)
    count_mine[...] = jnp.full((8, LANES), jnp.sum(found), F32)
    inside = row < valid[s]
    kind = state[s]
    lab[...] = jnp.zeros_like(lab)
    lab[:, 0 : TILE * A] = jnp.where(
        inside,
        jnp.where(kind == 1, labels[s].astype(F32) + 2.0, jnp.where(kind == 2, 0.0, 1.0)),
        0.0,
    )
    lab[:, LAB : LAB + targets_in.shape[2]] = targets_in[s]

    pl.semaphore_wait(barrier, len(peers))

    for kind_name, src, dst in (("T", own, w), ("H", own_h, hp)):
        for k in (1, 3, 2):
            at = dst.at[s, shard(my_z, my_c), :] if kind_name == "T" else dst.at[s, my_z]
            net.send(("z", kind_name, k), src.at[plane(k) % 2], at, to_z(k))
        if kind_name == "T":
            for name, peer, sec in (("x", to_x, sx), ("y", to_y, sy), ("g", to_g, sg)):
                net.send(("f", name), features.at[sec], x.at[0, pl.ds(pl.multiple_of(64 * s, 64), 64), :], peer)
            net.send("count c", count_mine, count_in.at[0], to_c)
            net.send("lab", lab, lab_in, to_pair)
    w[s, shard(my_z, my_c), :] = own[role]
    hp[s, my_z] = own_h[role]

    def piece(kind_name, sec, j):
        z = (my_z + PLANES - j) % PLANES
        return w.at[sec, shard(z, my_c), :] if kind_name == "T" else hp.at[sec, z]

    def ways(way):
        return ((to_x, sx), (to_y, sy)) if way == "A" else ((to_y, sy), (to_x, sx))

    def gather_first(kind_name, j, way):
        (n1, s1), (n2, s2) = ways(way)
        if j:
            net.arrived(("z", kind_name, j), piece(kind_name, s, j), to_z(PLANES - j))
        mine = piece(kind_name, s, j)
        net.send(("g1", kind_name, j), mine, mine, n1)
        if kind_name == "T":
            net.send(("swap", kind_name, j, 0), mine, mine, to_c)

    def gather_second(kind_name, j, way):
        (n1, s1), (n2, s2) = ways(way)
        mine, first = piece(kind_name, s, j), piece(kind_name, s1, j)
        net.send(("g2", kind_name, j), mine, mine, n2)
        net.arrived(("g1", kind_name, j), first, n1)
        net.send(("g3", kind_name, j), first, first, n2)
        if kind_name == "T":
            net.send(("swap", kind_name, j, 1), first, first, to_c)

    def gather_third(kind_name, j, way):
        (n1, s1), (n2, s2) = ways(way)
        for i, (name, sec) in enumerate((("g2", s2), ("g3", sg))):
            got = piece(kind_name, sec, j)
            net.arrived((name, kind_name, j), got, n2)
            if kind_name == "T":
                net.send(("swap", kind_name, j, 2 + i), got, got, to_c)
        if kind_name == "H":
            z = (my_z + PLANES - j) % PLANES
            at = pl.multiple_of(ROWS * (2 * z + my_c), 16)
            for sec in range(SECTIONS):
                wh[pl.ds(at, ROWS), sec * LANES : (sec + 1) * LANES] = hp[sec, z, 0:ROWS, :]
            for q in range(2):
                lanes = slice((SECTIONS + q) * LANES, (SECTIONS + q + 1) * LANES)
                top, bottom = swap_halves(hp[2 * q, z, ROWS:PACK, :], hp[2 * q + 1, z, ROWS:PACK, :])
                wh[pl.ds(at, HALF), lanes] = top.astype(BF16)
                wh[pl.ds(at + HALF, HALF), lanes] = bottom.astype(BF16)
            block = wh.at[pl.ds(at, ROWS), :]
            net.send(("swap", "H", j), block, block, to_c)

    def swapped(kind_name, j):
        z = (my_z + PLANES - j) % PLANES
        if kind_name == "H":
            net.arrived(("swap", "H", j), wh.at[shard(z, 1 - my_c), :], to_c)
            return
        (_, s1), (_, s2) = ways(dict((entry[:2], entry[2]) for entry in GATHER_ORDER)[(kind_name, j)])
        for i, sec in enumerate((s, s1, s2, sg)):
            net.arrived(("swap", "T", j, i), w.at[sec, shard(z, 1 - my_c), :], to_c)

    def start():
        for ref in (act3, g3, g3h):
            for t in range(2):
                ref[t, 0:TILE, :] = jnp.zeros((TILE, ref.shape[2]), BF16)
                ref[t, TILE + PX : 2 * TILE + PX, :] = jnp.zeros((TILE, ref.shape[2]), BF16)
        grad_bias[...] = jnp.zeros_like(grad_bias)
        x[0, pl.ds(pl.multiple_of(64 * s, 64), 64), :] = features[s]
        for name, peer, sec in (("x", to_x, sx), ("y", to_y, sy), ("g", to_g, sg)):
            net.arrived(("f", name), x.at[0, pl.ds(pl.multiple_of(64 * sec, 64), 64), :], peer)
        net.send("tile", x.at[0], x.at[1], to_pair)
        net.arrived("count c", count_in.at[0], to_c)
        count_sum[...] = count_mine[...] + count_in[0]
        for k in (1, 2, 3):
            net.send(("count", k), count_sum, count_in.at[k], to_z(k))

    def prepare():
        net.arrived("lab", lab_in, to_pair)
        prepare_loss(m)
        net.arrived("tile", x.at[1], to_pair)
        for t in range(2):
            v = x[t].astype(F32)
            put_shifted(act3, t, v, 1, CH)
            act_t[0, :, t * PX : (t + 1) * PX] = v.T.astype(BF16)

    stages = len(GATHER_ORDER) + 2
    towers_done = max(i for i, entry in enumerate(GATHER_ORDER) if entry[0] == "T") + 2
    for i in range(stages):
        if i < len(GATHER_ORDER):
            gather_first(*GATHER_ORDER[i])
        if 1 <= i < len(GATHER_ORDER) + 1:
            gather_second(*GATHER_ORDER[i - 1])
        if i >= 2:
            gather_third(*GATHER_ORDER[i - 2])
        if i == 1:
            start()
        if i == 2:
            prepare()
        if i == towers_done:
            for j in range(PLANES):
                swapped("T", j)
        if towers_done <= i < towers_done + LAYERS:
            forward_layer(m, i - towers_done)
    for l in range(max(0, stages - towers_done), LAYERS):
        forward_layer(m, l)
    for k in (1, 2, 3):
        net.arrived(("count", k), count_in.at[k], to_z(PLANES - k))
    for j in range(PLANES):
        swapped("H", j)

    def summed(refs_into, refs_from):
        refs_into[...] = (refs_into[...].astype(F32) + refs_from[...].astype(F32)).astype(BF16)

    def reduce_start(l, zp):
        if l is None:
            net.send(("rc", l, zp), gh.at[shard(zp, 1 - my_c), :], rch.at[zp], to_c)
        else:
            net.send(("rc", l, zp), g.at[l, shard(zp, 1 - my_c), :], rc.at[l, zp], to_c)

    def bound(l, zp):
        x_here, y_here = my_x == l % 2, my_y == l // 2
        if zp < 2:
            return x_here, y_here, to_x, to_y
        return y_here, x_here, to_y, to_x

    def buffers(kind_name, l, zp):
        if kind_name == "T":
            return rc.at[l, zp], r1.at[l, zp], r2.at[zp]
        return sh.at[l, zp], r1h.at[l, zp], r2h.at[zp]

    def reduce_first_send(kind_name, l, zp):
        here1, here2, n1, n2 = bound(l, zp)
        mine, into1, into2 = buffers(kind_name, l, zp)
        away = jnp.logical_not(here1)

        net.send(("r1", kind_name, l, zp), mine, into1, n1, away)

    def reduce_cores_tower(l, zp):
        net.arrived(("rc", l, zp), rc.at[l, zp], to_c)
        rc[l, zp] = (rc[l, zp].astype(F32) + g[l, shard(zp, my_c), :].astype(F32)).astype(BF16)
        reduce_first_send("T", l, zp)

    def reduce_cores_head(zp):
        net.arrived(("rc", None, zp), rch.at[zp], to_c)
        at = pl.multiple_of(ROWS * (2 * zp + my_c), 16)
        for sec in range(SECTIONS):
            lanes = slice(sec * LANES, (sec + 1) * LANES)
            sh[sec, zp, 0:ROWS, :] = (
                rch[zp, :, lanes].astype(F32) + gh[pl.ds(at, ROWS), lanes].astype(F32)
            ).astype(BF16)
        for q in range(2):
            lanes = slice((SECTIONS + q) * LANES, (SECTIONS + q + 1) * LANES)
            top = rch[zp, 0:HALF, lanes].astype(F32) + gh[pl.ds(at, HALF), lanes].astype(F32)
            bottom = rch[zp, HALF:ROWS, lanes].astype(F32) + gh[pl.ds(at + HALF, HALF), lanes].astype(F32)
            first, second = swap_halves(top, bottom)
            sh[2 * q, zp, ROWS:PACK, :] = first.astype(BF16)
            sh[2 * q + 1, zp, ROWS:PACK, :] = second.astype(BF16)
        for sec in range(SECTIONS):
            reduce_first_send("H", sec, zp)

    def reduce_second(kind_name, l, zp):
        here1, here2, n1, n2 = bound(l, zp)
        mine, into1, into2 = buffers(kind_name, l, zp)

        @pl.when(here1)
        def _():
            net.arrived(("r1", kind_name, l, zp), into1, n1)
            summed(mine, into1)

        away = jnp.logical_and(here1, jnp.logical_not(here2))

        net.send(("r2", kind_name, zp), mine, into2, n2, away)

    def reduce_third(kind_name, l, zp):
        here1, here2, n1, n2 = bound(l, zp)
        mine, into1, into2 = buffers(kind_name, l, zp)

        @pl.when(s == l)
        def _():
            net.arrived(("r2", kind_name, zp), into2, n2)
            summed(mine, into2)

        away = jnp.logical_and(s == l, my_z != zp)
        out = rz if kind_name == "T" else rzh
        k = (zp + PLANES - my_z) % PLANES
        net.send(("rz", kind_name), mine, out.at[my_z], (s, 2 * zp + my_c), away, span=PLANES, offset=k)

    def collect(kind_name):
        mine, others = (rc, rz) if kind_name == "T" else (sh, rzh)
        for k in (1, 2, 3):
            source = plane(PLANES - k)
            net.arrived(("rz", kind_name), others.at[source], to_z(PLANES - k), span=PLANES, offset=k)
        same = mine[s, my_z].astype(F32) + others[plane(2)].astype(F32)
        return same, others[plane(1)].astype(F32) + others[plane(3)].astype(F32)

    def by_role(same, other, store):
        @pl.when(role == 0)
        def _():
            store(same, other)

        @pl.when(role == 1)
        def _():
            store(other, same)

    def store_towers(of_class, of_boxes):
        out_class[0] = of_class
        out_boxes[0] = of_boxes

    def store_heads(of_class, of_boxes):
        for packed, out in ((of_class, out_head_class), (of_boxes, out_head_boxes)):
            width = out.shape[1]
            main, rest = min(width, LANES), max(0, width - LANES)
            out[:, 0:main] = packed[0:ROWS, 0:main]
            if rest:
                out[0:HALF, LANES:width] = packed[ROWS:PACK, 0:rest]
                out[HALF:ROWS, LANES:width] = pltpu.roll(packed[ROWS:PACK, :], TAIL, 1)[:, 0:rest]

    head_forward(m)
    loss_gradient(m)
    for r in range(3):
        head_kernel_gradient(m, r)
        for zp in ((0,), (1,), (2, 3))[r]:
            reduce_start(None, zp)
        if r:
            reduce_cores_head(r - 1)
    da[...] = input_gradient(m, g3h, HEAD, wh)
    reduce_cores_head(2)
    reduce_cores_head(3)
    for l in range(LAYERS - 1, -1, -1):
        layer_upstream(m, l)
        if l == 0:
            net.send("bias c", grad_bias, bias_in.at[0], to_c)
        for r in range(3):
            layer_kernel_gradient(m, l, r)
            for zp in ((0,), (1,), (2, 3))[r]:
                reduce_start(l, zp)
        da[...] = input_gradient(m, g3, CH, w.at[l])
        if l == 0:
            dx[...] = da[PX : 2 * PX, :].astype(BF16)
            net.send("dx", dx, dx_in, to_pair)
        for zp in range(PLANES):
            reduce_cores_tower(l, zp)

    net.arrived("bias c", bias_in.at[0], to_c)
    bias_z[0] = grad_bias[...] + bias_in[0]
    net.send("bias x", bias_z.at[0], bias_in.at[1], to_x)

    for zp in range(PLANES):
        for sec in range(SECTIONS):
            reduce_second("H", sec, zp)
    net.arrived("bias x", bias_in.at[1], to_x)
    bias_z[1] = bias_z[0] + bias_in[1]
    net.send("bias y", bias_z.at[1], bias_in.at[2], to_y)

    net.arrived("dx", dx_in, to_pair)
    tile_out[...] = (da[0:PX, :] + dx_in[...].astype(F32)).astype(BF16)
    mine_at = pl.ds(pl.multiple_of(64 * s, 64), 64)
    for name, peer, sec in (("x", to_x, sx), ("y", to_y, sy), ("g", to_g, sg)):
        net.send(
            ("b", name), tile_out.at[pl.ds(pl.multiple_of(64 * sec, 64), 64), :], features_in.at[s], peer
        )
    for l in range(LAYERS - 1, -1, -1):
        for zp in range(PLANES):
            reduce_second("T", l, zp)
        if l == LAYERS - 1:
            net.arrived("bias y", bias_in.at[2], to_y)
            bias_z[2] = bias_z[1] + bias_in[2]
            for k in (1, 2, 3):
                net.send(("bias z", k), bias_z.at[2], bias_in.at[2 + k], to_z(k))
            for zp in range(PLANES):
                for sec in range(SECTIONS):
                    reduce_third("H", sec, zp)
        else:
            for zp in range(PLANES):
                reduce_third("T", l + 1, zp)
    for name, peer, sec in (("x", to_x, sx), ("y", to_y, sy), ("g", to_g, sg)):
        net.arrived(("b", name), features_in.at[sec], peer)
        out_features[sec] = features_in[sec]
    out_features[s] = tile_out[mine_at, :]
    for k in (1, 2, 3):
        net.arrived(("bias z", k), bias_in.at[2 + k], to_z(PLANES - k))
    out_bias[role] = bias_z[2] + bias_in[4]
    out_bias[1 - role] = bias_in[3] + bias_in[5]
    by_role(*collect("H"), store_heads)
    for zp in range(PLANES):
        reduce_third("T", 0, zp)
    by_role(*collect("T"), store_towers)
    net.finish()


def fast(features, tower_class, bias_class, tower_boxes, bias_boxes, head_class, head_class_bias, head_boxes,
         head_boxes_bias, anchor_state, class_labels, box_targets, valid_rows):
    class_width, boxes_width = head_class_bias.shape[0], head_boxes_bias.shape[0]

    def lay(vector):
        parts = vector.reshape(SECTIONS, -1)
        main = parts[:, :LANES]
        rest = parts[:, LANES:]
        main = jnp.pad(main, ((0, 0), (0, LANES - main.shape[1]))).reshape(-1)
        rest = jnp.pad(rest, ((0, 0), (0, TAIL - rest.shape[1]))).reshape(-1)
        return jnp.concatenate([main, rest])[None]

    def unlay(row, width):
        per = width // SECTIONS
        main = row[: SECTIONS * LANES].reshape(SECTIONS, LANES)[:, : min(per, LANES)]
        rest = row[SECTIONS * LANES :].reshape(SECTIONS, TAIL)[:, : max(0, per - LANES)]
        return jnp.concatenate([main, rest], axis=1).reshape(width)

    bias = jnp.stack(
        [
            jnp.concatenate([jnp.pad(tower, ((0, 0), (0, HEAD - CH))), lay(head), jnp.zeros((3, HEAD), F32)])
            for tower, head in ((bias_class, head_class_bias), (bias_boxes, head_boxes_bias))
        ]
    )
    tiles = features.shape[0]
    vmem = pl.BlockSpec(memory_space=pltpu.VMEM)
    smem = pl.BlockSpec(memory_space=pltpu.SMEM)
    v = lambda shape, dtype: pltpu.VMEM(shape, dtype)
    out = lambda shape, dtype: jax.ShapeDtypeStruct(shape, dtype)
    results = pl.pallas_call(
        head_kernel,
        out_shape=(
            out((tiles, 64, CH), BF16),
            out((1, ROWS, CH), F32),
            out((1, ROWS, CH), F32),
            out(head_class.shape, F32),
            out(head_boxes.shape, F32),
            out((2, 8, HEAD), F32),
        ),
        in_specs=[vmem] * 9 + [smem] + [vmem] * 5,
        out_specs=(vmem,) * 6,
        scratch_shapes=[
            v((2, ROWS, CH), BF16),
            v((2, PACK, LANES), BF16),
            v((LAYERS, DEEP, CH), BF16),
            v((DEEP, HEAD), BF16),
            v((SECTIONS, PLANES, PACK, LANES), BF16),
            v((LAYERS, DEEP, CH), BF16),
            v((DEEP, HEAD), BF16),
            v((LAYERS, PLANES, ROWS, CH), BF16),
            v((PLANES, ROWS, HEAD), BF16),
            v((SECTIONS, PLANES, PACK, LANES), BF16),
            v((LAYERS, PLANES, ROWS, CH), BF16),
            v((SECTIONS, PLANES, PACK, LANES), BF16),
            v((PLANES, ROWS, CH), BF16),
            v((PLANES, PACK, LANES), BF16),
            v((PLANES, ROWS, CH), BF16),
            v((PLANES, PACK, LANES), BF16),
            v((2, PX + 2 * TILE, 3 * CH), BF16),
            v((2, PX + 2 * TILE, 3 * CH), BF16),
            v((2, PX + 2 * TILE, 3 * HEAD), BF16),
            v((LAYERS + 1, CH, 2 * PX), BF16),
            v((LAYERS, 2 * PX, CH), F32),
            v((2 * PX, HEAD), F32),
            v((2 * PX, HEAD), F32),
            v((2 * PX, HEAD), F32),
            v((2 * PX, CH), F32),
            v((2, PX, CH), BF16),
            v((TILE, LAB + TGT), F32),
            v((TILE, LAB + TGT), F32),
            v((8, LANES), F32),
            v((8, LANES), F32),
            v((4, 8, LANES), F32),
            v((8, HEAD), F32),
            v((6, 8, HEAD), F32),
            v((3, 8, HEAD), F32),
            v((PX, CH), BF16),
            v((PX, CH), BF16),
            v((PX, CH), BF16),
            v((SECTIONS, 64, CH), BF16),
            pltpu.SemaphoreType.DMA((SEMAPHORES,)),
            pltpu.SemaphoreType.DMA((SEMAPHORES,)),
        ],
        compiler_params=pltpu.CompilerParams(
            collective_id=0, has_side_effects=True, vmem_limit_bytes=62 * 2**20
        ),
    )(
        features.reshape(tiles, 64, CH), tower_class, tower_boxes, head_class, head_boxes, bias,
        anchor_state, class_labels, box_targets, valid_rows, *constants(class_width, boxes_width),
    )
    grad_features, grad_class, grad_boxes, grad_head_class, grad_head_boxes, sums = results
    return (
        grad_features.reshape(features.shape),
        grad_class,
        sums[0, :LAYERS, :CH],
        grad_boxes,
        sums[1, :LAYERS, :CH],
        grad_head_class,
        unlay(sums[0, LAYERS], class_width),
        grad_head_boxes,
        unlay(sums[1, LAYERS], boxes_width),
    )


def shifted(block, axis, distance):
    devices = range(lax.axis_size(axis))
    route = [(i - distance, i) for i in devices if i - distance in devices]
    return lax.ppermute(block, axis, route)


def anchor_masks(anchor_state, valid_rows):
    tile_count = anchor_state.shape[0]
    anchor_kind = anchor_state.reshape(tile_count, TILE, TILE, A)
    row_index = lax.broadcasted_iota(jnp.int32, (tile_count, TILE, 1, 1), 1)
    inside = row_index < valid_rows.reshape(tile_count, 1, 1, 1)
    positive = jnp.logical_and(anchor_kind == 1, inside).astype(jnp.float32)
    counted = jnp.logical_and(anchor_kind != 2, inside).astype(jnp.float32)
    return (positive, counted)


def head_loss(logits, box_values, positive, counted, class_labels, box_targets, normalizer):
    tile_count = logits.shape[0]
    scores = logits.reshape(tile_count, TILE, TILE, A, K)
    labels = class_labels.reshape(tile_count, TILE, TILE, A, 1)
    classes = lax.broadcasted_iota(jnp.int32, (1, 1, 1, 1, K), 4)
    target = (labels == classes).astype(jnp.float32) * positive[..., None]
    chance = jax.nn.sigmoid(scores)
    entropy = jax.nn.softplus(scores) - target * scores
    agreement = chance * target + (1.0 - chance) * (1.0 - target)
    balance = 0.25 * target + 0.75 * (1.0 - target)
    focal_terms = balance * (1.0 - agreement) ** 2 * entropy
    focal_sum = jnp.sum(focal_terms * counted[..., None])
    offsets = box_values.reshape(tile_count, TILE, TILE, A, 4) - box_targets.reshape(
        tile_count, TILE, TILE, A, 4
    )
    spread = jnp.abs(offsets)
    huber_terms = jnp.where(
        spread < huber_beta, 0.5 * offsets * offsets / huber_beta, spread - 0.5 * huber_beta
    )
    box_sum = jnp.sum(huber_terms * positive[..., None])
    return (focal_sum + box_sum) / normalizer


def unfold(values):
    tile_count, tile_side, channels = (values.shape[0], values.shape[1], values.shape[3])
    padded = jnp.pad(values, ((0, 0), (1, 1), (1, 1), (0, 0)))
    pieces = [
        padded[:, row_shift : row_shift + tile_side, col_shift : col_shift + tile_side, :]
        for row_shift in range(3)
        for col_shift in range(3)
    ]
    return jnp.concatenate(pieces, axis=-1).reshape(
        tile_count * tile_side * tile_side, 9 * channels
    )


def fold_back(columns, tile_count, tile_side, channels):
    shaped = columns.reshape(tile_count, tile_side, tile_side, 9 * channels)
    padded = jnp.zeros((tile_count, tile_side + 2, tile_side + 2, channels), jnp.float32)
    for tap_index in range(9):
        row_shift = tap_index // 3
        col_shift = tap_index % 3
        padded = padded.at[
            :, row_shift : row_shift + tile_side, col_shift : col_shift + tile_side, :
        ].add(shaped[..., tap_index * channels : (tap_index + 1) * channels])
    return padded[:, 1 : tile_side + 1, 1 : tile_side + 1, :]


def weight_grad(columns, upstream):
    return jnp.einsum("pk,pc->kc", columns, upstream, preferred_element_type=jnp.float32)


def input_cols(upstream, weight):
    return jnp.einsum("pc,kc->pk", upstream, weight, preferred_element_type=jnp.float32)


def pick(buffer, slot_index):
    return lax.dynamic_index_in_dim(buffer, slot_index, 0, keepdims=False)


def store(buffer, update, slot_index, active):
    return lax.dynamic_update_index_in_dim(
        buffer, jnp.where(active, update, pick(buffer, slot_index)), slot_index, 0
    )


def per_device(
    features,
    tower_class,
    bias_class,
    tower_boxes,
    bias_boxes,
    head_class,
    head_class_bias,
    head_boxes,
    head_boxes_bias,
    anchor_state,
    class_labels,
    box_targets,
    valid_rows,
):
    section_count = lax.axis_size("section")
    section_index = lax.axis_index("section")
    final_section = section_count - 1
    is_first = section_index == 0
    is_final = section_index == final_section
    tile_dev = features.shape[0]
    per_micro = tile_dev // MICRO
    whole = lax.all_gather(features, "section", axis=1, tiled=True)
    tile_side = whole.shape[1]
    channels = whole.shape[3]
    pixels = per_micro * tile_side * tile_side
    act_shape = (per_micro, tile_side, tile_side, channels)
    positive, counted = anchor_masks(anchor_state, valid_rows)
    found = lax.psum(jnp.sum(positive), "dp")
    normalizer = jnp.maximum(found, 1.0)
    gathered = (
        lax.all_gather(tower_class.astype(jnp.bfloat16), "dp", axis=1, tiled=True),
        lax.all_gather(tower_boxes.astype(jnp.bfloat16), "dp", axis=1, tiled=True),
        lax.all_gather(head_class.astype(jnp.bfloat16), "dp", axis=0, tiled=True),
        lax.all_gather(head_boxes.astype(jnp.bfloat16), "dp", axis=0, tiled=True),
    )
    weight_class = gathered[0][0]
    weight_boxes = gathered[1][0]
    head_weight_class, head_weight_boxes = (
        lax.all_gather(gathered[2], "section", axis=1, tiled=True),
        lax.all_gather(gathered[3], "section", axis=1, tiled=True),
    )
    layer_bias_class = lax.dynamic_index_in_dim(bias_class, section_index, 0, keepdims=False)
    layer_bias_boxes = lax.dynamic_index_in_dim(bias_boxes, section_index, 0, keepdims=False)
    class_width = head_weight_class.shape[1]
    boxes_width = head_weight_boxes.shape[1]
    patch_width = head_weight_class.shape[0]

    def head_pass(stored_class, stored_boxes, slot_index):
        cols_class = unfold(stored_class)
        cols_boxes = unfold(stored_boxes)
        logits = (
            jnp.dot(cols_class, head_weight_class, preferred_element_type=jnp.float32)
            + head_class_bias
        )
        box_values = (
            jnp.dot(cols_boxes, head_weight_boxes, preferred_element_type=jnp.float32)
            + head_boxes_bias
        )
        start = slot_index * per_micro
        pos_here = lax.dynamic_slice_in_dim(positive, start, per_micro, 0)
        counted_here = lax.dynamic_slice_in_dim(counted, start, per_micro, 0)
        labels_here = lax.dynamic_slice_in_dim(class_labels, start, per_micro, 0)
        targets_here = lax.dynamic_slice_in_dim(box_targets, start, per_micro, 0)

        def local_loss(logit_part, box_part):
            return head_loss(
                logit_part.reshape(per_micro, tile_side, tile_side, class_width),
                box_part.reshape(per_micro, tile_side, tile_side, boxes_width),
                pos_here,
                counted_here,
                labels_here,
                targets_here,
                normalizer,
            )

        total_loss, pullback = jax.vjp(local_loss, logits, box_values)
        grad_logits, grad_box = pullback(jnp.ones_like(total_loss))
        grad_logits = grad_logits.astype(jnp.bfloat16)
        grad_box = grad_box.astype(jnp.bfloat16)
        back_class = fold_back(
            input_cols(grad_logits, head_weight_class), per_micro, tile_side, channels
        )
        back_boxes = fold_back(
            input_cols(grad_box, head_weight_boxes), per_micro, tile_side, channels
        )
        return (
            weight_grad(cols_class, grad_logits),
            weight_grad(cols_boxes, grad_box),
            jnp.sum(grad_logits.astype(jnp.float32), 0),
            jnp.sum(grad_box.astype(jnp.float32), 0),
            back_class,
            back_boxes,
        )

    def head_spare(stored_class, stored_boxes, slot_index):
        return (
            jnp.zeros((patch_width, class_width), jnp.float32),
            jnp.zeros((patch_width, boxes_width), jnp.float32),
            jnp.zeros((class_width,), jnp.float32),
            jnp.zeros((boxes_width,), jnp.float32),
            jnp.zeros(act_shape, jnp.float32),
            jnp.zeros(act_shape, jnp.float32),
        )

    kept_class = jnp.zeros((MICRO,) + act_shape, jnp.bfloat16)
    kept_boxes = jnp.zeros((MICRO,) + act_shape, jnp.bfloat16)
    kept_pre_class = jnp.zeros((MICRO, pixels, channels), jnp.float32)
    kept_pre_boxes = jnp.zeros((MICRO, pixels, channels), jnp.float32)
    head_back_class = jnp.zeros((MICRO,) + act_shape, jnp.float32)
    head_back_boxes = jnp.zeros((MICRO,) + act_shape, jnp.float32)
    grad_head_class = jnp.zeros((patch_width, class_width), jnp.float32)
    grad_head_boxes = jnp.zeros((patch_width, boxes_width), jnp.float32)
    grad_hbias_class = jnp.zeros((class_width,), jnp.float32)
    grad_hbias_boxes = jnp.zeros((boxes_width,), jnp.float32)
    total_moments = MICRO + section_count - 1
    empty_act = jnp.zeros(act_shape, jnp.bfloat16)
    received = (empty_act, empty_act)
    for moment in range(total_moments):
        micro_index = moment - section_index
        active = jnp.logical_and(micro_index >= 0, micro_index < MICRO)
        slot_index = jnp.clip(micro_index, 0, MICRO - 1)
        if moment < MICRO:
            entering = whole[moment * per_micro : (moment + 1) * per_micro]
        else:
            entering = empty_act
        input_class = jnp.where(is_first, entering, received[0])
        input_boxes = jnp.where(is_first, entering, received[1])
        kept_class = store(kept_class, input_class, slot_index, active)
        kept_boxes = store(kept_boxes, input_boxes, slot_index, active)
        pre_class = (
            jnp.dot(unfold(input_class), weight_class, preferred_element_type=jnp.float32)
            + layer_bias_class
        )
        pre_boxes = (
            jnp.dot(unfold(input_boxes), weight_boxes, preferred_element_type=jnp.float32)
            + layer_bias_boxes
        )
        kept_pre_class = store(kept_pre_class, pre_class, slot_index, active)
        kept_pre_boxes = store(kept_pre_boxes, pre_boxes, slot_index, active)
        act_class = jax.nn.gelu(pre_class).astype(jnp.bfloat16).reshape(act_shape)
        act_boxes = jax.nn.gelu(pre_boxes).astype(jnp.bfloat16).reshape(act_shape)
        results = lax.cond(
            jnp.logical_and(is_final, active),
            head_pass,
            head_spare,
            act_class,
            act_boxes,
            slot_index,
        )
        grad_head_class = grad_head_class + results[0]
        grad_head_boxes = grad_head_boxes + results[1]
        grad_hbias_class = grad_hbias_class + results[2]
        grad_hbias_boxes = grad_hbias_boxes + results[3]
        head_back_class = store(head_back_class, results[4], slot_index, active)
        head_back_boxes = store(head_back_boxes, results[5], slot_index, active)
        if moment < total_moments - 1:
            received = shifted((act_class, act_boxes), "section", 1)
    grad_layer_class = jnp.zeros((patch_width, channels), jnp.float32)
    grad_layer_boxes = jnp.zeros((patch_width, channels), jnp.float32)
    grad_lbias_class = jnp.zeros((channels,), jnp.float32)
    grad_lbias_boxes = jnp.zeros((channels,), jnp.float32)
    input_back = jnp.zeros((MICRO,) + act_shape, jnp.float32)
    returned = (empty_act, empty_act)
    for moment in range(total_moments):
        micro_index = moment - (final_section - section_index)
        active = jnp.logical_and(micro_index >= 0, micro_index < MICRO)
        slot_index = jnp.clip(micro_index, 0, MICRO - 1)
        upstream_class = jnp.where(
            is_final, pick(head_back_class, slot_index), returned[0].astype(jnp.float32)
        ).reshape(pixels, channels)
        upstream_boxes = jnp.where(
            is_final, pick(head_back_boxes, slot_index), returned[1].astype(jnp.float32)
        ).reshape(pixels, channels)
        cols_class = unfold(pick(kept_class, slot_index))
        cols_boxes = unfold(pick(kept_boxes, slot_index))
        pre_class = pick(kept_pre_class, slot_index)
        pre_boxes = pick(kept_pre_boxes, slot_index)
        gelu_class = jax.vjp(jax.nn.gelu, pre_class)[1](upstream_class)[0]
        gelu_boxes = jax.vjp(jax.nn.gelu, pre_boxes)[1](upstream_boxes)[0]
        grad_pre_class = jnp.where(active, gelu_class, 0.0).astype(jnp.bfloat16)
        grad_pre_boxes = jnp.where(active, gelu_boxes, 0.0).astype(jnp.bfloat16)
        grad_layer_class = grad_layer_class + weight_grad(cols_class, grad_pre_class)
        grad_layer_boxes = grad_layer_boxes + weight_grad(cols_boxes, grad_pre_boxes)
        grad_lbias_class = grad_lbias_class + jnp.sum(grad_pre_class.astype(jnp.float32), 0)
        grad_lbias_boxes = grad_lbias_boxes + jnp.sum(grad_pre_boxes.astype(jnp.float32), 0)
        back_class = fold_back(
            input_cols(grad_pre_class, weight_class), per_micro, tile_side, channels
        )
        back_boxes = fold_back(
            input_cols(grad_pre_boxes, weight_boxes), per_micro, tile_side, channels
        )
        input_back = store(
            input_back, back_class + back_boxes, slot_index, jnp.logical_and(active, is_first)
        )
        if moment < total_moments - 1:
            returned = shifted(
                (back_class.astype(jnp.bfloat16), back_boxes.astype(jnp.bfloat16)), "section", -1
            )
    spread_back = jnp.where(
        is_first, input_back.reshape(tile_dev, tile_side, tile_side, channels), 0.0
    )
    grad_features = lax.psum_scatter(
        spread_back.astype(jnp.bfloat16), "section", scatter_dimension=1, tiled=True
    )
    summed = (
        lax.psum_scatter(grad_layer_class, "dp", scatter_dimension=0, tiled=True),
        lax.psum_scatter(grad_layer_boxes, "dp", scatter_dimension=0, tiled=True),
        lax.psum_scatter(grad_head_class, "dp", scatter_dimension=0, tiled=True),
        lax.psum_scatter(grad_head_boxes, "dp", scatter_dimension=0, tiled=True),
    )
    final_head_class, final_head_boxes = (
        lax.psum_scatter(
            summed[2].astype(jnp.bfloat16), "section", scatter_dimension=1, tiled=True
        ).astype(jnp.float32),
        lax.psum_scatter(
            summed[3].astype(jnp.bfloat16), "section", scatter_dimension=1, tiled=True
        ).astype(jnp.float32),
    )
    rows_class = lax.dynamic_update_index_in_dim(
        jnp.zeros((LAYERS, channels), jnp.float32), grad_lbias_class, section_index, 0
    )
    rows_boxes = lax.dynamic_update_index_in_dim(
        jnp.zeros((LAYERS, channels), jnp.float32), grad_lbias_boxes, section_index, 0
    )
    bias_sums = lax.psum(
        (rows_class, rows_boxes, grad_hbias_class, grad_hbias_boxes), ("section", "dp")
    )
    return (
        grad_features,
        summed[0][None],
        bias_sums[0],
        summed[1][None],
        bias_sums[1],
        final_head_class,
        bias_sums[2],
        final_head_boxes,
        bias_sums[3],
    )


def solution(mesh):
    fits = mesh.shape["section"] == SECTIONS == LAYERS and mesh.shape["dp"] == PLANES * CORES
    placed = (
        P("dp", "section", None, None),
        P("section", "dp", None),
        P(),
        P("section", "dp", None),
        P(),
        P("dp", "section"),
        P(),
        P("dp", "section"),
        P(),
        P("dp", None, None),
        P("dp", None, None),
        P("dp", None, None),
        P("dp"),
    )
    return jax.shard_map(
        fast if fits else per_device,
        mesh=mesh,
        in_specs=placed,
        out_specs=(
            P("dp", "section", None, None),
            P("section", "dp", None),
            P(),
            P("section", "dp", None),
            P(),
            P("dp", "section"),
            P(),
            P("dp", "section"),
            P(),
        ),
        check_vma=False,
    )
```

```python
import functools
import math
from types import SimpleNamespace

import jax
import jax.numpy as jnp
import numpy as np
from jax import lax
from jax.experimental import pallas as pl
from jax.experimental.pallas import tpu as pltpu
from jax.sharding import PartitionSpec as P

K = 80
A = 9
LAYERS = 4
TILE = 16
MICRO = 4


huber_beta = 1.0 / 9.0

F32 = jnp.float32
BF16 = jnp.bfloat16
MESH = pl.DeviceIdType.MESH
GELU_C = math.sqrt(2.0 / math.pi)

SECTIONS = 4
PLANES = 4
CORES = 2
CH = 256
PX = TILE * TILE
ROWS = 288
HALF = ROWS // 2
PACK = ROWS + HALF
LANES = 128
TAIL = 64
MAIN = SECTIONS * LANES
HEAD = MAIN + SECTIONS * TAIL
LAB = 256
TGT = 640
DEEP = 9 * CH


def head_layout(width):
    per = width // SECTIONS
    columns = np.full((HEAD,), -1)
    for s in range(SECTIONS):
        main = min(per, LANES)
        columns[s * LANES : s * LANES + main] = s * per + np.arange(main)
        rest = per - main
        at = SECTIONS * LANES + s * TAIL
        columns[at : at + rest] = s * per + main + np.arange(rest)
    return columns


def constants(class_width, boxes_width):
    classes, boxes = head_layout(class_width), head_layout(boxes_width)
    spread = np.zeros((2, LAB, HEAD), np.float32)
    targets = np.zeros((TGT, MAIN), np.float32)
    for j in range(TILE):
        for col in range(HEAD):
            if classes[col] >= 0:
                spread[0, j * A + classes[col] // K, col] = 1
            if boxes[col] >= 0:
                spread[1, j * A + boxes[col] // 4, col] = 1
                targets[j * boxes_width + boxes[col], col] = 1
    pixel = np.arange(PX)[:, None] % TILE
    mask_lab = (np.arange(LAB)[None, :] // A == pixel) & (np.arange(LAB)[None, :] < TILE * A)
    mask_tgt = (np.arange(TGT)[None, :] // boxes_width == pixel) & (np.arange(TGT)[None, :] < TILE * boxes_width)
    label = np.where(classes >= 0, classes % K, -9).astype(np.float32)[None, :] + 2.0
    bf = lambda v: jnp.asarray(v.astype(np.float32), BF16)
    return bf(spread), bf(targets), bf(mask_lab), bf(mask_tgt), jnp.asarray(np.repeat(label, 8, 0))


def dot(a, b):
    return jnp.dot(a, b, preferred_element_type=F32)


def dot_nt(a, b):
    return lax.dot_general(a, b, (((1,), (1,)), ((), ())), preferred_element_type=F32)


def moved_right(v):
    col = lax.broadcasted_iota(jnp.int32, v.shape, 0) % TILE
    return jnp.where(col == 0, 0.0, pltpu.roll(v, 1, 0))


def moved_left(v):
    col = lax.broadcasted_iota(jnp.int32, v.shape, 0) % TILE
    return jnp.where(col == TILE - 1, 0.0, pltpu.roll(v, PX - 1, 0))


def put_shifted(ref, t, v, order, width):
    blocks = (moved_right(v), v, moved_left(v))[::order]
    for s, block in enumerate(blocks):
        ref[t, TILE : TILE + PX, s * width : (s + 1) * width] = block.astype(BF16)


def shifted_rows(ref, r, lanes=slice(None)):
    return ref[:, TILE * r : TILE * r + PX, lanes].reshape(2 * PX, -1)


def swap_halves(p, q):
    p, q = p.astype(F32), q.astype(F32)
    low = lax.broadcasted_iota(jnp.int32, p.shape, 1) < TAIL
    p_turned, q_turned = pltpu.roll(p, TAIL, 1), pltpu.roll(q, TAIL, 1)
    return jnp.where(low, p, q_turned), jnp.where(low, p_turned, q)


def forward_layer(m, l):
    z = sum(dot(shifted_rows(m.act3, r), m.w[l, 3 * CH * r : 3 * CH * (r + 1), :]) for r in range(3))
    z = z + m.bias[l : l + 1, 0:CH]
    for t in range(2):
        zt = z[t * PX : (t + 1) * PX]
        square = zt * zt
        th = jnp.tanh(GELU_C * (zt + 0.044715 * zt * square))
        half = 0.5 * (1.0 + th)
        a = zt * half
        m.slope[l, t * PX : (t + 1) * PX, :] = half + (0.5 * GELU_C) * zt * (1.0 - th * th) * (
            1.0 + (3 * 0.044715) * square
        )
        put_shifted(m.act3, t, a, 1, CH)
        if l + 1 < LAYERS:
            m.act_t[l + 1, :, t * PX : (t + 1) * PX] = a.T.astype(BF16)
        else:
            for i, moved in enumerate((moved_right(a), a, moved_left(a))):
                m.last_t[i, :, t * PX : (t + 1) * PX] = moved.T.astype(BF16)


def head_forward(m, lanes):
    for n in range(lanes.start, lanes.stop, 256):
        m.logits[:, n : n + 256] = sum(
            dot(shifted_rows(m.act3, r), m.wh[3 * CH * r : 3 * CH * (r + 1), n : n + 256]) for r in range(3)
        )


def expand(row, mask):
    lanes = row.shape[-1]
    return jnp.broadcast_to(row[:, None, :], (TILE, TILE, lanes)).reshape(PX, lanes) * mask[...].astype(F32)


def prepare_loss(m):
    for t, lab in enumerate((m.lab, m.lab_in)):
        codes = expand(lab[:, 0:LAB], m.mask_lab).astype(BF16)
        m.code[t * PX : (t + 1) * PX, :] = dot(codes, m.spread[...])

    @pl.when(m.role == 1)
    def _():
        for t, lab in enumerate((m.lab, m.lab_in)):
            values = expand(lab[:, LAB : LAB + TGT], m.mask_tgt)
            m.target[t * PX : (t + 1) * PX, :] = jnp.dot(
                values, m.targets[...].astype(F32), precision=lax.Precision.HIGHEST, preferred_element_type=F32
            )


def loss_gradient(m, lanes):
    total = m.count_sum[0:1, :] + m.count_in[1, 0:1, :] + m.count_in[2, 0:1, :] + m.count_in[3, 0:1, :]
    width = lanes.stop - lanes.start
    scale = jnp.concatenate([1.0 / jnp.maximum(total, 1.0)] * (width // LANES), axis=1)
    bias = m.bias[4:5, lanes]

    def keep(t, g):
        g = g.astype(BF16)
        m.grad_bias[4:5, lanes] += jnp.sum(g.astype(F32), axis=0, keepdims=True)
        m.gl[t, TILE : TILE + PX, lanes] = g

    @pl.when(m.role == 0)
    def _():
        for t in range(2):
            at = slice(t * PX, (t + 1) * PX)
            x = m.logits[at, lanes] + bias
            code = m.code[at, lanes]
            labeled = code == m.label[0:1, lanes]
            y = jnp.where(labeled, -x, x)
            e = jnp.exp(-jnp.abs(y))
            more = 1.0 + e
            q = jnp.where(y >= 0, 1.0, e) / more
            softplus = jnp.maximum(y, 0.0) + jnp.log(more)
            slope = q * q * (2.0 * (1.0 - q) * softplus + q)
            keep(t, slope * (jnp.where(labeled, -0.25, jnp.where(code > 0.5, 0.75, 0.0)) * scale))

    @pl.when(m.role == 1)
    def _():
        for t in range(2):
            at = slice(t * PX, (t + 1) * PX)
            if lanes.start < MAIN:
                offset = m.logits[at, lanes] + bias - m.target[at, lanes]
                g = jnp.where(m.code[at, lanes] > 1.5, jnp.clip(offset / huber_beta, -1.0, 1.0), 0.0)
                keep(t, g * scale)
            else:
                m.gl[t, TILE : TILE + PX, lanes] = jnp.zeros((PX, width), BF16)


def head_kernel_gradient(m, lanes, r):
    for s in range(3):
        at = (3 * r + s) * CH
        m.gh[at : at + CH, lanes] = dot(m.last_t[s], shifted_rows(m.gl, 2 - r, lanes)).astype(BF16)


def head_input_gradient(m):
    columns = []
    for s in range(3):
        acc = None
        for r in range(3):
            at = (3 * r + s) * CH
            part = dot_nt(shifted_rows(m.gl, 2 - r), m.wh[at : at + CH, :])
            acc = part if acc is None else acc + part
        columns.append(acc)
    for t in range(2):
        at = slice(t * PX, (t + 1) * PX)
        m.da[at, :] = moved_left(columns[0][at]) + columns[1][at] + moved_right(columns[2][at])


def input_gradient(m, g3, kernel):
    acc = None
    for r in range(3):
        for s in range(3):
            at = (3 * r + s) * CH
            part = dot_nt(shifted_rows(g3, 2 - r, slice(s * CH, (s + 1) * CH)), kernel[at : at + CH, :])
            acc = part if acc is None else acc + part
    return acc


def layer_upstream(m, l):
    g = (m.da[...] * m.slope[l]).astype(BF16).astype(F32)
    m.grad_bias[l : l + 1, 0:CH] = jnp.sum(g, axis=0, keepdims=True)
    for t in range(2):
        put_shifted(m.g3, t, g[t * PX : (t + 1) * PX], -1, CH)


def layer_kernel_gradient(m, l, r):
    part = dot(m.act_t[l], shifted_rows(m.g3, 2 - r))
    for s in range(3):
        at = (3 * r + s) * CH
        m.g[l, at : at + CH, :] = part[:, s * CH : (s + 1) * CH].astype(BF16)


class Traffic:
    def __init__(self, send_sem, recv_sem):
        self.send_sem, self.recv_sem = send_sem, recv_sem
        self.names, self.used, self.sent = {}, 0, []

    def copy(self, name, src, dst, peer, span=1, offset=0):
        if name not in self.names:
            self.names[name] = self.used
            self.used += span
        i = self.names[name] + offset
        return pltpu.make_async_remote_copy(
            src, dst, self.send_sem.at[i], self.recv_sem.at[i], device_id=peer, device_id_type=MESH
        )

    def send(self, name, src, dst, peer, when=None, **at):
        copy = self.copy(name, src, dst, peer, **at)
        if when is None:
            copy.start()
        else:
            pl.when(when)(copy.start)
        self.sent.append((when, copy))

    def arrived(self, name, dst, peer, **at):
        self.copy(name, dst, dst, peer, **at).wait_recv()

    def finish(self):
        for when, copy in self.sent:
            if when is None:
                copy.wait_send()
            else:
                pl.when(when)(copy.wait_send)


SEMAPHORES = 192
WAYS = {
    "T0": "A", "T1": "B", "T3": "A", "T2": "B", "M0": "B", "M1": "A", "M3": "B", "M2": "A", "U0": "A", "U1": "B", "U3": "A", "U2": "B",
}
SCHEDULE = (
    "aT0", "zT", "f", "aM0", "aT1", "bM0", "bT0", "zM", "e", "bT1", "aT3", "aT2", "cT1", "zU", "cM0", "bT3", "bT2",
    "aM2", "aM1", "aU0", "cT0", "aM3", "y", "aU1", "cT3", "cT2", "F0", "bM2", "F1", "bM3", "bM1", "aU2", "F2",
    "cM2", "bU0", "aU3", "F3", "cM1", "cM3", "bU2", "bU1", "cU0", "bU3", "HM", "cU3", "WM0", "WM1", "WM2", "cU2",
    "kM0", "cU1", "kM2", "kM3", "kM1", "HU", "X", "u3", "pM0", "pM3", "w3", "x3", "k3", "u2", "pM2", "w2", "pM1",
    "x2", "k2", "qM0", "u1", "x1", "w1", "qM2", "qM1", "p3", "u0", "WU0", "qM3", "WU1", "k1", "WU2", "w0", "p2",
    "k0", "q3", "p1", "x0", "kU2", "q2", "s3", "p0", "kU3", "Bk", "q1", "kU1", "kU0", "q0", "Bp", "D", "pU3", "s2",
    "pU0", "sM", "pU1", "Bq", "s1", "E", "pU2", "qU0", "s0", "qU3", "qU1", "qU2", "Bs", "t", "sU",
)


def head_kernel(
    features, tower_class, tower_boxes, head_class, head_boxes, bias_class, bias_boxes, head_class_bias, head_boxes_bias,
    state, labels, targets_in, valid, label, spread_any, targets_any, mask_lab_any, mask_tgt_any,
    out_features, out_towers, out_heads, out_bias,
    spread, targets, mask_lab, mask_tgt, bias, fetch_sem,
    own, own_h, w, wh, hp, g, gh, rc, rch, sm, su, r1a, r1b, r1m, r1u, r2, r2m, r2u, quarter, sum_m, sum_u, rz, rzm, rzu, done, layer_in,
    act3, g3, gl, act_t, last_t, slope, logits, code, target, da,
    x, lab, lab_in, count_mine, count_sum, count_in, grad_bias, bias_in, bias_z, dx, dx_in, tile_out, features_in,
    send_sem, recv_sem,
):
    s, dp = lax.axis_index("section"), lax.axis_index("dp")
    my_y, my_x, my_z, my_c = s // 2, s % 2, dp // 2, dp % 2
    sx, sy, sg = 2 * my_y + (1 - my_x), 2 * (1 - my_y) + my_x, 2 * (1 - my_y) + (1 - my_x)
    to_x, to_y, to_g, to_c = (sx, dp), (sy, dp), (sg, dp), (s, 2 * my_z + 1 - my_c)
    plane = lambda k: (my_z + k) % PLANES
    to_z = lambda k: (s, 2 * plane(k) + my_c)
    to_pair = (s, 2 * (my_z + 1 - 2 * (my_z % 2)) + my_c)
    role = my_z % 2
    net = Traffic(send_sem, recv_sem)
    m = SimpleNamespace(
        w=w, wh=wh, g=g, gh=gh, act3=act3, g3=g3, gl=gl, act_t=act_t, last_t=last_t, slope=slope, logits=logits, code=code,
        target=target, da=da, lab=lab, lab_in=lab_in, count_sum=count_sum, count_in=count_in, grad_bias=grad_bias,
        bias=bias, spread=spread, targets=targets, mask_lab=mask_lab, mask_tgt=mask_tgt, label=label, role=role,
    )

    def shard(z, c):
        return pl.ds(pl.multiple_of(ROWS * (2 * z + c), 16), ROWS)

    barrier = pltpu.get_barrier_semaphore()
    peers = (to_x, to_y, to_g, to_c, to_z(1), to_z(2), to_z(3))
    for peer in peers:
        pl.semaphore_signal(barrier, inc=1, device_id=peer, device_id_type=MESH)

    constants_in = [
        pltpu.make_async_copy(src, dst, fetch_sem.at[i])
        for i, (src, dst) in enumerate(
            ((mask_lab_any, mask_lab), (spread_any.at[role], spread), (mask_tgt_any, mask_tgt), (targets_any, targets))
        )
    ]
    for copy in constants_in:
        copy.start()

    for role_at, (tower, head) in enumerate(((tower_class, head_class), (tower_boxes, head_boxes))):
        own[role_at] = tower[0].astype(BF16)
        width = head.shape[0]
        main = min(width, LANES)
        own_h[role_at] = jnp.zeros((PACK, LANES), BF16)
        own_h[role_at, 0:ROWS, 0:main] = head[0:main, :].T.astype(BF16)
        if width > LANES:
            logits[0:ROWS, 0:LANES] = jnp.zeros((ROWS, LANES), F32)
            logits[0:ROWS, 0 : width - LANES] = head[LANES:width, :].T
            own_h[role_at, ROWS:PACK, :] = (
                logits[0:HALF, 0:LANES] + pltpu.roll(logits[HALF:ROWS, 0:LANES], TAIL, 1)
            ).astype(BF16)

    row = lax.broadcasted_iota(jnp.int32, (TILE, TILE * A), 0)
    found = jnp.zeros((TILE, TILE * A), F32)
    for t in range(SECTIONS):
        found += jnp.where(jnp.logical_and(state[t] == 1, row < valid[t]), 1.0, 0.0)
    count_mine[...] = jnp.full((8, LANES), jnp.sum(found), F32)
    inside = row < valid[s]
    kind = state[s]
    lab[...] = jnp.zeros_like(lab)
    lab[:, 0 : TILE * A] = jnp.where(
        inside,
        jnp.where(kind == 1, labels[s].astype(F32) + 2.0, jnp.where(kind == 2, 0.0, 1.0)),
        0.0,
    )
    lab[:, LAB : LAB + targets_in.shape[2]] = targets_in[s]

    pl.semaphore_wait(barrier, len(peers))

    def head_lanes(sec):
        return pl.ds(pl.multiple_of(LANES * sec, LANES), LANES)

    def place(kind_name, sec, z):
        if kind_name == "T":
            return w.at[sec, shard(z, my_c), :]
        if kind_name == "M":
            return wh.at[shard(z, my_c), head_lanes(sec)]
        return hp.at[sec, z]

    def own_shard(kind_name, which):
        if kind_name == "T":
            return own.at[which]
        return own_h.at[which, pl.ds(0, ROWS) if kind_name == "M" else pl.ds(ROWS, HALF), :]

    def planes_send(kind_name):
        for k in (1, 3, 2):
            net.send(
                ("z", kind_name, k), own_shard(kind_name, plane(k) % 2), place(kind_name, s, my_z), to_z(k)
            )

    in_plane = (("x", to_x, sx), ("y", to_y, sy), ("g", to_g, sg))

    def rows_of(sec):
        return pl.ds(pl.multiple_of(64 * sec, 64), 64)

    def features_send():
        for name, peer, sec in in_plane:
            net.send(("f", name), features.at[sec], x.at[0, rows_of(s), :], peer)
        net.send("count c", count_mine, count_in.at[0], to_c)
        net.send("lab", lab, lab_in, to_pair)

    def piece(kind_name, sec, j):
        return place(kind_name, sec, (my_z + PLANES - j) % PLANES)

    def ways(kind_name, j):
        if WAYS[kind_name + str(j)] == "A":
            return (to_x, sx), (to_y, sy)
        return (to_y, sy), (to_x, sx)

    def gather_mine(kind_name, j):
        mine = piece(kind_name, s, j)
        if j:
            net.arrived(("z", kind_name, j), mine, to_z(PLANES - j))
        for (n, _), name in zip(ways(kind_name, j), ("g1", "g2")):
            net.send((name, kind_name, j), mine, mine, n)
        if kind_name == "T":
            net.send(("swap", kind_name, j, 0), mine, mine, to_c)

    def gather_pass(kind_name, j):
        (n1, s1), (n2, s2) = ways(kind_name, j)
        first = piece(kind_name, s1, j)
        net.arrived(("g1", kind_name, j), first, n1)
        net.send(("g3", kind_name, j), first, first, n2)
        if kind_name == "T":
            net.send(("swap", kind_name, j, 1), first, first, to_c)

    def gather_last(kind_name, j):
        (n1, s1), (n2, s2) = ways(kind_name, j)
        for i, (name, sec) in enumerate((("g2", s2), ("g3", sg))):
            got = piece(kind_name, sec, j)
            net.arrived((name, kind_name, j), got, n2)
            if kind_name == "T":
                net.send(("swap", kind_name, j, 2 + i), got, got, to_c)
        z = (my_z + PLANES - j) % PLANES
        at = pl.multiple_of(ROWS * (2 * z + my_c), 16)
        if kind_name == "M":
            block = wh.at[pl.ds(at, ROWS), 0:MAIN]
            net.send(("swap", "M", j), block, block, to_c)
        if kind_name == "U":
            for q in range(2):
                lanes = slice((SECTIONS + q) * LANES, (SECTIONS + q + 1) * LANES)
                top, bottom = swap_halves(hp[2 * q, z], hp[2 * q + 1, z])
                wh[pl.ds(at, HALF), lanes] = top.astype(BF16)
                wh[pl.ds(at + HALF, HALF), lanes] = bottom.astype(BF16)
            block = wh.at[pl.ds(at, ROWS), MAIN:HEAD]
            net.send(("swap", "U", j), block, block, to_c)

    def swapped(kind_name, j):
        z = (my_z + PLANES - j) % PLANES
        if kind_name != "T":
            lanes = slice(0, MAIN) if kind_name == "M" else slice(MAIN, HEAD)
            net.arrived(("swap", kind_name, j), wh.at[shard(z, 1 - my_c), lanes], to_c)
            return
        (_, s1), (_, s2) = ways(kind_name, j)
        for i, sec in enumerate((s, s1, s2, sg)):
            net.arrived(("swap", "T", j, i), w.at[sec, shard(z, 1 - my_c), :], to_c)

    def features_tile():
        x[0, rows_of(s), :] = features[s]
        for name, peer, sec in in_plane:
            net.arrived(("f", name), x.at[0, rows_of(sec), :], peer)
        net.send("tile", x.at[0], x.at[1], to_pair)
        net.arrived("count c", count_in.at[0], to_c)
        count_sum[...] = count_mine[...] + count_in[0]
        for k in (1, 2, 3):
            net.send(("count", k), count_sum, count_in.at[k], to_z(k))

    def prepare():
        for ref in (act3, g3, gl):
            for t in range(2):
                ref[t, 0:TILE, :] = jnp.zeros((TILE, ref.shape[2]), BF16)
                ref[t, TILE + PX : 2 * TILE + PX, :] = jnp.zeros((TILE, ref.shape[2]), BF16)
        grad_bias[...] = jnp.zeros_like(grad_bias)
        for copy in constants_in:
            copy.wait()
        bias[0:LAYERS, 0:CH] = jnp.where(role == 0, bias_class[...], bias_boxes[...])
        bias[4:5, :] = jnp.where(role == 0, lay(head_class_bias[...]), lay(head_boxes_bias[...]))
        net.arrived("lab", lab_in, to_pair)
        prepare_loss(m)
        net.arrived("tile", x.at[1], to_pair)
        for t in range(2):
            v = x[t].astype(F32)
            put_shifted(act3, t, v, 1, CH)
            act_t[0, :, t * PX : (t + 1) * PX] = v.T.astype(BF16)

    def forward(l):
        if l == 0:
            for j in range(PLANES):
                swapped("T", j)
        forward_layer(m, l)

    def head(kind_name):
        if kind_name == "M":
            for k in (1, 2, 3):
                net.arrived(("count", k), count_in.at[k], to_z(PLANES - k))
        for j in range(PLANES):
            swapped(kind_name, j)
        head_forward(m, head_part[kind_name])
        loss_gradient(m, head_part[kind_name])

    head_part = dict(M=slice(0, MAIN), U=slice(MAIN, HEAD))
    w[s, shard(my_z, my_c), :] = own[role]
    wh[shard(my_z, my_c), head_lanes(s)] = own_h[role, 0:ROWS, :]
    hp[s, my_z] = own_h[role, ROWS:PACK, :]

    def added(*values):
        return sum(v.astype(F32) for v in values).astype(BF16)

    def half_rows(which):
        return pl.ds(pl.multiple_of(HALF * which, 16), HALF)

    def half_lanes(which):
        return pl.ds(pl.multiple_of(LANES * which, LANES), LANES)

    def core_send(l, zp):
        theirs = shard(zp, 1 - my_c)
        if l in head_part:
            net.send(("rc", l, zp), gh.at[theirs, head_part[l]], rch.at[zp, :, head_part[l]], to_c)
        else:
            net.send(("rc", l, zp), g.at[l, theirs, :], rc.at[l, zp], to_c)

    first, second = pl.ds(0, 2), pl.ds(2, 2)

    def tower_cores(l):
        for zp in range(PLANES):
            net.arrived(("rc", l, zp), rc.at[l, zp], to_c)
            rc[l, zp] = added(rc[l, zp], g[l, shard(zp, my_c), :])
            if zp == 1:
                net.send(("r1a", l), rc.at[l, first, :, half_lanes(1 - my_x)], r1a.at[l], to_x)
        net.send(("r1b", l), rc.at[l, second, half_rows(1 - my_y), :], r1b.at[l], to_y)

    def tower_plane(l):
        net.arrived(("r1a", l), r1a.at[l], to_x)
        for zp in (0, 1):
            rc[l, zp, :, half_lanes(my_x)] = added(rc[l, zp, :, half_lanes(my_x)], r1a[l, zp])
        net.send(("r2a", l), rc.at[l, first, half_rows(1 - my_y), half_lanes(my_x)], r2.at[l, first], to_y)
        net.arrived(("r1b", l), r1b.at[l], to_y)
        for zp in (2, 3):
            rc[l, zp, half_rows(my_y), :] = added(rc[l, zp, half_rows(my_y), :], r1b[l, zp - 2])
        net.send(("r2b", l), rc.at[l, second, half_rows(my_y), half_lanes(1 - my_x)], r2.at[l, second], to_x)

    def to_planes(name, src, dst):
        for zp in range(PLANES):
            k = (zp + PLANES - my_z) % PLANES
            net.send(name, src.at[zp], dst.at[my_z], (s, 2 * zp + my_c), my_z != zp, span=PLANES, offset=k)

    def tower_planes(l):
        net.arrived(("r2a", l), r2.at[l, first], to_y)
        net.arrived(("r2b", l), r2.at[l, second], to_x)
        for zp in range(PLANES):
            quarter[l, zp] = added(rc[l, zp, half_rows(my_y), half_lanes(my_x)], r2[l, zp])
        to_planes(("rz", l), quarter.at[l], rz.at[l])

    def from_planes(name, mine, others):
        for k in (1, 2, 3):
            net.arrived(name, others.at[plane(PLANES - k)], to_z(PLANES - k), span=PLANES, offset=k)
        same = mine[my_z].astype(F32) + others[plane(2)].astype(F32)
        return same, others[plane(1)].astype(F32) + others[plane(3)].astype(F32)

    def tower_sum(l):
        same, other = from_planes(("rz", l), quarter.at[l], rz.at[l])
        done[l, role] = same.astype(BF16)
        done[l, 1 - role] = other.astype(BF16)
        to_l = (l, dp)
        net.send("layer", done.at[l], layer_in.at[s], to_l, s != l, span=SECTIONS, offset=s)

        @pl.when(s == l)
        def _():
            out_towers[role, half_rows(my_y), half_lanes(my_x)] = same
            out_towers[1 - role, half_rows(my_y), half_lanes(my_x)] = other

    def tower_store():
        for sec, peer in ((sx, to_x), (sy, to_y), (sg, to_g)):
            net.arrived("layer", layer_in.at[sec], peer, span=SECTIONS, offset=sec)
            for i in range(2):
                out_towers[i, half_rows(sec // 2), half_lanes(sec % 2)] = layer_in[sec, i].astype(F32)

    def head_refs(kind_name):
        return (sm, r1m, r2m, sum_m, rzm) if kind_name == "M" else (su, r1u, r2u, sum_u, rzu)

    def head_cores(kind_name, zp):
        lanes = head_part[kind_name]
        net.arrived(("rc", kind_name, zp), rch.at[zp, :, lanes], to_c)
        at = pl.multiple_of(ROWS * (2 * zp + my_c), 16)
        into, landing = head_refs(kind_name)[:2]
        if kind_name == "M":
            for sec in range(SECTIONS):
                lanes = slice(sec * LANES, (sec + 1) * LANES)
                into[sec // 2, sec % 2, zp] = added(rch[zp, :, lanes], gh[pl.ds(at, ROWS), lanes])
        else:
            for q in range(2):
                lanes = slice((SECTIONS + q) * LANES, (SECTIONS + q + 1) * LANES)
                top = rch[zp, 0:HALF, lanes].astype(F32) + gh[pl.ds(at, HALF), lanes].astype(F32)
                bottom = rch[zp, HALF:ROWS, lanes].astype(F32) + gh[pl.ds(at + HALF, HALF), lanes].astype(F32)
                left, right = swap_halves(top, bottom)
                into[q, 0, zp] = left.astype(BF16)
                into[q, 1, zp] = right.astype(BF16)
        if zp % 2 == 0:
            net.send(("h1", kind_name, zp), into.at[:, 1 - my_x, zp], landing.at[zp], to_x)
        else:
            net.send(("h1", kind_name, zp), into.at[1 - my_y, :, zp], landing.at[zp], to_y)

    def head_plane(kind_name, zp):
        into, landing, landing2 = head_refs(kind_name)[:3]
        net.arrived(("h1", kind_name, zp), landing.at[zp], to_x if zp % 2 == 0 else to_y)
        for i in range(2):
            at = (i, my_x, zp) if zp % 2 == 0 else (my_y, i, zp)
            into[at] = added(into[at], landing[zp, i])
        if zp % 2 == 0:
            net.send(("h2", kind_name, zp), into.at[1 - my_y, my_x, zp], landing2.at[zp], to_y)
        else:
            net.send(("h2", kind_name, zp), into.at[my_y, 1 - my_x, zp], landing2.at[zp], to_x)

    def head_planes(kind_name, zp):
        into, _, landing2, total, others = head_refs(kind_name)
        net.arrived(("h2", kind_name, zp), landing2.at[zp], to_y if zp % 2 == 0 else to_x)
        total[zp] = added(into[my_y, my_x, zp], landing2[zp])
        k = (zp + PLANES - my_z) % PLANES
        net.send(
            ("hz", kind_name), total.at[zp], others.at[my_z], (s, 2 * zp + my_c), my_z != zp, span=PLANES, offset=k
        )

    def head_store(kind_name):
        total, others = head_refs(kind_name)[3:]
        same, other = from_planes(("hz", kind_name), total, others)
        at = slice(0, ROWS) if kind_name == "M" else slice(ROWS, PACK)
        out_heads[role, at] = same
        out_heads[1 - role, at] = other

    def bias_cores():
        net.arrived("bias c", bias_in.at[0], to_c)
        bias_z[0] = grad_bias[...] + bias_in[0]
        net.send("bias x", bias_z.at[0], bias_in.at[1], to_x)

    def bias_plane():
        net.arrived("bias x", bias_in.at[1], to_x)
        bias_z[1] = bias_z[0] + bias_in[1]
        net.send("bias y", bias_z.at[1], bias_in.at[2], to_y)

    def bias_planes():
        net.arrived("bias y", bias_in.at[2], to_y)
        bias_z[2] = bias_z[1] + bias_in[2]
        for k in (1, 2, 3):
            net.send(("bias z", k), bias_z.at[2], bias_in.at[2 + k], to_z(k))

    def bias_store():
        for k in (1, 2, 3):
            net.arrived(("bias z", k), bias_in.at[2 + k], to_z(PLANES - k))
        out_bias[role] = bias_z[2] + bias_in[4]
        out_bias[1 - role] = bias_in[3] + bias_in[5]

    def features_sum():
        net.arrived("dx", dx_in, to_pair)
        tile_out[...] = (da[0:PX, :] + dx_in[...].astype(F32)).astype(BF16)
        for name, peer, sec in in_plane:
            net.send(("b", name), tile_out.at[rows_of(sec), :], features_in.at[s], peer)

    def features_store():
        for name, peer, sec in in_plane:
            net.arrived(("b", name), features_in.at[sec], peer)
            out_features[sec] = features_in[sec]
        out_features[s] = tile_out[rows_of(s), :]

    def head_gradient(kind_name, r):
        head_kernel_gradient(m, head_part[kind_name], r)
        for zp in ((0,), (1,), (2, 3))[r]:
            core_send(kind_name, zp)

    def head_input():
        head_input_gradient(m)

    def upstream(l):
        layer_upstream(m, l)
        if l == 0:
            net.send("bias c", grad_bias, bias_in.at[0], to_c)

    def layer_gradient(l):
        for r in range(3):
            layer_kernel_gradient(m, l, r)
            for zp in ((0,), (1,), (2, 3))[r]:
                core_send(l, zp)

    def layer_input(l):
        da[...] = input_gradient(m, g3, w.at[l])
        if l == 0:
            dx[...] = da[PX : 2 * PX, :].astype(BF16)
            net.send("dx", dx, dx_in, to_pair)

    def either(of_head, of_tower):
        return lambda *which: of_head(*which) if which[0] in head_part else of_tower(*which)

    steps = dict(
        z=planes_send, f=features_send, e=features_tile, y=prepare, a=gather_mine, b=gather_pass, c=gather_last,
        F=forward, H=head, W=head_gradient, X=head_input, u=upstream, w=layer_gradient, x=layer_input,
        k=either(head_cores, tower_cores), p=either(head_plane, tower_plane), q=either(head_planes, tower_planes),
        s=either(head_store, tower_sum), t=tower_store, D=features_sum, E=features_store,
        B=lambda which: dict(k=bias_cores, p=bias_plane, q=bias_planes, s=bias_store)[which](),
    )
    for step in SCHEDULE:
        steps[step[0]](*(int(v) if v.isdigit() else v for v in step[1:]))
    net.finish()


def lay(vector):
    width = vector.shape[0]
    per = width // SECTIONS
    row = jnp.concatenate([vector.reshape(1, width), jnp.zeros((1, HEAD - width), F32)], axis=1)
    row = jnp.broadcast_to(row, (8, HEAD))
    lane = lax.broadcasted_iota(jnp.int32, (8, LANES), 1)
    main, tails = [], []
    for s in range(SECTIONS):
        turned = pltpu.roll(row, (HEAD - s * per) % HEAD, 1)
        main.append(jnp.where(lane < per, turned[:, 0:LANES], 0.0))
        tails.append(jnp.where(lane < per - LANES, turned[:, LANES : 2 * LANES], 0.0))
    folded = [tails[2 * q] + pltpu.roll(tails[2 * q + 1], TAIL, 1) for q in range(2)]
    return jnp.concatenate(main + folded, axis=1)[0:1, :]


def unlay(row, width):
    per = width // SECTIONS
    row = jnp.broadcast_to(row, (8, HEAD))
    lane = lax.broadcasted_iota(jnp.int32, (8, LANES), 1)
    total = jnp.zeros((8, HEAD), F32)
    for s in range(SECTIONS):
        tail = row[:, MAIN + (s // 2) * LANES : MAIN + (s // 2 + 1) * LANES]
        tail = pltpu.roll(tail, TAIL, 1) if s % 2 else tail
        parts = [jnp.where(lane < per, row[:, s * LANES : (s + 1) * LANES], 0.0), jnp.where(lane < per - LANES, tail, 0.0)]
        total += pltpu.roll(jnp.concatenate(parts + [jnp.zeros((8, HEAD - 2 * LANES), F32)], axis=1), s * per, 1)
    return total[0:1, 0:width].reshape(width)


def finish_kernel(
    features, towers, heads, sums,
    out_features, out_class, out_bias_class, out_boxes, out_bias_boxes, out_head_class, out_head_class_bias,
    out_head_boxes, out_head_boxes_bias,
):
    out_features[...] = features[...]
    for i, (tower, bias, head, head_bias) in enumerate(
        (
            (out_class, out_bias_class, out_head_class, out_head_class_bias),
            (out_boxes, out_bias_boxes, out_head_boxes, out_head_boxes_bias),
        )
    ):
        tower[0] = towers[i]
        bias[...] = sums[i, 0:LAYERS, 0:CH]
        width = head.shape[0]
        main, rest = min(width, LANES), max(0, width - LANES)
        head[0:main, :] = heads[i, 0:ROWS, :].T[0:main, :]
        if rest:
            low = heads[i, ROWS:PACK, :]
            both = jnp.concatenate([low, pltpu.roll(low, TAIL, 1)], axis=0)
            head[LANES:width, :] = both.T[0:rest, :]
        head_bias[...] = unlay(sums[i, LAYERS : LAYERS + 1, :], head_bias.shape[0])


def fast(features, tower_class, bias_class, tower_boxes, bias_boxes, head_class, head_class_bias, head_boxes,
         head_boxes_bias, anchor_state, class_labels, box_targets, valid_rows):
    class_width, boxes_width = head_class_bias.shape[0], head_boxes_bias.shape[0]
    spread, targets, mask_lab, mask_tgt, label = constants(class_width, boxes_width)
    tiles = features.shape[0]
    vmem = pl.BlockSpec(memory_space=pltpu.VMEM)
    smem = pl.BlockSpec(memory_space=pltpu.SMEM)
    v = lambda shape, dtype: pltpu.VMEM(shape, dtype)
    out = lambda shape, dtype: jax.ShapeDtypeStruct(shape, dtype)
    anywhere = pl.BlockSpec(memory_space=pl.ANY)
    raw = pl.pallas_call(
        head_kernel,
        out_shape=(
            out((tiles, 64, CH), BF16),
            out((2, ROWS, CH), F32),
            out((2, PACK, LANES), F32),
            out((2, 8, HEAD), F32),
        ),
        in_specs=[vmem] * 12 + [smem, vmem] + [anywhere] * 4,
        out_specs=(vmem,) * 4,
        scratch_shapes=[
            v(spread.shape[1:], BF16),
            v(targets.shape, BF16),
            v(mask_lab.shape, BF16),
            v(mask_tgt.shape, BF16),
            v((8, HEAD), F32),
            pltpu.SemaphoreType.DMA((4,)),
            v((2, ROWS, CH), BF16),
            v((2, PACK, LANES), BF16),
            v((LAYERS, DEEP, CH), BF16),
            v((DEEP, HEAD), BF16),
            v((SECTIONS, PLANES, HALF, LANES), BF16),
            v((LAYERS, DEEP, CH), BF16),
            v((DEEP, HEAD), BF16),
            v((LAYERS, PLANES, ROWS, CH), BF16),
            v((PLANES, ROWS, HEAD), BF16),
            v((2, 2, PLANES, ROWS, LANES), BF16),
            v((2, 2, PLANES, HALF, LANES), BF16),
            v((LAYERS, 2, ROWS, LANES), BF16),
            v((LAYERS, 2, HALF, CH), BF16),
            v((PLANES, 2, ROWS, LANES), BF16),
            v((PLANES, 2, HALF, LANES), BF16),
            v((LAYERS, PLANES, HALF, LANES), BF16),
            v((PLANES, ROWS, LANES), BF16),
            v((PLANES, HALF, LANES), BF16),
            v((LAYERS, PLANES, HALF, LANES), BF16),
            v((PLANES, ROWS, LANES), BF16),
            v((PLANES, HALF, LANES), BF16),
            v((LAYERS, PLANES, HALF, LANES), BF16),
            v((PLANES, ROWS, LANES), BF16),
            v((PLANES, HALF, LANES), BF16),
            v((LAYERS, 2, HALF, LANES), BF16),
            v((SECTIONS, 2, HALF, LANES), BF16),
            v((2, PX + 2 * TILE, 3 * CH), BF16),
            v((2, PX + 2 * TILE, 3 * CH), BF16),
            v((2, PX + 2 * TILE, HEAD), BF16),
            v((LAYERS, CH, 2 * PX), BF16),
            v((3, CH, 2 * PX), BF16),
            v((LAYERS, 2 * PX, CH), F32),
            v((2 * PX, HEAD), F32),
            v((2 * PX, HEAD), F32),
            v((2 * PX, MAIN), F32),
            v((2 * PX, CH), F32),
            v((2, PX, CH), BF16),
            v((TILE, LAB + TGT), F32),
            v((TILE, LAB + TGT), F32),
            v((8, LANES), F32),
            v((8, LANES), F32),
            v((4, 8, LANES), F32),
            v((8, HEAD), F32),
            v((6, 8, HEAD), F32),
            v((3, 8, HEAD), F32),
            v((PX, CH), BF16),
            v((PX, CH), BF16),
            v((PX, CH), BF16),
            v((SECTIONS, 64, CH), BF16),
            pltpu.SemaphoreType.DMA((SEMAPHORES,)),
            pltpu.SemaphoreType.DMA((SEMAPHORES,)),
        ],
        compiler_params=pltpu.CompilerParams(
            collective_id=0, has_side_effects=True, vmem_limit_bytes=62 * 2**20
        ),
    )(
        features.reshape(tiles, 64, CH), tower_class, tower_boxes, head_class.T, head_boxes.T, bias_class, bias_boxes,
        head_class_bias, head_boxes_bias, anchor_state, class_labels, box_targets, valid_rows, label,
        spread, targets, mask_lab, mask_tgt,
    )
    results = pl.pallas_call(
        finish_kernel,
        out_shape=(
            out((tiles, 64, CH), BF16),
            out(tower_class.shape, F32),
            out(bias_class.shape, F32),
            out(tower_boxes.shape, F32),
            out(bias_boxes.shape, F32),
            out(head_class.shape[::-1], F32),
            out(head_class_bias.shape, F32),
            out(head_boxes.shape[::-1], F32),
            out(head_boxes_bias.shape, F32),
        ),
        in_specs=[vmem] * 4,
        out_specs=(vmem,) * 9,
    )(*raw)
    of_features, of_class, of_bias_class, of_boxes, of_bias_boxes, of_head_class, *rest = results
    of_head_class_bias, of_head_boxes, of_head_boxes_bias = rest
    return (
        of_features.reshape(features.shape), of_class, of_bias_class, of_boxes, of_bias_boxes,
        of_head_class.T, of_head_class_bias, of_head_boxes.T, of_head_boxes_bias,
    )


def shifted(block, axis, distance):
    devices = range(lax.axis_size(axis))
    route = [(i - distance, i) for i in devices if i - distance in devices]
    return lax.ppermute(block, axis, route)


def anchor_masks(anchor_state, valid_rows):
    tile_count = anchor_state.shape[0]
    anchor_kind = anchor_state.reshape(tile_count, TILE, TILE, A)
    row_index = lax.broadcasted_iota(jnp.int32, (tile_count, TILE, 1, 1), 1)
    inside = row_index < valid_rows.reshape(tile_count, 1, 1, 1)
    positive = jnp.logical_and(anchor_kind == 1, inside).astype(jnp.float32)
    counted = jnp.logical_and(anchor_kind != 2, inside).astype(jnp.float32)
    return (positive, counted)


def head_loss(logits, box_values, positive, counted, class_labels, box_targets, normalizer):
    tile_count = logits.shape[0]
    scores = logits.reshape(tile_count, TILE, TILE, A, K)
    labels = class_labels.reshape(tile_count, TILE, TILE, A, 1)
    classes = lax.broadcasted_iota(jnp.int32, (1, 1, 1, 1, K), 4)
    target = (labels == classes).astype(jnp.float32) * positive[..., None]
    chance = jax.nn.sigmoid(scores)
    entropy = jax.nn.softplus(scores) - target * scores
    agreement = chance * target + (1.0 - chance) * (1.0 - target)
    balance = 0.25 * target + 0.75 * (1.0 - target)
    focal_terms = balance * (1.0 - agreement) ** 2 * entropy
    focal_sum = jnp.sum(focal_terms * counted[..., None])
    offsets = box_values.reshape(tile_count, TILE, TILE, A, 4) - box_targets.reshape(
        tile_count, TILE, TILE, A, 4
    )
    spread = jnp.abs(offsets)
    huber_terms = jnp.where(
        spread < huber_beta, 0.5 * offsets * offsets / huber_beta, spread - 0.5 * huber_beta
    )
    box_sum = jnp.sum(huber_terms * positive[..., None])
    return (focal_sum + box_sum) / normalizer


def unfold(values):
    tile_count, tile_side, channels = (values.shape[0], values.shape[1], values.shape[3])
    padded = jnp.pad(values, ((0, 0), (1, 1), (1, 1), (0, 0)))
    pieces = [
        padded[:, row_shift : row_shift + tile_side, col_shift : col_shift + tile_side, :]
        for row_shift in range(3)
        for col_shift in range(3)
    ]
    return jnp.concatenate(pieces, axis=-1).reshape(
        tile_count * tile_side * tile_side, 9 * channels
    )


def fold_back(columns, tile_count, tile_side, channels):
    shaped = columns.reshape(tile_count, tile_side, tile_side, 9 * channels)
    padded = jnp.zeros((tile_count, tile_side + 2, tile_side + 2, channels), jnp.float32)
    for tap_index in range(9):
        row_shift = tap_index // 3
        col_shift = tap_index % 3
        padded = padded.at[
            :, row_shift : row_shift + tile_side, col_shift : col_shift + tile_side, :
        ].add(shaped[..., tap_index * channels : (tap_index + 1) * channels])
    return padded[:, 1 : tile_side + 1, 1 : tile_side + 1, :]


def weight_grad(columns, upstream):
    return jnp.einsum("pk,pc->kc", columns, upstream, preferred_element_type=jnp.float32)


def input_cols(upstream, weight):
    return jnp.einsum("pc,kc->pk", upstream, weight, preferred_element_type=jnp.float32)


def pick(buffer, slot_index):
    return lax.dynamic_index_in_dim(buffer, slot_index, 0, keepdims=False)


def store(buffer, update, slot_index, active):
    return lax.dynamic_update_index_in_dim(
        buffer, jnp.where(active, update, pick(buffer, slot_index)), slot_index, 0
    )


def per_device(
    features,
    tower_class,
    bias_class,
    tower_boxes,
    bias_boxes,
    head_class,
    head_class_bias,
    head_boxes,
    head_boxes_bias,
    anchor_state,
    class_labels,
    box_targets,
    valid_rows,
):
    section_count = lax.axis_size("section")
    section_index = lax.axis_index("section")
    final_section = section_count - 1
    is_first = section_index == 0
    is_final = section_index == final_section
    tile_dev = features.shape[0]
    per_micro = tile_dev // MICRO
    whole = lax.all_gather(features, "section", axis=1, tiled=True)
    tile_side = whole.shape[1]
    channels = whole.shape[3]
    pixels = per_micro * tile_side * tile_side
    act_shape = (per_micro, tile_side, tile_side, channels)
    positive, counted = anchor_masks(anchor_state, valid_rows)
    found = lax.psum(jnp.sum(positive), "dp")
    normalizer = jnp.maximum(found, 1.0)
    gathered = (
        lax.all_gather(tower_class.astype(jnp.bfloat16), "dp", axis=1, tiled=True),
        lax.all_gather(tower_boxes.astype(jnp.bfloat16), "dp", axis=1, tiled=True),
        lax.all_gather(head_class.astype(jnp.bfloat16), "dp", axis=0, tiled=True),
        lax.all_gather(head_boxes.astype(jnp.bfloat16), "dp", axis=0, tiled=True),
    )
    weight_class = gathered[0][0]
    weight_boxes = gathered[1][0]
    head_weight_class, head_weight_boxes = (
        lax.all_gather(gathered[2], "section", axis=1, tiled=True),
        lax.all_gather(gathered[3], "section", axis=1, tiled=True),
    )
    layer_bias_class = lax.dynamic_index_in_dim(bias_class, section_index, 0, keepdims=False)
    layer_bias_boxes = lax.dynamic_index_in_dim(bias_boxes, section_index, 0, keepdims=False)
    class_width = head_weight_class.shape[1]
    boxes_width = head_weight_boxes.shape[1]
    patch_width = head_weight_class.shape[0]

    def head_pass(stored_class, stored_boxes, slot_index):
        cols_class = unfold(stored_class)
        cols_boxes = unfold(stored_boxes)
        logits = (
            jnp.dot(cols_class, head_weight_class, preferred_element_type=jnp.float32)
            + head_class_bias
        )
        box_values = (
            jnp.dot(cols_boxes, head_weight_boxes, preferred_element_type=jnp.float32)
            + head_boxes_bias
        )
        start = slot_index * per_micro
        pos_here = lax.dynamic_slice_in_dim(positive, start, per_micro, 0)
        counted_here = lax.dynamic_slice_in_dim(counted, start, per_micro, 0)
        labels_here = lax.dynamic_slice_in_dim(class_labels, start, per_micro, 0)
        targets_here = lax.dynamic_slice_in_dim(box_targets, start, per_micro, 0)

        def local_loss(logit_part, box_part):
            return head_loss(
                logit_part.reshape(per_micro, tile_side, tile_side, class_width),
                box_part.reshape(per_micro, tile_side, tile_side, boxes_width),
                pos_here,
                counted_here,
                labels_here,
                targets_here,
                normalizer,
            )

        total_loss, pullback = jax.vjp(local_loss, logits, box_values)
        grad_logits, grad_box = pullback(jnp.ones_like(total_loss))
        grad_logits = grad_logits.astype(jnp.bfloat16)
        grad_box = grad_box.astype(jnp.bfloat16)
        back_class = fold_back(
            input_cols(grad_logits, head_weight_class), per_micro, tile_side, channels
        )
        back_boxes = fold_back(
            input_cols(grad_box, head_weight_boxes), per_micro, tile_side, channels
        )
        return (
            weight_grad(cols_class, grad_logits),
            weight_grad(cols_boxes, grad_box),
            jnp.sum(grad_logits.astype(jnp.float32), 0),
            jnp.sum(grad_box.astype(jnp.float32), 0),
            back_class,
            back_boxes,
        )

    def head_spare(stored_class, stored_boxes, slot_index):
        return (
            jnp.zeros((patch_width, class_width), jnp.float32),
            jnp.zeros((patch_width, boxes_width), jnp.float32),
            jnp.zeros((class_width,), jnp.float32),
            jnp.zeros((boxes_width,), jnp.float32),
            jnp.zeros(act_shape, jnp.float32),
            jnp.zeros(act_shape, jnp.float32),
        )

    kept_class = jnp.zeros((MICRO,) + act_shape, jnp.bfloat16)
    kept_boxes = jnp.zeros((MICRO,) + act_shape, jnp.bfloat16)
    kept_pre_class = jnp.zeros((MICRO, pixels, channels), jnp.float32)
    kept_pre_boxes = jnp.zeros((MICRO, pixels, channels), jnp.float32)
    head_back_class = jnp.zeros((MICRO,) + act_shape, jnp.float32)
    head_back_boxes = jnp.zeros((MICRO,) + act_shape, jnp.float32)
    grad_head_class = jnp.zeros((patch_width, class_width), jnp.float32)
    grad_head_boxes = jnp.zeros((patch_width, boxes_width), jnp.float32)
    grad_hbias_class = jnp.zeros((class_width,), jnp.float32)
    grad_hbias_boxes = jnp.zeros((boxes_width,), jnp.float32)
    total_moments = MICRO + section_count - 1
    empty_act = jnp.zeros(act_shape, jnp.bfloat16)
    received = (empty_act, empty_act)
    for moment in range(total_moments):
        micro_index = moment - section_index
        active = jnp.logical_and(micro_index >= 0, micro_index < MICRO)
        slot_index = jnp.clip(micro_index, 0, MICRO - 1)
        if moment < MICRO:
            entering = whole[moment * per_micro : (moment + 1) * per_micro]
        else:
            entering = empty_act
        input_class = jnp.where(is_first, entering, received[0])
        input_boxes = jnp.where(is_first, entering, received[1])
        kept_class = store(kept_class, input_class, slot_index, active)
        kept_boxes = store(kept_boxes, input_boxes, slot_index, active)
        pre_class = (
            jnp.dot(unfold(input_class), weight_class, preferred_element_type=jnp.float32)
            + layer_bias_class
        )
        pre_boxes = (
            jnp.dot(unfold(input_boxes), weight_boxes, preferred_element_type=jnp.float32)
            + layer_bias_boxes
        )
        kept_pre_class = store(kept_pre_class, pre_class, slot_index, active)
        kept_pre_boxes = store(kept_pre_boxes, pre_boxes, slot_index, active)
        act_class = jax.nn.gelu(pre_class).astype(jnp.bfloat16).reshape(act_shape)
        act_boxes = jax.nn.gelu(pre_boxes).astype(jnp.bfloat16).reshape(act_shape)
        results = lax.cond(
            jnp.logical_and(is_final, active),
            head_pass,
            head_spare,
            act_class,
            act_boxes,
            slot_index,
        )
        grad_head_class = grad_head_class + results[0]
        grad_head_boxes = grad_head_boxes + results[1]
        grad_hbias_class = grad_hbias_class + results[2]
        grad_hbias_boxes = grad_hbias_boxes + results[3]
        head_back_class = store(head_back_class, results[4], slot_index, active)
        head_back_boxes = store(head_back_boxes, results[5], slot_index, active)
        if moment < total_moments - 1:
            received = shifted((act_class, act_boxes), "section", 1)
    grad_layer_class = jnp.zeros((patch_width, channels), jnp.float32)
    grad_layer_boxes = jnp.zeros((patch_width, channels), jnp.float32)
    grad_lbias_class = jnp.zeros((channels,), jnp.float32)
    grad_lbias_boxes = jnp.zeros((channels,), jnp.float32)
    input_back = jnp.zeros((MICRO,) + act_shape, jnp.float32)
    returned = (empty_act, empty_act)
    for moment in range(total_moments):
        micro_index = moment - (final_section - section_index)
        active = jnp.logical_and(micro_index >= 0, micro_index < MICRO)
        slot_index = jnp.clip(micro_index, 0, MICRO - 1)
        upstream_class = jnp.where(
            is_final, pick(head_back_class, slot_index), returned[0].astype(jnp.float32)
        ).reshape(pixels, channels)
        upstream_boxes = jnp.where(
            is_final, pick(head_back_boxes, slot_index), returned[1].astype(jnp.float32)
        ).reshape(pixels, channels)
        cols_class = unfold(pick(kept_class, slot_index))
        cols_boxes = unfold(pick(kept_boxes, slot_index))
        pre_class = pick(kept_pre_class, slot_index)
        pre_boxes = pick(kept_pre_boxes, slot_index)
        gelu_class = jax.vjp(jax.nn.gelu, pre_class)[1](upstream_class)[0]
        gelu_boxes = jax.vjp(jax.nn.gelu, pre_boxes)[1](upstream_boxes)[0]
        grad_pre_class = jnp.where(active, gelu_class, 0.0).astype(jnp.bfloat16)
        grad_pre_boxes = jnp.where(active, gelu_boxes, 0.0).astype(jnp.bfloat16)
        grad_layer_class = grad_layer_class + weight_grad(cols_class, grad_pre_class)
        grad_layer_boxes = grad_layer_boxes + weight_grad(cols_boxes, grad_pre_boxes)
        grad_lbias_class = grad_lbias_class + jnp.sum(grad_pre_class.astype(jnp.float32), 0)
        grad_lbias_boxes = grad_lbias_boxes + jnp.sum(grad_pre_boxes.astype(jnp.float32), 0)
        back_class = fold_back(
            input_cols(grad_pre_class, weight_class), per_micro, tile_side, channels
        )
        back_boxes = fold_back(
            input_cols(grad_pre_boxes, weight_boxes), per_micro, tile_side, channels
        )
        input_back = store(
            input_back, back_class + back_boxes, slot_index, jnp.logical_and(active, is_first)
        )
        if moment < total_moments - 1:
            returned = shifted(
                (back_class.astype(jnp.bfloat16), back_boxes.astype(jnp.bfloat16)), "section", -1
            )
    spread_back = jnp.where(
        is_first, input_back.reshape(tile_dev, tile_side, tile_side, channels), 0.0
    )
    grad_features = lax.psum_scatter(
        spread_back.astype(jnp.bfloat16), "section", scatter_dimension=1, tiled=True
    )
    summed = (
        lax.psum_scatter(grad_layer_class, "dp", scatter_dimension=0, tiled=True),
        lax.psum_scatter(grad_layer_boxes, "dp", scatter_dimension=0, tiled=True),
        lax.psum_scatter(grad_head_class, "dp", scatter_dimension=0, tiled=True),
        lax.psum_scatter(grad_head_boxes, "dp", scatter_dimension=0, tiled=True),
    )
    final_head_class, final_head_boxes = (
        lax.psum_scatter(
            summed[2].astype(jnp.bfloat16), "section", scatter_dimension=1, tiled=True
        ).astype(jnp.float32),
        lax.psum_scatter(
            summed[3].astype(jnp.bfloat16), "section", scatter_dimension=1, tiled=True
        ).astype(jnp.float32),
    )
    rows_class = lax.dynamic_update_index_in_dim(
        jnp.zeros((LAYERS, channels), jnp.float32), grad_lbias_class, section_index, 0
    )
    rows_boxes = lax.dynamic_update_index_in_dim(
        jnp.zeros((LAYERS, channels), jnp.float32), grad_lbias_boxes, section_index, 0
    )
    bias_sums = lax.psum(
        (rows_class, rows_boxes, grad_hbias_class, grad_hbias_boxes), ("section", "dp")
    )
    return (
        grad_features,
        summed[0][None],
        bias_sums[0],
        summed[1][None],
        bias_sums[1],
        final_head_class,
        bias_sums[2],
        final_head_boxes,
        bias_sums[3],
    )


def solution(mesh):
    fits = mesh.shape["section"] == SECTIONS == LAYERS and mesh.shape["dp"] == PLANES * CORES
    placed = (
        P("dp", "section", None, None),
        P("section", "dp", None),
        P(),
        P("section", "dp", None),
        P(),
        P("dp", "section"),
        P(),
        P("dp", "section"),
        P(),
        P("dp", None, None),
        P("dp", None, None),
        P("dp", None, None),
        P("dp"),
    )
    return jax.shard_map(
        fast if fits else per_device,
        mesh=mesh,
        in_specs=placed,
        out_specs=(
            P("dp", "section", None, None),
            P("section", "dp", None),
            P(),
            P("section", "dp", None),
            P(),
            P("dp", "section"),
            P(),
            P("dp", "section"),
            P(),
        ),
        check_vma=False,
    )
```

```python
import functools
import math
from types import SimpleNamespace

import jax
import jax.numpy as jnp
import numpy as np
from jax import lax
from jax.experimental import pallas as pl
from jax.experimental.pallas import tpu as pltpu
from jax.sharding import PartitionSpec as P

K = 80
A = 9
LAYERS = 4
TILE = 16
MICRO = 4


huber_beta = 1.0 / 9.0

F32 = jnp.float32
BF16 = jnp.bfloat16
MESH = pl.DeviceIdType.MESH
GELU_C = math.sqrt(2.0 / math.pi)

SECTIONS = 4
PLANES = 4
CORES = 2
CH = 256
PX = TILE * TILE
ROWS = 288
HALF = ROWS // 2
PACK = ROWS + HALF
LANES = 128
TAIL = 64
MAIN = SECTIONS * LANES
HEAD = MAIN + SECTIONS * TAIL
LAB = 256
TGT = 640
DEEP = 9 * CH
FOLD = 3
FOLD_ROWS = ROWS // FOLD
FOLD_LANES = 32


def head_layout(width):
    per = width // SECTIONS
    columns = np.full((HEAD,), -1)
    for s in range(SECTIONS):
        main = min(per, LANES)
        columns[s * LANES : s * LANES + main] = s * per + np.arange(main)
        rest = per - main
        at = SECTIONS * LANES + s * TAIL
        columns[at : at + rest] = s * per + main + np.arange(rest)
    return columns


def constants(class_width, boxes_width):
    classes, boxes = head_layout(class_width), head_layout(boxes_width)
    spread = np.zeros((2, LAB, HEAD), np.float32)
    targets = np.zeros((TGT, MAIN), np.float32)
    for j in range(TILE):
        for col in range(HEAD):
            if classes[col] >= 0:
                spread[0, j * A + classes[col] // K, col] = 1
            if boxes[col] >= 0:
                spread[1, j * A + boxes[col] // 4, col] = 1
                targets[j * boxes_width + boxes[col], col] = 1
    pixel = np.arange(PX)[:, None] % TILE
    mask_lab = (np.arange(LAB)[None, :] // A == pixel) & (np.arange(LAB)[None, :] < TILE * A)
    mask_tgt = (np.arange(TGT)[None, :] // boxes_width == pixel) & (np.arange(TGT)[None, :] < TILE * boxes_width)
    label = np.where(classes >= 0, classes % K, -9).astype(np.float32)[None, :] + 2.0
    bf = lambda v: jnp.asarray(v.astype(np.float32), BF16)
    return bf(spread), bf(targets), bf(mask_lab), bf(mask_tgt), jnp.asarray(np.repeat(label, 8, 0))


def dot(a, b):
    return jnp.dot(a, b, preferred_element_type=F32)


def dot_nt(a, b):
    return lax.dot_general(a, b, (((1,), (1,)), ((), ())), preferred_element_type=F32)


def moved_right(v):
    col = lax.broadcasted_iota(jnp.int32, v.shape, 0) % TILE
    return jnp.where(col == 0, 0.0, pltpu.roll(v, 1, 0))


def moved_left(v):
    col = lax.broadcasted_iota(jnp.int32, v.shape, 0) % TILE
    return jnp.where(col == TILE - 1, 0.0, pltpu.roll(v, PX - 1, 0))


def put_shifted(ref, t, v, order, width):
    blocks = (moved_right(v), v, moved_left(v))[::order]
    for s, block in enumerate(blocks):
        ref[t, TILE : TILE + PX, s * width : (s + 1) * width] = block.astype(BF16)


def shifted_rows(ref, r, lanes=slice(None)):
    return ref[:, TILE * r : TILE * r + PX, lanes].reshape(2 * PX, -1)


def swap_halves(p, q):
    p, q = p.astype(F32), q.astype(F32)
    low = lax.broadcasted_iota(jnp.int32, p.shape, 1) < TAIL
    p_turned, q_turned = pltpu.roll(p, TAIL, 1), pltpu.roll(q, TAIL, 1)
    return jnp.where(low, p, q_turned), jnp.where(low, p_turned, q)


def folded(v):
    parts = [v[i * FOLD_ROWS : (i + 1) * FOLD_ROWS] for i in range(FOLD)]
    return parts[0] + sum(pltpu.roll(part, i * FOLD_LANES, 1) for i, part in enumerate(parts) if i)


def unfolded(v):
    v = v.astype(F32)
    low = lax.broadcasted_iota(jnp.int32, v.shape, 1) < FOLD_LANES
    return [
        jnp.where(low, pltpu.roll(v, LANES - i * FOLD_LANES, 1) if i else v, 0.0) for i in range(FOLD)
    ]


def conv(act3, t, kernel, lanes=slice(None)):
    return sum(
        dot(act3[t, TILE * r : TILE * r + PX, :], kernel[3 * CH * r : 3 * CH * (r + 1), lanes]) for r in range(3)
    )


def forward_layer(m, l):
    for t in range(2):
        z = conv(m.act3, t, m.w.at[l]) + m.bias[l : l + 1, 0:CH]
        square = z * z
        th = jnp.tanh(GELU_C * (z + 0.044715 * z * square))
        half = 0.5 * (1.0 + th)
        a = z * half
        m.slope[l, t * PX : (t + 1) * PX, :] = half + (0.5 * GELU_C) * z * (1.0 - th * th) * (
            1.0 + (3 * 0.044715) * square
        )
        put_shifted(m.act3, t, a, 1, CH)
        if l + 1 < LAYERS:
            m.act_t[l + 1, :, t * PX : (t + 1) * PX] = a.T.astype(BF16)
        else:
            for i, moved in enumerate((moved_right(a), a, moved_left(a))):
                m.last_t[i, :, t * PX : (t + 1) * PX] = moved.T.astype(BF16)


def expand(row, mask):
    lanes = row.shape[-1]
    return jnp.broadcast_to(row[:, None, :], (TILE, TILE, lanes)).reshape(PX, lanes) * mask[...].astype(F32)


def prepare_loss(m):
    for t, lab in enumerate((m.lab, m.lab_in)):
        codes = expand(lab[:, 0:LAB], m.mask_lab).astype(BF16)
        m.code[t * PX : (t + 1) * PX, :] = dot(codes, m.spread[...])

    @pl.when(m.role == 1)
    def _():
        for t, lab in enumerate((m.lab, m.lab_in)):
            values = expand(lab[:, LAB : LAB + TGT], m.mask_tgt)
            m.target[t * PX : (t + 1) * PX, :] = jnp.dot(
                values, m.targets[...].astype(F32), precision=lax.Precision.HIGHEST, preferred_element_type=F32
            )


def head_gradients(m, lanes):
    total = m.count_sum[0:1, :] + m.count_in[1, 0:1, :] + m.count_in[2, 0:1, :] + m.count_in[3, 0:1, :]
    scale = jnp.concatenate([1.0 / jnp.maximum(total, 1.0)] * 2, axis=1)

    def of_class(x, t, at):
        code = m.code[t * PX : (t + 1) * PX, at]
        labeled = code == m.label[0:1, at]
        y = jnp.where(labeled, -x, x)
        e = jnp.exp(-jnp.abs(y))
        more = 1.0 + e
        q = jnp.where(y >= 0, 1.0, e) / more
        softplus = jnp.maximum(y, 0.0) + jnp.log(more)
        slope = q * q * (2.0 * (1.0 - q) * softplus + q)
        return slope * (jnp.where(labeled, -0.25, jnp.where(code > 0.5, 0.75, 0.0)) * scale)

    def of_boxes(x, t, at):
        rows = slice(t * PX, (t + 1) * PX)
        g = jnp.clip((x - m.target[rows, at]) / huber_beta, -1.0, 1.0)
        return jnp.where(m.code[rows, at] > 1.5, g, 0.0) * scale

    def run(gradient):
        blocks = [(t, slice(n, n + 256)) for n in range(lanes.start, lanes.stop, 256) for t in range(2)]
        logits = [conv(m.act3, blocks[0][0], m.wh, blocks[0][1])]
        for i, (t, at) in enumerate(blocks):
            if i + 1 < len(blocks):
                logits.append(conv(m.act3, blocks[i + 1][0], m.wh, blocks[i + 1][1]))
            g = gradient(logits[i] + m.bias[4:5, at], t, at).astype(BF16)
            m.grad_bias[4:5, at] += jnp.sum(g.astype(F32), axis=0, keepdims=True)
            m.gl[t, TILE : TILE + PX, at] = g

    pl.when(m.role == 0)(lambda: run(of_class))
    if lanes.start < MAIN:
        pl.when(m.role == 1)(lambda: run(of_boxes))


def head_kernel_gradient(m, lanes, r):
    for s in range(3):
        at = (3 * r + s) * CH
        m.gh[at : at + CH, lanes] = dot(m.last_t[s], shifted_rows(m.gl, 2 - r, lanes)).astype(BF16)


def head_input_gradient(m, lanes):
    for t in range(2):
        columns = []
        for s in range(3):
            acc = None
            for r in range(3):
                at = (3 * r + s) * CH
                g = m.gl[t, TILE * (2 - r) : TILE * (2 - r) + PX, lanes]
                part = dot_nt(g, m.wh[at : at + CH, lanes])
                acc = part if acc is None else acc + part
            columns.append(acc)
        layer_upstream(m, LAYERS - 1, t, moved_left(columns[0]) + columns[1] + moved_right(columns[2]))


def input_gradient(m, l, t):
    acc = None
    for r in range(3):
        for s in range(3):
            at = (3 * r + s) * CH
            g = m.g3[l, t, TILE * (2 - r) : TILE * (2 - r) + PX, s * CH : (s + 1) * CH]
            part = dot_nt(g, m.w[l, at : at + CH, :])
            acc = part if acc is None else acc + part
    return acc


def layer_upstream(m, l, t, da):
    g = (da * m.slope[l, t * PX : (t + 1) * PX, :]).astype(BF16).astype(F32)
    m.grad_bias[l : l + 1, 0:CH] += jnp.sum(g, axis=0, keepdims=True)
    put_shifted(m.g3.at[l], t, g, -1, CH)


def layer_kernel_gradient(m, l, r):
    part = dot(m.act_t[l], shifted_rows(m.g3.at[l], 2 - r))
    for s in range(3):
        at = (3 * r + s) * CH
        m.g[l, at : at + CH, :] = part[:, s * CH : (s + 1) * CH].astype(BF16)


class Traffic:
    def __init__(self, send_sem, recv_sem):
        self.send_sem, self.recv_sem = send_sem, recv_sem
        self.names, self.used, self.sent = {}, 0, []

    def copy(self, name, src, dst, peer, span=1, offset=0):
        if name not in self.names:
            self.names[name] = self.used
            self.used += span
        i = self.names[name] + offset
        return pltpu.make_async_remote_copy(
            src, dst, self.send_sem.at[i], self.recv_sem.at[i], device_id=peer, device_id_type=MESH
        )

    def send(self, name, src, dst, peer, when=None, **at):
        copy = self.copy(name, src, dst, peer, **at)
        if when is None:
            copy.start()
        else:
            pl.when(when)(copy.start)
        self.sent.append((when, copy))

    def arrived(self, name, dst, peer, when=None, **at):
        copy = self.copy(name, dst, dst, peer, **at)
        if when is None:
            copy.wait_recv()
        else:
            pl.when(when)(copy.wait_recv)

    def finish(self):
        for when, copy in self.sent:
            if when is None:
                copy.wait_send()
            else:
                pl.when(when)(copy.wait_send)


SEMAPHORES = 224
WAYS = {
    "T0": "A", "T1": "B", "T3": "A", "T2": "B", "M0": "B", "M1": "A", "M3": "B", "M2": "A", "U0": "A", "U1": "B", "U3": "A", "U2": "B",
}
SCHEDULE = (
    "zT", "aM0", "aT0", "aU0", "aT1", "bT0", "f", "aT3", "bT1", "bM0", "zU", "aT2", "zM", "bU0", "e", "aU1", "aU3",
    "bT3", "bT2", "bU3", "aM1", "bU1", "aU2", "aM2", "cU0", "cT0", "y", "cT3", "cM0", "cT1", "cU3", "aM3", "cU1",
    "cT2", "bM1", "bU2", "F0", "bM2", "cU2", "bM3", "F1", "F2", "cM1", "dU3", "cM3", "cM2", "F3", "HM", "dU2",
    "dU0", "dU1", "WM0", "WM1", "HU", "X", "kM1", "kM0", "WU0", "w3", "x3", "kU0", "WU1", "k3", "w2", "kU1", "WU2",
    "x2", "k2", "kU2", "w1", "x1", "p3", "kU3", "Bk", "p2", "k1", "w0", "WM2", "Bp", "q2", "k0", "x0", "p1", "rU0",
    "q3", "kM3", "kM2", "Bq", "rU1", "rU2", "rU3", "q1", "pU0", "p0", "pM2", "pM0", "pM3", "s2", "q0", "pU3", "Bs",
    "pU1", "s3", "qU0", "pU2", "s1", "pM1", "D", "qM3", "qM0", "qM2", "s0", "qM1", "E", "qU3", "qU1", "qU2", "sM",
    "t", "sU",
)


def head_kernel(
    features, tower_class, tower_boxes, head_class, head_boxes, bias_class, bias_boxes, head_class_bias, head_boxes_bias,
    state, labels, targets_in, valid, label, spread_any, targets_any, mask_lab_any, mask_tgt_any,
    out_features, out_towers, out_heads, out_bias,
    spread, targets, mask_lab, mask_tgt, bias, fetch_sem,
    own, own_h, own_v, w, wh, hp, hv, g, gh, rc, rch, sm, su, sv, r1a, r1b, r1m, r1u, r1v, r2, r2m, r2u, r2v,
    quarter, sum_m, sum_u, sum_v, rz, rzm, rzu, rzv, done, layer_in,
    act3, g3, gl, act_t, last_t, slope, spare, code, target, da,
    x, lab, lab_in, count_mine, count_sum, count_in, grad_bias, bias_in, bias_z, dx, dx_in, tile_out, features_in,
    send_sem, recv_sem,
):
    s, dp = lax.axis_index("section"), lax.axis_index("dp")
    my_y, my_x, my_z, my_c = s // 2, s % 2, dp // 2, dp % 2
    sx, sy, sg = 2 * my_y + (1 - my_x), 2 * (1 - my_y) + my_x, 2 * (1 - my_y) + (1 - my_x)
    to_x, to_y, to_g, to_c = (sx, dp), (sy, dp), (sg, dp), (s, 2 * my_z + 1 - my_c)
    plane = lambda k: (my_z + k) % PLANES
    to_z = lambda k: (s, 2 * plane(k) + my_c)
    to_pair = (s, 2 * (my_z + 1 - 2 * (my_z % 2)) + my_c)
    role = my_z % 2
    on_class, on_boxes = role == 0, role == 1
    net = Traffic(send_sem, recv_sem)
    m = SimpleNamespace(
        w=w, wh=wh, g=g, gh=gh, act3=act3, g3=g3, gl=gl, act_t=act_t, last_t=last_t, slope=slope, code=code,
        target=target, lab=lab, lab_in=lab_in, count_sum=count_sum, count_in=count_in, grad_bias=grad_bias,
        bias=bias, spread=spread, targets=targets, mask_lab=mask_lab, mask_tgt=mask_tgt, label=label, role=role,
    )

    def shard(z, c):
        return pl.ds(pl.multiple_of(ROWS * (2 * z + c), 16), ROWS)

    barrier = pltpu.get_barrier_semaphore()
    peers = (to_x, to_y, to_g, to_c, to_z(1), to_z(2), to_z(3))
    for peer in peers:
        pl.semaphore_signal(barrier, inc=1, device_id=peer, device_id_type=MESH)

    constants_in = [
        pltpu.make_async_copy(src, dst, fetch_sem.at[i])
        for i, (src, dst) in enumerate(
            ((mask_lab_any, mask_lab), (spread_any.at[role], spread), (mask_tgt_any, mask_tgt), (targets_any, targets))
        )
    ]
    for copy in constants_in:
        copy.start()

    own[0] = tower_class[0].astype(BF16)
    own[1] = tower_boxes[0].astype(BF16)
    own_h[0:ROWS, :] = head_class[0:LANES, :].T.astype(BF16)
    rest, narrow = head_class.shape[0] - LANES, head_boxes.shape[0]
    spare[...] = jnp.zeros((ROWS, 2 * LANES), F32)
    spare[:, 0:rest] = head_class[LANES : LANES + rest, :].T
    spare[:, LANES : LANES + narrow] = head_boxes[...].T
    own_h[ROWS:PACK, :] = (spare[0:HALF, 0:LANES] + pltpu.roll(spare[HALF:ROWS, 0:LANES], TAIL, 1)).astype(BF16)
    own_v[...] = folded(spare[:, LANES : 2 * LANES]).astype(BF16)

    row = lax.broadcasted_iota(jnp.int32, (TILE, TILE * A), 0)
    found = jnp.zeros((TILE, TILE * A), F32)
    for t in range(SECTIONS):
        found += jnp.where(jnp.logical_and(state[t] == 1, row < valid[t]), 1.0, 0.0)
    count_mine[...] = jnp.full((8, LANES), jnp.sum(found), F32)
    inside = row < valid[s]
    kind = state[s]
    lab[...] = jnp.zeros_like(lab)
    lab[:, 0 : TILE * A] = jnp.where(
        inside,
        jnp.where(kind == 1, labels[s].astype(F32) + 2.0, jnp.where(kind == 2, 0.0, 1.0)),
        0.0,
    )
    lab[:, LAB : LAB + targets_in.shape[2]] = targets_in[s]

    pl.semaphore_wait(barrier, len(peers))

    def kinds(kind_name):
        return ("M", "V") if kind_name == "M" else (kind_name,)

    def due(kind_name):
        return dict(T=None, M=on_class, U=on_boxes, V=on_boxes)[kind_name]

    def head_lanes(sec):
        return pl.ds(pl.multiple_of(LANES * sec, LANES), LANES)

    def place(kind_name, sec, z):
        if kind_name == "T":
            return w.at[sec, shard(z, my_c), :]
        if kind_name == "M":
            return wh.at[shard(z, my_c), head_lanes(sec)]
        if kind_name == "V":
            return hv.at[sec, z]
        return hp.at[sec, z]

    def own_shard(kind_name, which):
        if kind_name == "T":
            return own.at[which]
        if kind_name == "V":
            return own_v
        return own_h.at[pl.ds(0, ROWS) if kind_name == "M" else pl.ds(ROWS, HALF), :]

    def planes_send(kind_name):
        for k in (1, 3, 2):
            other = plane(k) % 2
            for kind in kinds(kind_name):
                when = dict(T=None, M=other == 0, U=other == 1, V=other == 1)[kind]
                net.send(("z", kind, k), own_shard(kind, other), place(kind, s, my_z), to_z(k), when)

    in_plane = (("x", to_x, sx), ("y", to_y, sy), ("g", to_g, sg))

    def rows_of(sec):
        return pl.ds(pl.multiple_of(64 * sec, 64), 64)

    def features_send():
        for name, peer, sec in in_plane:
            net.send(("f", name), features.at[sec], x.at[0, rows_of(s), :], peer)
        net.send("count c", count_mine, count_in.at[0], to_c)
        net.send("lab", lab, lab_in, to_pair)

    def piece(kind_name, sec, j):
        return place(kind_name, sec, (my_z + PLANES - j) % PLANES)

    def ways(kind_name, j):
        if WAYS[kind_name.replace("V", "M") + str(j)] == "A":
            return (to_x, sx), (to_y, sy)
        return (to_y, sy), (to_x, sx)

    def gather_mine(kind_name, j):
        for kind in kinds(kind_name):
            mine = piece(kind, s, j)
            if j:
                net.arrived(("z", kind, j), mine, to_z(PLANES - j), due(kind))
            for (n, _), name in zip(ways(kind, j), ("g1", "g2")):
                net.send((name, kind, j), mine, mine, n, due(kind))
        if kind_name == "T":
            net.send(("swap", "T", j, 0), mine, mine, to_c)

    def gather_pass(kind_name, j):
        (n1, s1), (n2, s2) = ways(kind_name, j)
        for kind in kinds(kind_name):
            first = piece(kind, s1, j)
            net.arrived(("g1", kind, j), first, n1, due(kind))
            net.send(("g3", kind, j), first, first, n2, due(kind))
        if kind_name == "T":
            net.send(("swap", "T", j, 1), first, first, to_c)

    def gather_last(kind_name, j):
        (n1, s1), (n2, s2) = ways(kind_name, j)
        for i, (name, sec) in enumerate((("g2", s2), ("g3", sg))):
            for kind in kinds(kind_name):
                got = piece(kind, sec, j)
                net.arrived((name, kind, j), got, n2, due(kind))
            if kind_name == "T":
                net.send(("swap", "T", j, 2 + i), got, got, to_c)
        z = (my_z + PLANES - j) % PLANES
        at = pl.multiple_of(ROWS * (2 * z + my_c), 16)
        if kind_name == "M":

            @pl.when(on_boxes)
            def _():
                for sec in range(SECTIONS):
                    for i, part in enumerate(unfolded(hv[sec, z])):
                        rows = pl.ds(at + i * FOLD_ROWS, FOLD_ROWS)
                        wh[rows, sec * LANES : (sec + 1) * LANES] = part.astype(BF16)

            block = wh.at[pl.ds(at, ROWS), 0:MAIN]
            net.send(("swap", "M", j), block, block, to_c)
        if kind_name == "U":

            @pl.when(on_boxes)
            def _():
                for q in range(2):
                    lanes = slice((SECTIONS + q) * LANES, (SECTIONS + q + 1) * LANES)
                    top, bottom = swap_halves(hp[2 * q, z], hp[2 * q + 1, z])
                    wh[pl.ds(at, HALF), lanes] = top.astype(BF16)
                    wh[pl.ds(at + HALF, HALF), lanes] = bottom.astype(BF16)

            block = wh.at[pl.ds(at, ROWS), MAIN:HEAD]
            net.send(("up", j), block, block, to_pair, on_boxes)

    def relayed_plane(j):
        return (my_z + 1 + PLANES - j) % PLANES

    def gather_relayed(kind_name, j):
        block = wh.at[shard(relayed_plane(j), my_c), MAIN:HEAD]
        net.arrived(("up", j), block, to_pair, on_class)
        net.send(("swap", "U", j), block, block, to_c, on_class)

    def swapped(kind_name, j):
        z = (my_z + PLANES - j) % PLANES
        if kind_name == "M":
            net.arrived(("swap", "M", j), wh.at[shard(z, 1 - my_c), 0:MAIN], to_c)
            return
        if kind_name == "U":
            net.arrived(("swap", "U", j), wh.at[shard(relayed_plane(j), 1 - my_c), MAIN:HEAD], to_c, on_class)
            return
        (_, s1), (_, s2) = ways(kind_name, j)
        for i, sec in enumerate((s, s1, s2, sg)):
            net.arrived(("swap", "T", j, i), w.at[sec, shard(z, 1 - my_c), :], to_c)

    def features_tile():
        x[0, rows_of(s), :] = features[s]
        for name, peer, sec in in_plane:
            net.arrived(("f", name), x.at[0, rows_of(sec), :], peer)
        net.send("tile", x.at[0], x.at[1], to_pair)
        net.arrived("count c", count_in.at[0], to_c)
        count_sum[...] = count_mine[...] + count_in[0]
        for k in (1, 2, 3):
            net.send(("count", k), count_sum, count_in.at[k], to_z(k))

    def prepare():
        for ref in (act3, *(g3.at[l] for l in range(LAYERS)), gl):
            for t in range(2):
                ref[t, 0:TILE, :] = jnp.zeros((TILE, ref.shape[2]), BF16)
                ref[t, TILE + PX : 2 * TILE + PX, :] = jnp.zeros((TILE, ref.shape[2]), BF16)
        grad_bias[...] = jnp.zeros_like(grad_bias)
        for copy in constants_in:
            copy.wait()
        bias[0:LAYERS, 0:CH] = jnp.where(role == 0, bias_class[...], bias_boxes[...])
        bias[4:5, :] = jnp.where(role == 0, lay(head_class_bias[...]), lay(head_boxes_bias[...]))
        net.arrived("lab", lab_in, to_pair)
        prepare_loss(m)
        net.arrived("tile", x.at[1], to_pair)
        for t in range(2):
            v = x[t].astype(F32)
            put_shifted(act3, t, v, 1, CH)
            act_t[0, :, t * PX : (t + 1) * PX] = v.T.astype(BF16)

    def forward(l):
        if l == 0:
            for j in range(PLANES):
                swapped("T", j)
        forward_layer(m, l)

    def head(kind_name):
        if kind_name == "M":
            for k in (1, 2, 3):
                net.arrived(("count", k), count_in.at[k], to_z(PLANES - k))
        for j in range(PLANES):
            swapped(kind_name, j)
        head_gradients(m, head_part[kind_name])

    head_part = dict(M=slice(0, MAIN), U=slice(MAIN, HEAD))
    w[s, shard(my_z, my_c), :] = own[role]
    hp[s, my_z] = own_h[ROWS:PACK, :]
    hv[s, my_z] = own_v[...]

    @pl.when(on_class)
    def _():
        wh[shard(my_z, my_c), head_lanes(s)] = own_h[0:ROWS, :]


    def added(a, b):
        return a + b

    def half_rows(which):
        return pl.ds(pl.multiple_of(HALF * which, 16), HALF)

    def half_lanes(which):
        return pl.ds(pl.multiple_of(LANES * which, LANES), LANES)

    def core_send(l, zp):
        theirs = shard(zp, 1 - my_c)
        if l in head_part:
            when = on_class if l == "U" else None
            net.send(("rc", l, zp), gh.at[theirs, head_part[l]], rch.at[zp, :, head_part[l]], to_c, when)
        else:
            net.send(("rc", l, zp), g.at[l, theirs, :], rc.at[l, zp], to_c)

    first, second = pl.ds(0, 2), pl.ds(2, 2)

    def tower_cores(l):
        for zp in range(PLANES):
            net.arrived(("rc", l, zp), rc.at[l, zp], to_c)
            rc[l, zp] = added(rc[l, zp], g[l, shard(zp, my_c), :])
            if zp == 1:
                net.send(("r1a", l), rc.at[l, first, :, half_lanes(1 - my_x)], r1a.at[l], to_x)
        net.send(("r1b", l), rc.at[l, second, half_rows(1 - my_y), :], r1b.at[l], to_y)

    def tower_plane(l):
        net.arrived(("r1a", l), r1a.at[l], to_x)
        for zp in (0, 1):
            rc[l, zp, :, half_lanes(my_x)] = added(rc[l, zp, :, half_lanes(my_x)], r1a[l, zp])
        net.send(("r2a", l), rc.at[l, first, half_rows(1 - my_y), half_lanes(my_x)], r2.at[l, first], to_y)
        net.arrived(("r1b", l), r1b.at[l], to_y)
        for zp in (2, 3):
            rc[l, zp, half_rows(my_y), :] = added(rc[l, zp, half_rows(my_y), :], r1b[l, zp - 2])
        net.send(("r2b", l), rc.at[l, second, half_rows(my_y), half_lanes(1 - my_x)], r2.at[l, second], to_x)

    def to_planes(name, src, dst):
        for zp in range(PLANES):
            k = (zp + PLANES - my_z) % PLANES
            net.send(name, src.at[zp], dst.at[my_z], (s, 2 * zp + my_c), my_z != zp, span=PLANES, offset=k)

    def tower_planes(l):
        net.arrived(("r2a", l), r2.at[l, first], to_y)
        net.arrived(("r2b", l), r2.at[l, second], to_x)
        for zp in range(PLANES):
            quarter[l, zp] = added(rc[l, zp, half_rows(my_y), half_lanes(my_x)], r2[l, zp])
        to_planes(("rz", l), quarter.at[l], rz.at[l])

    def from_planes(name, mine, others):
        for k in (1, 2, 3):
            net.arrived(name, others.at[plane(PLANES - k)], to_z(PLANES - k), span=PLANES, offset=k)
        same = mine[my_z].astype(F32) + others[plane(2)].astype(F32)
        return same, others[plane(1)].astype(F32) + others[plane(3)].astype(F32)

    def tower_sum(l):
        same, other = from_planes(("rz", l), quarter.at[l], rz.at[l])
        done[l, role] = same.astype(BF16)
        done[l, 1 - role] = other.astype(BF16)
        to_l = (l, dp)
        net.send("layer", done.at[l], layer_in.at[s], to_l, s != l, span=SECTIONS, offset=s)

        @pl.when(s == l)
        def _():
            out_towers[role, half_rows(my_y), half_lanes(my_x)] = same
            out_towers[1 - role, half_rows(my_y), half_lanes(my_x)] = other

    def tower_store():
        for sec, peer in ((sx, to_x), (sy, to_y), (sg, to_g)):
            net.arrived("layer", layer_in.at[sec], peer, span=SECTIONS, offset=sec)
            for i in range(2):
                out_towers[i, half_rows(sec // 2), half_lanes(sec % 2)] = layer_in[sec, i].astype(F32)

    def head_refs(kind):
        return dict(
            M=(sm, r1m, r2m, sum_m, rzm), U=(su, r1u, r2u, sum_u, rzu), V=(sv, r1v, r2v, sum_v, rzv)
        )[kind]

    def both_cores(zp, rows, lanes):
        at = pl.multiple_of(ROWS * (2 * zp + my_c) + rows[0], 16)
        mine = gh[pl.ds(at, rows[1]), lanes]
        return rch[zp, rows[0] : rows[0] + rows[1], lanes].astype(F32) + mine.astype(F32)

    def head_cores(kind_name, zp):
        landed = rch.at[zp, :, head_part[kind_name]]
        if kind_name == "M":
            net.arrived(("rc", "M", zp), landed, to_c)

            def store(kind):
                for sec in range(SECTIONS):
                    v = both_cores(zp, (0, ROWS), slice(sec * LANES, (sec + 1) * LANES))
                    v = v if kind == "M" else folded(v)
                    head_refs(kind)[0][sec // 2, sec % 2, zp] = v.astype(BF16)

            for kind in kinds("M"):
                pl.when(due(kind))(functools.partial(store, kind))
            head_first_send("M", zp)
            return
        net.arrived(("rc", "U", zp), landed, to_c, on_class)

        @pl.when(on_class)
        def _():
            for q in range(2):
                lanes = slice((SECTIONS + q) * LANES, (SECTIONS + q + 1) * LANES)
                left, right = swap_halves(both_cores(zp, (0, HALF), lanes), both_cores(zp, (HALF, HALF), lanes))
                su[q, 0, zp] = left.astype(BF16)
                su[q, 1, zp] = right.astype(BF16)

        block = su.at[:, :, zp]
        net.send(("ru", zp), block, block, to_pair, on_class)

    def head_relayed(kind_name, zp):
        net.arrived(("ru", zp), su.at[:, :, zp], to_pair, on_boxes)
        head_first_send(kind_name, zp)

    def head_first_send(kind_name, zp):
        for kind in kinds(kind_name):
            into, landing = head_refs(kind)[:2]
            if zp % 2 == 0:
                net.send(("h1", kind, zp), into.at[:, 1 - my_x, zp], landing.at[zp], to_x, due(kind))
            else:
                net.send(("h1", kind, zp), into.at[1 - my_y, :, zp], landing.at[zp], to_y, due(kind))

    def head_plane(kind_name, zp):
        for kind in kinds(kind_name):
            into, landing, landing2 = head_refs(kind)[:3]
            net.arrived(("h1", kind, zp), landing.at[zp], to_x if zp % 2 == 0 else to_y, due(kind))

            @pl.when(due(kind))
            def _():
                for i in range(2):
                    at = (i, my_x, zp) if zp % 2 == 0 else (my_y, i, zp)
                    into[at] = added(into[at], landing[zp, i])

            if zp % 2 == 0:
                net.send(("h2", kind, zp), into.at[1 - my_y, my_x, zp], landing2.at[zp], to_y, due(kind))
            else:
                net.send(("h2", kind, zp), into.at[my_y, 1 - my_x, zp], landing2.at[zp], to_x, due(kind))

    def head_planes(kind_name, zp):
        k = (zp + PLANES - my_z) % PLANES
        for kind in kinds(kind_name):
            into, _, landing2, total, others = head_refs(kind)
            net.arrived(("h2", kind, zp), landing2.at[zp], to_y if zp % 2 == 0 else to_x, due(kind))

            @pl.when(due(kind))
            def _():
                total[zp] = added(into[my_y, my_x, zp], landing2[zp])

            away = jnp.logical_and(due(kind), my_z != zp)
            to_zp = (s, 2 * zp + my_c)
            net.send(("hz", kind), total.at[zp], others.at[my_z], to_zp, away, span=PLANES, offset=k)

    def head_store(kind_name):
        for kind in kinds(kind_name):
            total, others = head_refs(kind)[3:]
            here = due(kind)
            for k in (1, 2, 3):
                when = here if k == 2 else jnp.logical_not(here)
                source = others.at[plane(PLANES - k)]
                net.arrived(("hz", kind), source, to_z(PLANES - k), when, span=PLANES, offset=k)

            def store(v):
                if kind == "M":
                    out_heads[0, 0:ROWS] = v
                elif kind == "U":
                    out_heads[0, ROWS:PACK] = v
                else:
                    for i, part in enumerate(unfolded(v)):
                        out_heads[1, i * FOLD_ROWS : (i + 1) * FOLD_ROWS] = part

            @pl.when(here)
            def _():
                store(total[my_z].astype(F32) + others[plane(2)].astype(F32))

            @pl.when(jnp.logical_not(here))
            def _():
                store(others[plane(1)].astype(F32) + others[plane(3)].astype(F32))

        if kind_name == "U":
            out_heads[1, ROWS:PACK] = jnp.zeros((HALF, LANES), F32)

    def bias_cores():
        net.arrived("bias c", bias_in.at[0], to_c)
        bias_z[0] = grad_bias[...] + bias_in[0]
        net.send("bias x", bias_z.at[0], bias_in.at[1], to_x)

    def bias_plane():
        net.arrived("bias x", bias_in.at[1], to_x)
        bias_z[1] = bias_z[0] + bias_in[1]
        net.send("bias y", bias_z.at[1], bias_in.at[2], to_y)

    def bias_planes():
        net.arrived("bias y", bias_in.at[2], to_y)
        bias_z[2] = bias_z[1] + bias_in[2]
        for k in (1, 2, 3):
            net.send(("bias z", k), bias_z.at[2], bias_in.at[2 + k], to_z(k))

    def bias_store():
        for k in (1, 2, 3):
            net.arrived(("bias z", k), bias_in.at[2 + k], to_z(PLANES - k))
        out_bias[role] = bias_z[2] + bias_in[4]
        out_bias[1 - role] = bias_in[3] + bias_in[5]

    def features_sum():
        net.arrived("dx", dx_in, to_pair)
        tile_out[...] = (da[...] + dx_in[...].astype(F32)).astype(BF16)
        for name, peer, sec in in_plane:
            net.send(("b", name), tile_out.at[rows_of(sec), :], features_in.at[s], peer)

    def features_store():
        for name, peer, sec in in_plane:
            net.arrived(("b", name), features_in.at[sec], peer)
            out_features[sec] = features_in[sec]
        out_features[s] = tile_out[rows_of(s), :]

    def head_gradient(kind_name, r):
        if kind_name == "M":
            head_kernel_gradient(m, head_part["M"], r)
        else:
            pl.when(on_class)(lambda: head_kernel_gradient(m, head_part["U"], r))
        for zp in ((0,), (1,), (2, 3))[r]:
            core_send(kind_name, zp)

    def head_input():
        pl.when(on_class)(lambda: head_input_gradient(m, slice(0, HEAD)))
        pl.when(on_boxes)(lambda: head_input_gradient(m, slice(0, MAIN)))

    def layer_gradient(l):
        for r in range(3):
            layer_kernel_gradient(m, l, r)
        for zp in range(PLANES):
            core_send(l, zp)

    def layer_input(l):
        for t in range(2):
            v = input_gradient(m, l, t)
            if l:
                layer_upstream(m, l - 1, t, v)
            elif t == 0:
                da[...] = v
            else:
                dx[...] = v.astype(BF16)
        if l == 0:
            net.send("dx", dx, dx_in, to_pair)
        if l == 1:
            net.send("bias c", grad_bias, bias_in.at[0], to_c)

    def either(of_head, of_tower):
        return lambda *which: of_head(*which) if which[0] in head_part else of_tower(*which)

    steps = dict(
        d=gather_relayed, r=head_relayed, z=planes_send, f=features_send, e=features_tile, y=prepare, a=gather_mine, b=gather_pass, c=gather_last,
        F=forward, H=head, W=head_gradient, X=head_input, w=layer_gradient, x=layer_input,
        k=either(head_cores, tower_cores), p=either(head_plane, tower_plane), q=either(head_planes, tower_planes),
        s=either(head_store, tower_sum), t=tower_store, D=features_sum, E=features_store,
        B=lambda which: dict(k=bias_cores, p=bias_plane, q=bias_planes, s=bias_store)[which](),
    )
    for step in SCHEDULE:
        steps[step[0]](*(int(v) if v.isdigit() else v for v in step[1:]))
    net.finish()


def lay(vector):
    width = vector.shape[0]
    per = width // SECTIONS
    row = jnp.concatenate([vector.reshape(1, width), jnp.zeros((1, HEAD - width), F32)], axis=1)
    row = jnp.broadcast_to(row, (8, HEAD))
    lane = lax.broadcasted_iota(jnp.int32, (8, LANES), 1)
    main, tails = [], []
    for s in range(SECTIONS):
        turned = pltpu.roll(row, (HEAD - s * per) % HEAD, 1)
        main.append(jnp.where(lane < per, turned[:, 0:LANES], 0.0))
        tails.append(jnp.where(lane < per - LANES, turned[:, LANES : 2 * LANES], 0.0))
    folded = [tails[2 * q] + pltpu.roll(tails[2 * q + 1], TAIL, 1) for q in range(2)]
    return jnp.concatenate(main + folded, axis=1)[0:1, :]


def unlay(row, width):
    per = width // SECTIONS
    row = jnp.broadcast_to(row, (8, HEAD))
    lane = lax.broadcasted_iota(jnp.int32, (8, LANES), 1)
    total = jnp.zeros((8, HEAD), F32)
    for s in range(SECTIONS):
        tail = row[:, MAIN + (s // 2) * LANES : MAIN + (s // 2 + 1) * LANES]
        tail = pltpu.roll(tail, TAIL, 1) if s % 2 else tail
        parts = [jnp.where(lane < per, row[:, s * LANES : (s + 1) * LANES], 0.0), jnp.where(lane < per - LANES, tail, 0.0)]
        total += pltpu.roll(jnp.concatenate(parts + [jnp.zeros((8, HEAD - 2 * LANES), F32)], axis=1), s * per, 1)
    return total[0:1, 0:width].reshape(width)


def finish_kernel(
    features, towers, heads, sums,
    out_features, out_class, out_bias_class, out_boxes, out_bias_boxes, out_head_class, out_head_class_bias,
    out_head_boxes, out_head_boxes_bias,
):
    out_features[...] = features[...]
    for i, (tower, bias, head, head_bias) in enumerate(
        (
            (out_class, out_bias_class, out_head_class, out_head_class_bias),
            (out_boxes, out_bias_boxes, out_head_boxes, out_head_boxes_bias),
        )
    ):
        tower[0] = towers[i]
        bias[...] = sums[i, 0:LAYERS, 0:CH]
        width = head.shape[0]
        main, rest = min(width, LANES), max(0, width - LANES)
        head[0:main, :] = heads[i, 0:ROWS, :].T[0:main, :]
        if rest:
            low = heads[i, ROWS:PACK, :]
            both = jnp.concatenate([low, pltpu.roll(low, TAIL, 1)], axis=0)
            head[LANES:width, :] = both.T[0:rest, :]
        head_bias[...] = unlay(sums[i, LAYERS : LAYERS + 1, :], head_bias.shape[0])


def fast(features, tower_class, bias_class, tower_boxes, bias_boxes, head_class, head_class_bias, head_boxes,
         head_boxes_bias, anchor_state, class_labels, box_targets, valid_rows):
    class_width, boxes_width = head_class_bias.shape[0], head_boxes_bias.shape[0]
    spread, targets, mask_lab, mask_tgt, label = constants(class_width, boxes_width)
    tiles = features.shape[0]
    vmem = pl.BlockSpec(memory_space=pltpu.VMEM)
    smem = pl.BlockSpec(memory_space=pltpu.SMEM)
    v = lambda shape, dtype: pltpu.VMEM(shape, dtype)
    out = lambda shape, dtype: jax.ShapeDtypeStruct(shape, dtype)
    anywhere = pl.BlockSpec(memory_space=pl.ANY)
    raw = pl.pallas_call(
        head_kernel,
        out_shape=(
            out((tiles, 64, CH), BF16),
            out((2, ROWS, CH), F32),
            out((2, PACK, LANES), F32),
            out((2, 8, HEAD), F32),
        ),
        in_specs=[vmem] * 12 + [smem, vmem] + [anywhere] * 4,
        out_specs=(vmem,) * 4,
        scratch_shapes=[
            v(spread.shape[1:], BF16),
            v(targets.shape, BF16),
            v(mask_lab.shape, BF16),
            v(mask_tgt.shape, BF16),
            v((8, HEAD), F32),
            pltpu.SemaphoreType.DMA((4,)),
            v((2, ROWS, CH), BF16),
            v((PACK, LANES), BF16),
            v((FOLD_ROWS, LANES), BF16),
            v((LAYERS, DEEP, CH), BF16),
            v((DEEP, HEAD), BF16),
            v((SECTIONS, PLANES, HALF, LANES), BF16),
            v((SECTIONS, PLANES, FOLD_ROWS, LANES), BF16),
            v((LAYERS, DEEP, CH), BF16),
            v((DEEP, HEAD), BF16),
            v((LAYERS, PLANES, ROWS, CH), BF16),
            v((PLANES, ROWS, HEAD), BF16),
            v((2, 2, PLANES, ROWS, LANES), BF16),
            v((2, 2, PLANES, HALF, LANES), BF16),
            v((2, 2, PLANES, FOLD_ROWS, LANES), BF16),
            v((LAYERS, 2, ROWS, LANES), BF16),
            v((LAYERS, 2, HALF, CH), BF16),
            v((PLANES, 2, ROWS, LANES), BF16),
            v((PLANES, 2, HALF, LANES), BF16),
            v((PLANES, 2, FOLD_ROWS, LANES), BF16),
            v((LAYERS, PLANES, HALF, LANES), BF16),
            v((PLANES, ROWS, LANES), BF16),
            v((PLANES, HALF, LANES), BF16),
            v((PLANES, FOLD_ROWS, LANES), BF16),
            v((LAYERS, PLANES, HALF, LANES), BF16),
            v((PLANES, ROWS, LANES), BF16),
            v((PLANES, HALF, LANES), BF16),
            v((PLANES, FOLD_ROWS, LANES), BF16),
            v((LAYERS, PLANES, HALF, LANES), BF16),
            v((PLANES, ROWS, LANES), BF16),
            v((PLANES, HALF, LANES), BF16),
            v((PLANES, FOLD_ROWS, LANES), BF16),
            v((LAYERS, 2, HALF, LANES), BF16),
            v((SECTIONS, 2, HALF, LANES), BF16),
            v((2, PX + 2 * TILE, 3 * CH), BF16),
            v((LAYERS, 2, PX + 2 * TILE, 3 * CH), BF16),
            v((2, PX + 2 * TILE, HEAD), BF16),
            v((LAYERS, CH, 2 * PX), BF16),
            v((3, CH, 2 * PX), BF16),
            v((LAYERS, 2 * PX, CH), F32),
            v((ROWS, 2 * LANES), F32),
            v((2 * PX, HEAD), F32),
            v((2 * PX, MAIN), F32),
            v((PX, CH), F32),
            v((2, PX, CH), BF16),
            v((TILE, LAB + TGT), F32),
            v((TILE, LAB + TGT), F32),
            v((8, LANES), F32),
            v((8, LANES), F32),
            v((4, 8, LANES), F32),
            v((8, HEAD), F32),
            v((6, 8, HEAD), F32),
            v((3, 8, HEAD), F32),
            v((PX, CH), BF16),
            v((PX, CH), BF16),
            v((PX, CH), BF16),
            v((SECTIONS, 64, CH), BF16),
            pltpu.SemaphoreType.DMA((SEMAPHORES,)),
            pltpu.SemaphoreType.DMA((SEMAPHORES,)),
        ],
        compiler_params=pltpu.CompilerParams(
            collective_id=0, has_side_effects=True, vmem_limit_bytes=62 * 2**20
        ),
    )(
        features.reshape(tiles, 64, CH), tower_class, tower_boxes, head_class.T, head_boxes.T, bias_class, bias_boxes,
        head_class_bias, head_boxes_bias, anchor_state, class_labels, box_targets, valid_rows, label,
        spread, targets, mask_lab, mask_tgt,
    )
    results = pl.pallas_call(
        finish_kernel,
        out_shape=(
            out((tiles, 64, CH), BF16),
            out(tower_class.shape, F32),
            out(bias_class.shape, F32),
            out(tower_boxes.shape, F32),
            out(bias_boxes.shape, F32),
            out(head_class.shape[::-1], F32),
            out(head_class_bias.shape, F32),
            out(head_boxes.shape[::-1], F32),
            out(head_boxes_bias.shape, F32),
        ),
        in_specs=[vmem] * 4,
        out_specs=(vmem,) * 9,
    )(*raw)
    of_features, of_class, of_bias_class, of_boxes, of_bias_boxes, of_head_class, *rest = results
    of_head_class_bias, of_head_boxes, of_head_boxes_bias = rest
    return (
        of_features.reshape(features.shape), of_class, of_bias_class, of_boxes, of_bias_boxes,
        of_head_class.T, of_head_class_bias, of_head_boxes.T, of_head_boxes_bias,
    )


def shifted(block, axis, distance):
    devices = range(lax.axis_size(axis))
    route = [(i - distance, i) for i in devices if i - distance in devices]
    return lax.ppermute(block, axis, route)


def anchor_masks(anchor_state, valid_rows):
    tile_count = anchor_state.shape[0]
    anchor_kind = anchor_state.reshape(tile_count, TILE, TILE, A)
    row_index = lax.broadcasted_iota(jnp.int32, (tile_count, TILE, 1, 1), 1)
    inside = row_index < valid_rows.reshape(tile_count, 1, 1, 1)
    positive = jnp.logical_and(anchor_kind == 1, inside).astype(jnp.float32)
    counted = jnp.logical_and(anchor_kind != 2, inside).astype(jnp.float32)
    return (positive, counted)


def head_loss(logits, box_values, positive, counted, class_labels, box_targets, normalizer):
    tile_count = logits.shape[0]
    scores = logits.reshape(tile_count, TILE, TILE, A, K)
    labels = class_labels.reshape(tile_count, TILE, TILE, A, 1)
    classes = lax.broadcasted_iota(jnp.int32, (1, 1, 1, 1, K), 4)
    target = (labels == classes).astype(jnp.float32) * positive[..., None]
    chance = jax.nn.sigmoid(scores)
    entropy = jax.nn.softplus(scores) - target * scores
    agreement = chance * target + (1.0 - chance) * (1.0 - target)
    balance = 0.25 * target + 0.75 * (1.0 - target)
    focal_terms = balance * (1.0 - agreement) ** 2 * entropy
    focal_sum = jnp.sum(focal_terms * counted[..., None])
    offsets = box_values.reshape(tile_count, TILE, TILE, A, 4) - box_targets.reshape(
        tile_count, TILE, TILE, A, 4
    )
    spread = jnp.abs(offsets)
    huber_terms = jnp.where(
        spread < huber_beta, 0.5 * offsets * offsets / huber_beta, spread - 0.5 * huber_beta
    )
    box_sum = jnp.sum(huber_terms * positive[..., None])
    return (focal_sum + box_sum) / normalizer


def unfold(values):
    tile_count, tile_side, channels = (values.shape[0], values.shape[1], values.shape[3])
    padded = jnp.pad(values, ((0, 0), (1, 1), (1, 1), (0, 0)))
    pieces = [
        padded[:, row_shift : row_shift + tile_side, col_shift : col_shift + tile_side, :]
        for row_shift in range(3)
        for col_shift in range(3)
    ]
    return jnp.concatenate(pieces, axis=-1).reshape(
        tile_count * tile_side * tile_side, 9 * channels
    )


def fold_back(columns, tile_count, tile_side, channels):
    shaped = columns.reshape(tile_count, tile_side, tile_side, 9 * channels)
    padded = jnp.zeros((tile_count, tile_side + 2, tile_side + 2, channels), jnp.float32)
    for tap_index in range(9):
        row_shift = tap_index // 3
        col_shift = tap_index % 3
        padded = padded.at[
            :, row_shift : row_shift + tile_side, col_shift : col_shift + tile_side, :
        ].add(shaped[..., tap_index * channels : (tap_index + 1) * channels])
    return padded[:, 1 : tile_side + 1, 1 : tile_side + 1, :]


def weight_grad(columns, upstream):
    return jnp.einsum("pk,pc->kc", columns, upstream, preferred_element_type=jnp.float32)


def input_cols(upstream, weight):
    return jnp.einsum("pc,kc->pk", upstream, weight, preferred_element_type=jnp.float32)


def pick(buffer, slot_index):
    return lax.dynamic_index_in_dim(buffer, slot_index, 0, keepdims=False)


def store(buffer, update, slot_index, active):
    return lax.dynamic_update_index_in_dim(
        buffer, jnp.where(active, update, pick(buffer, slot_index)), slot_index, 0
    )


def per_device(
    features,
    tower_class,
    bias_class,
    tower_boxes,
    bias_boxes,
    head_class,
    head_class_bias,
    head_boxes,
    head_boxes_bias,
    anchor_state,
    class_labels,
    box_targets,
    valid_rows,
):
    section_count = lax.axis_size("section")
    section_index = lax.axis_index("section")
    final_section = section_count - 1
    is_first = section_index == 0
    is_final = section_index == final_section
    tile_dev = features.shape[0]
    per_micro = tile_dev // MICRO
    whole = lax.all_gather(features, "section", axis=1, tiled=True)
    tile_side = whole.shape[1]
    channels = whole.shape[3]
    pixels = per_micro * tile_side * tile_side
    act_shape = (per_micro, tile_side, tile_side, channels)
    positive, counted = anchor_masks(anchor_state, valid_rows)
    found = lax.psum(jnp.sum(positive), "dp")
    normalizer = jnp.maximum(found, 1.0)
    gathered = (
        lax.all_gather(tower_class.astype(jnp.bfloat16), "dp", axis=1, tiled=True),
        lax.all_gather(tower_boxes.astype(jnp.bfloat16), "dp", axis=1, tiled=True),
        lax.all_gather(head_class.astype(jnp.bfloat16), "dp", axis=0, tiled=True),
        lax.all_gather(head_boxes.astype(jnp.bfloat16), "dp", axis=0, tiled=True),
    )
    weight_class = gathered[0][0]
    weight_boxes = gathered[1][0]
    head_weight_class, head_weight_boxes = (
        lax.all_gather(gathered[2], "section", axis=1, tiled=True),
        lax.all_gather(gathered[3], "section", axis=1, tiled=True),
    )
    layer_bias_class = lax.dynamic_index_in_dim(bias_class, section_index, 0, keepdims=False)
    layer_bias_boxes = lax.dynamic_index_in_dim(bias_boxes, section_index, 0, keepdims=False)
    class_width = head_weight_class.shape[1]
    boxes_width = head_weight_boxes.shape[1]
    patch_width = head_weight_class.shape[0]

    def head_pass(stored_class, stored_boxes, slot_index):
        cols_class = unfold(stored_class)
        cols_boxes = unfold(stored_boxes)
        logits = (
            jnp.dot(cols_class, head_weight_class, preferred_element_type=jnp.float32)
            + head_class_bias
        )
        box_values = (
            jnp.dot(cols_boxes, head_weight_boxes, preferred_element_type=jnp.float32)
            + head_boxes_bias
        )
        start = slot_index * per_micro
        pos_here = lax.dynamic_slice_in_dim(positive, start, per_micro, 0)
        counted_here = lax.dynamic_slice_in_dim(counted, start, per_micro, 0)
        labels_here = lax.dynamic_slice_in_dim(class_labels, start, per_micro, 0)
        targets_here = lax.dynamic_slice_in_dim(box_targets, start, per_micro, 0)

        def local_loss(logit_part, box_part):
            return head_loss(
                logit_part.reshape(per_micro, tile_side, tile_side, class_width),
                box_part.reshape(per_micro, tile_side, tile_side, boxes_width),
                pos_here,
                counted_here,
                labels_here,
                targets_here,
                normalizer,
            )

        total_loss, pullback = jax.vjp(local_loss, logits, box_values)
        grad_logits, grad_box = pullback(jnp.ones_like(total_loss))
        grad_logits = grad_logits.astype(jnp.bfloat16)
        grad_box = grad_box.astype(jnp.bfloat16)
        back_class = fold_back(
            input_cols(grad_logits, head_weight_class), per_micro, tile_side, channels
        )
        back_boxes = fold_back(
            input_cols(grad_box, head_weight_boxes), per_micro, tile_side, channels
        )
        return (
            weight_grad(cols_class, grad_logits),
            weight_grad(cols_boxes, grad_box),
            jnp.sum(grad_logits.astype(jnp.float32), 0),
            jnp.sum(grad_box.astype(jnp.float32), 0),
            back_class,
            back_boxes,
        )

    def head_spare(stored_class, stored_boxes, slot_index):
        return (
            jnp.zeros((patch_width, class_width), jnp.float32),
            jnp.zeros((patch_width, boxes_width), jnp.float32),
            jnp.zeros((class_width,), jnp.float32),
            jnp.zeros((boxes_width,), jnp.float32),
            jnp.zeros(act_shape, jnp.float32),
            jnp.zeros(act_shape, jnp.float32),
        )

    kept_class = jnp.zeros((MICRO,) + act_shape, jnp.bfloat16)
    kept_boxes = jnp.zeros((MICRO,) + act_shape, jnp.bfloat16)
    kept_pre_class = jnp.zeros((MICRO, pixels, channels), jnp.float32)
    kept_pre_boxes = jnp.zeros((MICRO, pixels, channels), jnp.float32)
    head_back_class = jnp.zeros((MICRO,) + act_shape, jnp.float32)
    head_back_boxes = jnp.zeros((MICRO,) + act_shape, jnp.float32)
    grad_head_class = jnp.zeros((patch_width, class_width), jnp.float32)
    grad_head_boxes = jnp.zeros((patch_width, boxes_width), jnp.float32)
    grad_hbias_class = jnp.zeros((class_width,), jnp.float32)
    grad_hbias_boxes = jnp.zeros((boxes_width,), jnp.float32)
    total_moments = MICRO + section_count - 1
    empty_act = jnp.zeros(act_shape, jnp.bfloat16)
    received = (empty_act, empty_act)
    for moment in range(total_moments):
        micro_index = moment - section_index
        active = jnp.logical_and(micro_index >= 0, micro_index < MICRO)
        slot_index = jnp.clip(micro_index, 0, MICRO - 1)
        if moment < MICRO:
            entering = whole[moment * per_micro : (moment + 1) * per_micro]
        else:
            entering = empty_act
        input_class = jnp.where(is_first, entering, received[0])
        input_boxes = jnp.where(is_first, entering, received[1])
        kept_class = store(kept_class, input_class, slot_index, active)
        kept_boxes = store(kept_boxes, input_boxes, slot_index, active)
        pre_class = (
            jnp.dot(unfold(input_class), weight_class, preferred_element_type=jnp.float32)
            + layer_bias_class
        )
        pre_boxes = (
            jnp.dot(unfold(input_boxes), weight_boxes, preferred_element_type=jnp.float32)
            + layer_bias_boxes
        )
        kept_pre_class = store(kept_pre_class, pre_class, slot_index, active)
        kept_pre_boxes = store(kept_pre_boxes, pre_boxes, slot_index, active)
        act_class = jax.nn.gelu(pre_class).astype(jnp.bfloat16).reshape(act_shape)
        act_boxes = jax.nn.gelu(pre_boxes).astype(jnp.bfloat16).reshape(act_shape)
        results = lax.cond(
            jnp.logical_and(is_final, active),
            head_pass,
            head_spare,
            act_class,
            act_boxes,
            slot_index,
        )
        grad_head_class = grad_head_class + results[0]
        grad_head_boxes = grad_head_boxes + results[1]
        grad_hbias_class = grad_hbias_class + results[2]
        grad_hbias_boxes = grad_hbias_boxes + results[3]
        head_back_class = store(head_back_class, results[4], slot_index, active)
        head_back_boxes = store(head_back_boxes, results[5], slot_index, active)
        if moment < total_moments - 1:
            received = shifted((act_class, act_boxes), "section", 1)
    grad_layer_class = jnp.zeros((patch_width, channels), jnp.float32)
    grad_layer_boxes = jnp.zeros((patch_width, channels), jnp.float32)
    grad_lbias_class = jnp.zeros((channels,), jnp.float32)
    grad_lbias_boxes = jnp.zeros((channels,), jnp.float32)
    input_back = jnp.zeros((MICRO,) + act_shape, jnp.float32)
    returned = (empty_act, empty_act)
    for moment in range(total_moments):
        micro_index = moment - (final_section - section_index)
        active = jnp.logical_and(micro_index >= 0, micro_index < MICRO)
        slot_index = jnp.clip(micro_index, 0, MICRO - 1)
        upstream_class = jnp.where(
            is_final, pick(head_back_class, slot_index), returned[0].astype(jnp.float32)
        ).reshape(pixels, channels)
        upstream_boxes = jnp.where(
            is_final, pick(head_back_boxes, slot_index), returned[1].astype(jnp.float32)
        ).reshape(pixels, channels)
        cols_class = unfold(pick(kept_class, slot_index))
        cols_boxes = unfold(pick(kept_boxes, slot_index))
        pre_class = pick(kept_pre_class, slot_index)
        pre_boxes = pick(kept_pre_boxes, slot_index)
        gelu_class = jax.vjp(jax.nn.gelu, pre_class)[1](upstream_class)[0]
        gelu_boxes = jax.vjp(jax.nn.gelu, pre_boxes)[1](upstream_boxes)[0]
        grad_pre_class = jnp.where(active, gelu_class, 0.0).astype(jnp.bfloat16)
        grad_pre_boxes = jnp.where(active, gelu_boxes, 0.0).astype(jnp.bfloat16)
        grad_layer_class = grad_layer_class + weight_grad(cols_class, grad_pre_class)
        grad_layer_boxes = grad_layer_boxes + weight_grad(cols_boxes, grad_pre_boxes)
        grad_lbias_class = grad_lbias_class + jnp.sum(grad_pre_class.astype(jnp.float32), 0)
        grad_lbias_boxes = grad_lbias_boxes + jnp.sum(grad_pre_boxes.astype(jnp.float32), 0)
        back_class = fold_back(
            input_cols(grad_pre_class, weight_class), per_micro, tile_side, channels
        )
        back_boxes = fold_back(
            input_cols(grad_pre_boxes, weight_boxes), per_micro, tile_side, channels
        )
        input_back = store(
            input_back, back_class + back_boxes, slot_index, jnp.logical_and(active, is_first)
        )
        if moment < total_moments - 1:
            returned = shifted(
                (back_class.astype(jnp.bfloat16), back_boxes.astype(jnp.bfloat16)), "section", -1
            )
    spread_back = jnp.where(
        is_first, input_back.reshape(tile_dev, tile_side, tile_side, channels), 0.0
    )
    grad_features = lax.psum_scatter(
        spread_back.astype(jnp.bfloat16), "section", scatter_dimension=1, tiled=True
    )
    summed = (
        lax.psum_scatter(grad_layer_class, "dp", scatter_dimension=0, tiled=True),
        lax.psum_scatter(grad_layer_boxes, "dp", scatter_dimension=0, tiled=True),
        lax.psum_scatter(grad_head_class, "dp", scatter_dimension=0, tiled=True),
        lax.psum_scatter(grad_head_boxes, "dp", scatter_dimension=0, tiled=True),
    )
    final_head_class, final_head_boxes = (
        lax.psum_scatter(
            summed[2].astype(jnp.bfloat16), "section", scatter_dimension=1, tiled=True
        ).astype(jnp.float32),
        lax.psum_scatter(
            summed[3].astype(jnp.bfloat16), "section", scatter_dimension=1, tiled=True
        ).astype(jnp.float32),
    )
    rows_class = lax.dynamic_update_index_in_dim(
        jnp.zeros((LAYERS, channels), jnp.float32), grad_lbias_class, section_index, 0
    )
    rows_boxes = lax.dynamic_update_index_in_dim(
        jnp.zeros((LAYERS, channels), jnp.float32), grad_lbias_boxes, section_index, 0
    )
    bias_sums = lax.psum(
        (rows_class, rows_boxes, grad_hbias_class, grad_hbias_boxes), ("section", "dp")
    )
    return (
        grad_features,
        summed[0][None],
        bias_sums[0],
        summed[1][None],
        bias_sums[1],
        final_head_class,
        bias_sums[2],
        final_head_boxes,
        bias_sums[3],
    )


def solution(mesh):
    fits = mesh.shape["section"] == SECTIONS == LAYERS and mesh.shape["dp"] == PLANES * CORES
    placed = (
        P("dp", "section", None, None),
        P("section", "dp", None),
        P(),
        P("section", "dp", None),
        P(),
        P("dp", "section"),
        P(),
        P("dp", "section"),
        P(),
        P("dp", None, None),
        P("dp", None, None),
        P("dp", None, None),
        P("dp"),
    )
    return jax.shard_map(
        fast if fits else per_device,
        mesh=mesh,
        in_specs=placed,
        out_specs=(
            P("dp", "section", None, None),
            P("section", "dp", None),
            P(),
            P("section", "dp", None),
            P(),
            P("dp", "section"),
            P(),
            P("dp", "section"),
            P(),
        ),
        check_vma=False,
    )
```

```python
import functools
import math
from types import SimpleNamespace

import jax
import jax.numpy as jnp
import numpy as np
from jax import lax
from jax.experimental import pallas as pl
from jax.experimental.pallas import tpu as pltpu
from jax.sharding import PartitionSpec as P

K = 80
A = 9
LAYERS = 4
TILE = 16
MICRO = 4


huber_beta = 1.0 / 9.0

F32 = jnp.float32
BF16 = jnp.bfloat16
MESH = pl.DeviceIdType.MESH
GELU_C = math.sqrt(2.0 / math.pi)

SECTIONS = 4
PLANES = 4
CORES = 2
CH = 256
PX = TILE * TILE
ROWS = 288
HALF = ROWS // 2
PACK = ROWS + HALF
LANES = 128
TAIL = 64
MAIN = SECTIONS * LANES
HEAD = MAIN + SECTIONS * TAIL
LAB = 256
TGT = 640
DEEP = 9 * CH
FOLD = 3
FOLD_ROWS = ROWS // FOLD
FOLD_LANES = 32


def head_layout(width):
    per = width // SECTIONS
    columns = np.full((HEAD,), -1)
    for s in range(SECTIONS):
        main = min(per, LANES)
        columns[s * LANES : s * LANES + main] = s * per + np.arange(main)
        rest = per - main
        at = SECTIONS * LANES + s * TAIL
        columns[at : at + rest] = s * per + main + np.arange(rest)
    return columns


def constants(class_width, boxes_width):
    classes, boxes = head_layout(class_width), head_layout(boxes_width)
    spread = np.zeros((2, LAB, HEAD), np.float32)
    targets = np.zeros((TGT, MAIN), np.float32)
    for j in range(TILE):
        for col in range(HEAD):
            if classes[col] >= 0:
                spread[0, j * A + classes[col] // K, col] = 1
            if boxes[col] >= 0:
                spread[1, j * A + boxes[col] // 4, col] = 1
                targets[j * boxes_width + boxes[col], col] = 1
    pixel = np.arange(PX)[:, None] % TILE
    mask_lab = (np.arange(LAB)[None, :] // A == pixel) & (np.arange(LAB)[None, :] < TILE * A)
    mask_tgt = (np.arange(TGT)[None, :] // boxes_width == pixel) & (np.arange(TGT)[None, :] < TILE * boxes_width)
    label = np.where(classes >= 0, classes % K, -9).astype(np.float32)[None, :] + 2.0
    bf = lambda v: jnp.asarray(v.astype(np.float32), BF16)
    return bf(spread), bf(targets), bf(mask_lab), bf(mask_tgt), jnp.asarray(np.repeat(label, 8, 0))


def dot(a, b):
    return jnp.dot(a, b, preferred_element_type=F32)


def dot_nt(a, b):
    return lax.dot_general(a, b, (((1,), (1,)), ((), ())), preferred_element_type=F32)


def moved_right(v):
    col = lax.broadcasted_iota(jnp.int32, v.shape, 0) % TILE
    return jnp.where(col == 0, 0.0, pltpu.roll(v, 1, 0))


def moved_left(v):
    col = lax.broadcasted_iota(jnp.int32, v.shape, 0) % TILE
    return jnp.where(col == TILE - 1, 0.0, pltpu.roll(v, PX - 1, 0))


def put_shifted(ref, t, v, order, width):
    blocks = (moved_right(v), v, moved_left(v))[::order]
    for s, block in enumerate(blocks):
        ref[t, TILE : TILE + PX, s * width : (s + 1) * width] = block.astype(BF16)


def shifted_rows(ref, r, lanes=slice(None)):
    return ref[:, TILE * r : TILE * r + PX, lanes].reshape(2 * PX, -1)


def swap_halves(p, q):
    p, q = p.astype(F32), q.astype(F32)
    low = lax.broadcasted_iota(jnp.int32, p.shape, 1) < TAIL
    p_turned, q_turned = pltpu.roll(p, TAIL, 1), pltpu.roll(q, TAIL, 1)
    return jnp.where(low, p, q_turned), jnp.where(low, p_turned, q)


def folded(v):
    parts = [v[i * FOLD_ROWS : (i + 1) * FOLD_ROWS] for i in range(FOLD)]
    return parts[0] + sum(pltpu.roll(part, i * FOLD_LANES, 1) for i, part in enumerate(parts) if i)


def unfolded(v):
    v = v.astype(F32)
    low = lax.broadcasted_iota(jnp.int32, v.shape, 1) < FOLD_LANES
    return [
        jnp.where(low, pltpu.roll(v, LANES - i * FOLD_LANES, 1) if i else v, 0.0) for i in range(FOLD)
    ]


def conv(act3, t, kernel, lanes=slice(None)):
    return sum(
        dot(act3[t, TILE * r : TILE * r + PX, :], kernel[3 * CH * r : 3 * CH * (r + 1), lanes]) for r in range(3)
    )


def forward_layer(m, l):
    for t in range(2):
        z = conv(m.act3, t, m.w.at[l]) + m.bias[l : l + 1, 0:CH]
        square = z * z
        th = jnp.tanh(GELU_C * (z + 0.044715 * z * square))
        half = 0.5 * (1.0 + th)
        a = z * half
        m.slope[l, t * PX : (t + 1) * PX, :] = half + (0.5 * GELU_C) * z * (1.0 - th * th) * (
            1.0 + (3 * 0.044715) * square
        )
        put_shifted(m.act3, t, a, 1, CH)
        if l + 1 < LAYERS:
            m.act_t[l + 1, :, t * PX : (t + 1) * PX] = a.T.astype(BF16)
        else:
            for i, moved in enumerate((moved_right(a), a, moved_left(a))):
                m.last_t[i, :, t * PX : (t + 1) * PX] = moved.T.astype(BF16)


def expand(row, mask):
    lanes = row.shape[-1]
    return jnp.broadcast_to(row[:, None, :], (TILE, TILE, lanes)).reshape(PX, lanes) * mask[...].astype(F32)


def prepare_loss(m):
    for t, lab in enumerate((m.lab, m.lab_in)):
        codes = expand(lab[:, 0:LAB], m.mask_lab).astype(BF16)
        m.code[t * PX : (t + 1) * PX, :] = dot(codes, m.spread[...])

    @pl.when(m.role == 1)
    def _():
        for t, lab in enumerate((m.lab, m.lab_in)):
            values = expand(lab[:, LAB : LAB + TGT], m.mask_tgt)
            m.target[t * PX : (t + 1) * PX, :] = jnp.dot(
                values, m.targets[...].astype(F32), precision=lax.Precision.HIGHEST, preferred_element_type=F32
            )


def head_gradients(m, lanes):
    total = m.count_sum[0:1, :] + m.count_in[1, 0:1, :] + m.count_in[2, 0:1, :] + m.count_in[3, 0:1, :]
    scale = jnp.concatenate([1.0 / jnp.maximum(total, 1.0)] * 2, axis=1)

    def of_class(x, t, at):
        code = m.code[t * PX : (t + 1) * PX, at]
        labeled = code == m.label[0:1, at]
        y = jnp.where(labeled, -x, x)
        e = jnp.exp(-jnp.abs(y))
        more = 1.0 + e
        q = jnp.where(y >= 0, 1.0, e) / more
        softplus = jnp.maximum(y, 0.0) + jnp.log(more)
        slope = q * q * (2.0 * (1.0 - q) * softplus + q)
        return slope * (jnp.where(labeled, -0.25, jnp.where(code > 0.5, 0.75, 0.0)) * scale)

    def of_boxes(x, t, at):
        rows = slice(t * PX, (t + 1) * PX)
        g = jnp.clip((x - m.target[rows, at]) / huber_beta, -1.0, 1.0)
        return jnp.where(m.code[rows, at] > 1.5, g, 0.0) * scale

    def run(gradient):
        blocks = [(t, slice(n, n + 256)) for n in range(lanes.start, lanes.stop, 256) for t in range(2)]
        logits = [conv(m.act3, blocks[0][0], m.wh, blocks[0][1])]
        for i, (t, at) in enumerate(blocks):
            if i + 1 < len(blocks):
                logits.append(conv(m.act3, blocks[i + 1][0], m.wh, blocks[i + 1][1]))
            g = gradient(logits[i] + m.bias[4:5, at], t, at).astype(BF16)
            m.grad_bias[4:5, at] += jnp.sum(g.astype(F32), axis=0, keepdims=True)
            m.gl[t, TILE : TILE + PX, at] = g

    pl.when(m.role == 0)(lambda: run(of_class))
    if lanes.start < MAIN:
        pl.when(m.role == 1)(lambda: run(of_boxes))


def head_kernel_gradient(m, lanes, r):
    for s in range(3):
        at = (3 * r + s) * CH
        m.gh[at : at + CH, lanes] = dot(m.last_t[s], shifted_rows(m.gl, 2 - r, lanes)).astype(BF16)


def head_input_gradient(m, lanes):
    for t in range(2):
        columns = []
        for s in range(3):
            acc = None
            for r in range(3):
                at = (3 * r + s) * CH
                g = m.gl[t, TILE * (2 - r) : TILE * (2 - r) + PX, lanes]
                part = dot_nt(g, m.wh[at : at + CH, lanes])
                acc = part if acc is None else acc + part
            columns.append(acc)
        layer_upstream(m, LAYERS - 1, t, moved_left(columns[0]) + columns[1] + moved_right(columns[2]))


def input_gradient(m, l, t):
    acc = None
    for r in range(3):
        for s in range(3):
            at = (3 * r + s) * CH
            g = m.g3[l, t, TILE * (2 - r) : TILE * (2 - r) + PX, s * CH : (s + 1) * CH]
            part = dot_nt(g, m.w[l, at : at + CH, :])
            acc = part if acc is None else acc + part
    return acc


def layer_upstream(m, l, t, da):
    g = (da * m.slope[l, t * PX : (t + 1) * PX, :]).astype(BF16).astype(F32)
    m.grad_bias[l : l + 1, 0:CH] += jnp.sum(g, axis=0, keepdims=True)
    put_shifted(m.g3.at[l], t, g, -1, CH)


def layer_kernel_gradient(m, l, r):
    part = dot(m.act_t[l], shifted_rows(m.g3.at[l], 2 - r))
    for s in range(3):
        at = (3 * r + s) * CH
        m.g[l, at : at + CH, :] = part[:, s * CH : (s + 1) * CH].astype(BF16)


class Traffic:
    def __init__(self, send_sem, recv_sem):
        self.send_sem, self.recv_sem = send_sem, recv_sem
        self.names, self.used, self.sent = {}, 0, []

    def copy(self, name, src, dst, peer, span=1, offset=0):
        if name not in self.names:
            self.names[name] = self.used
            self.used += span
        i = self.names[name] + offset
        return pltpu.make_async_remote_copy(
            src, dst, self.send_sem.at[i], self.recv_sem.at[i], device_id=peer, device_id_type=MESH
        )

    def send(self, name, src, dst, peer, when=None, **at):
        copy = self.copy(name, src, dst, peer, **at)
        if when is None:
            copy.start()
        else:
            pl.when(when)(copy.start)
        self.sent.append((when, copy))

    def arrived(self, name, dst, peer, when=None, **at):
        copy = self.copy(name, dst, dst, peer, **at)
        if when is None:
            copy.wait_recv()
        else:
            pl.when(when)(copy.wait_recv)

    def finish(self):
        for when, copy in self.sent:
            if when is None:
                copy.wait_send()
            else:
                pl.when(when)(copy.wait_send)


SEMAPHORES = 224
WAYS = {
    "T0": "A", "T1": "B", "T3": "A", "T2": "B", "M0": "B", "M1": "A", "M3": "B", "M2": "A", "U0": "A", "U1": "B", "U3": "A", "U2": "B",
}
SCHEDULE = (
    "zT", "aM0", "aT0", "aU0", "aT1", "bT0", "f", "aT3", "bT1", "bM0", "zU", "aT2", "zM", "bU0", "e", "aU1", "aU3",
    "bT3", "bT2", "bU3", "aM1", "bU1", "aU2", "aM2", "cU0", "cT0", "y", "cT3", "cM0", "cT1", "cU3", "aM3", "cU1",
    "cT2", "bM1", "bU2", "F0", "bM2", "cU2", "bM3", "F1", "F2", "cM1", "dU3", "cM3", "cM2", "F3", "HM", "dU2",
    "dU0", "dU1", "WM0", "WM1", "HU", "X", "kM1", "kM0", "WU0", "w3", "x3", "kU0", "WU1", "k3", "w2", "kU1", "WU2",
    "x2", "k2", "kU2", "w1", "kU3", "x1", "p3", "Bk", "p2", "k1", "w0", "WM2", "Bp", "q2", "k0", "x0", "p1", "rU0",
    "q3", "kM3", "kM2", "Bq", "rU1", "rU2", "rU3", "q1", "pU0", "p0", "pM2", "pM0", "pM3", "s2", "q0", "pU3", "Bs",
    "pU1", "s3", "qU0", "pU2", "s1", "pM1", "D", "qM3", "qM0", "qM2", "s0", "qM1", "E", "qU3", "qU1", "qU2", "sM",
    "t", "sU",
)


def head_kernel(
    features_any, tower_class_any, tower_boxes_any, head_class_any, head_boxes_any,
    bias_class_any, bias_boxes_any, head_class_bias_any, head_boxes_bias_any, state_any, labels_any, targets_in_any,
    valid_any, label_any, spread_any, targets_any, mask_lab_any, mask_tgt_any,
    to_features, to_towers, to_heads, to_bias,
    out_features, out_towers, out_heads, out_bias, out_sem,
    bias_class, bias_boxes, head_class_bias, head_boxes_bias, valid, label,
    tower_class, tower_boxes, head_class, head_boxes, features, state, labels, targets_in,
    spread, targets, mask_lab, mask_tgt, bias, fetch_sem,
    own, own_h, own_v, w, wh, hp, hv, g, gh, rc, rch, sm, su, sv, r1a, r1b, r1m, r1u, r1v, r2, r2m, r2u, r2v,
    quarter, sum_m, sum_u, sum_v, rz, rzm, rzu, rzv, done, layer_in,
    act3, g3, gl, act_t, last_t, slope, spare, code, target, da,
    x, lab, lab_in, count_mine, count_sum, count_in, grad_bias, bias_in, bias_z, dx, dx_in, tile_out, features_in,
    send_sem, recv_sem,
):
    s, dp = lax.axis_index("section"), lax.axis_index("dp")
    my_y, my_x, my_z, my_c = s // 2, s % 2, dp // 2, dp % 2
    sx, sy, sg = 2 * my_y + (1 - my_x), 2 * (1 - my_y) + my_x, 2 * (1 - my_y) + (1 - my_x)
    to_x, to_y, to_g, to_c = (sx, dp), (sy, dp), (sg, dp), (s, 2 * my_z + 1 - my_c)
    plane = lambda k: (my_z + k) % PLANES
    to_z = lambda k: (s, 2 * plane(k) + my_c)
    to_pair = (s, 2 * (my_z + 1 - 2 * (my_z % 2)) + my_c)
    role = my_z % 2
    on_class, on_boxes = role == 0, role == 1
    net = Traffic(send_sem, recv_sem)
    m = SimpleNamespace(
        w=w, wh=wh, g=g, gh=gh, act3=act3, g3=g3, gl=gl, act_t=act_t, last_t=last_t, slope=slope, code=code,
        target=target, lab=lab, lab_in=lab_in, count_sum=count_sum, count_in=count_in, grad_bias=grad_bias,
        bias=bias, spread=spread, targets=targets, mask_lab=mask_lab, mask_tgt=mask_tgt, label=label, role=role,
    )

    def shard(z, c):
        return pl.ds(pl.multiple_of(ROWS * (2 * z + c), 16), ROWS)

    barrier = pltpu.get_barrier_semaphore()
    peers = (to_x, to_y, to_g, to_c, to_z(1), to_z(2), to_z(3))
    for peer in peers:
        pl.semaphore_signal(barrier, inc=1, device_id=peer, device_id_type=MESH)

    fetched = [
        pltpu.make_async_copy(src, dst, fetch_sem.at[i])
        for i, (src, dst) in enumerate(
            (
                (tower_class_any, tower_class), (tower_boxes_any, tower_boxes), (head_class_any, head_class),
                (head_boxes_any, head_boxes), (features_any, features), (state_any, state), (labels_any, labels),
                (targets_in_any, targets_in), (valid_any, valid), (mask_lab_any, mask_lab),
                (spread_any.at[role], spread), (mask_tgt_any, mask_tgt), (targets_any, targets), (label_any, label),
                (bias_class_any, bias_class), (bias_boxes_any, bias_boxes),
                (head_class_bias_any, head_class_bias), (head_boxes_bias_any, head_boxes_bias),
            )
        )
    ]
    for copy in fetched:
        copy.start()
    for copy in fetched[:4]:
        copy.wait()

    own[0] = tower_class[0].astype(BF16)
    own[1] = tower_boxes[0].astype(BF16)
    own_h[0:ROWS, :] = head_class[0:LANES, :].T.astype(BF16)
    rest, narrow = head_class.shape[0] - LANES, head_boxes.shape[0]
    spare[...] = jnp.zeros((ROWS, 2 * LANES), F32)
    spare[:, 0:rest] = head_class[LANES : LANES + rest, :].T
    spare[:, LANES : LANES + narrow] = head_boxes[...].T
    own_h[ROWS:PACK, :] = (spare[0:HALF, 0:LANES] + pltpu.roll(spare[HALF:ROWS, 0:LANES], TAIL, 1)).astype(BF16)
    own_v[...] = folded(spare[:, LANES : 2 * LANES]).astype(BF16)

    pl.semaphore_wait(barrier, len(peers))

    def kinds(kind_name):
        return ("M", "V") if kind_name == "M" else (kind_name,)

    def due(kind_name):
        return dict(T=None, M=on_class, U=on_boxes, V=on_boxes)[kind_name]

    def head_lanes(sec):
        return pl.ds(pl.multiple_of(LANES * sec, LANES), LANES)

    def place(kind_name, sec, z):
        if kind_name == "T":
            return w.at[sec, shard(z, my_c), :]
        if kind_name == "M":
            return wh.at[shard(z, my_c), head_lanes(sec)]
        if kind_name == "V":
            return hv.at[sec, z]
        return hp.at[sec, z]

    def own_shard(kind_name, which):
        if kind_name == "T":
            return own.at[which]
        if kind_name == "V":
            return own_v
        return own_h.at[pl.ds(0, ROWS) if kind_name == "M" else pl.ds(ROWS, HALF), :]

    def planes_send(kind_name):
        for k in (1, 3, 2):
            other = plane(k) % 2
            for kind in kinds(kind_name):
                when = dict(T=None, M=other == 0, U=other == 1, V=other == 1)[kind]
                net.send(("z", kind, k), own_shard(kind, other), place(kind, s, my_z), to_z(k), when)

    in_plane = (("x", to_x, sx), ("y", to_y, sy), ("g", to_g, sg))

    def rows_of(sec):
        return pl.ds(pl.multiple_of(64 * sec, 64), 64)

    def features_send():
        for copy in fetched[4:9]:
            copy.wait()
        row = lax.broadcasted_iota(jnp.int32, (TILE, TILE * A), 0)
        found = jnp.zeros((TILE, TILE * A), F32)
        for t in range(SECTIONS):
            found += jnp.where(jnp.logical_and(state[t] == 1, row < valid[t]), 1.0, 0.0)
        count_mine[...] = jnp.full((8, LANES), jnp.sum(found), F32)
        inside = row < valid[s]
        kind = state[s]
        lab[...] = jnp.zeros_like(lab)
        lab[:, 0 : TILE * A] = jnp.where(
            inside,
            jnp.where(kind == 1, labels[s].astype(F32) + 2.0, jnp.where(kind == 2, 0.0, 1.0)),
            0.0,
        )
        lab[:, LAB : LAB + targets_in.shape[2]] = targets_in[s]
        for name, peer, sec in in_plane:
            net.send(("f", name), features.at[sec], x.at[0, rows_of(s), :], peer)
        net.send("count c", count_mine, count_in.at[0], to_c)
        net.send("lab", lab, lab_in, to_pair)

    def piece(kind_name, sec, j):
        return place(kind_name, sec, (my_z + PLANES - j) % PLANES)

    def ways(kind_name, j):
        if WAYS[kind_name.replace("V", "M") + str(j)] == "A":
            return (to_x, sx), (to_y, sy)
        return (to_y, sy), (to_x, sx)

    def gather_mine(kind_name, j):
        for kind in kinds(kind_name):
            mine = piece(kind, s, j)
            if j:
                net.arrived(("z", kind, j), mine, to_z(PLANES - j), due(kind))
            for (n, _), name in zip(ways(kind, j), ("g1", "g2")):
                net.send((name, kind, j), mine, mine, n, due(kind))
        if kind_name == "T":
            net.send(("swap", "T", j, 0), mine, mine, to_c)

    def gather_pass(kind_name, j):
        (n1, s1), (n2, s2) = ways(kind_name, j)
        for kind in kinds(kind_name):
            first = piece(kind, s1, j)
            net.arrived(("g1", kind, j), first, n1, due(kind))
            net.send(("g3", kind, j), first, first, n2, due(kind))
        if kind_name == "T":
            net.send(("swap", "T", j, 1), first, first, to_c)

    def gather_last(kind_name, j):
        (n1, s1), (n2, s2) = ways(kind_name, j)
        for i, (name, sec) in enumerate((("g2", s2), ("g3", sg))):
            for kind in kinds(kind_name):
                got = piece(kind, sec, j)
                net.arrived((name, kind, j), got, n2, due(kind))
            if kind_name == "T":
                net.send(("swap", "T", j, 2 + i), got, got, to_c)
        z = (my_z + PLANES - j) % PLANES
        at = pl.multiple_of(ROWS * (2 * z + my_c), 16)
        if kind_name == "M":

            @pl.when(on_boxes)
            def _():
                for sec in range(SECTIONS):
                    for i, part in enumerate(unfolded(hv[sec, z])):
                        rows = pl.ds(at + i * FOLD_ROWS, FOLD_ROWS)
                        wh[rows, sec * LANES : (sec + 1) * LANES] = part.astype(BF16)

            block = wh.at[pl.ds(at, ROWS), 0:MAIN]
            net.send(("swap", "M", j), block, block, to_c)
        if kind_name == "U":

            @pl.when(on_boxes)
            def _():
                for q in range(2):
                    lanes = slice((SECTIONS + q) * LANES, (SECTIONS + q + 1) * LANES)
                    top, bottom = swap_halves(hp[2 * q, z], hp[2 * q + 1, z])
                    wh[pl.ds(at, HALF), lanes] = top.astype(BF16)
                    wh[pl.ds(at + HALF, HALF), lanes] = bottom.astype(BF16)

            block = wh.at[pl.ds(at, ROWS), MAIN:HEAD]
            net.send(("up", j), block, block, to_pair, on_boxes)

    def relayed_plane(j):
        return (my_z + 1 + PLANES - j) % PLANES

    def gather_relayed(kind_name, j):
        block = wh.at[shard(relayed_plane(j), my_c), MAIN:HEAD]
        net.arrived(("up", j), block, to_pair, on_class)
        net.send(("swap", "U", j), block, block, to_c, on_class)

    def swapped(kind_name, j):
        z = (my_z + PLANES - j) % PLANES
        if kind_name == "M":
            net.arrived(("swap", "M", j), wh.at[shard(z, 1 - my_c), 0:MAIN], to_c)
            return
        if kind_name == "U":
            net.arrived(("swap", "U", j), wh.at[shard(relayed_plane(j), 1 - my_c), MAIN:HEAD], to_c, on_class)
            return
        (_, s1), (_, s2) = ways(kind_name, j)
        for i, sec in enumerate((s, s1, s2, sg)):
            net.arrived(("swap", "T", j, i), w.at[sec, shard(z, 1 - my_c), :], to_c)

    def features_tile():
        x[0, rows_of(s), :] = features[s]
        for name, peer, sec in in_plane:
            net.arrived(("f", name), x.at[0, rows_of(sec), :], peer)
        net.send("tile", x.at[0], x.at[1], to_pair)
        net.arrived("count c", count_in.at[0], to_c)
        count_sum[...] = count_mine[...] + count_in[0]
        for k in (1, 2, 3):
            net.send(("count", k), count_sum, count_in.at[k], to_z(k))

    def prepare():
        for ref in (act3, *(g3.at[l] for l in range(LAYERS)), gl):
            for t in range(2):
                ref[t, 0:TILE, :] = jnp.zeros((TILE, ref.shape[2]), BF16)
                ref[t, TILE + PX : 2 * TILE + PX, :] = jnp.zeros((TILE, ref.shape[2]), BF16)
        grad_bias[...] = jnp.zeros_like(grad_bias)
        for copy in fetched[9:]:
            copy.wait()
        bias[0:LAYERS, 0:CH] = jnp.where(role == 0, bias_class[...], bias_boxes[...])
        bias[4:5, :] = jnp.where(role == 0, lay(head_class_bias[...]), lay(head_boxes_bias[...]))
        net.arrived("lab", lab_in, to_pair)
        prepare_loss(m)
        net.arrived("tile", x.at[1], to_pair)
        for t in range(2):
            v = x[t].astype(F32)
            put_shifted(act3, t, v, 1, CH)
            act_t[0, :, t * PX : (t + 1) * PX] = v.T.astype(BF16)

    def forward(l):
        if l == 0:
            for j in range(PLANES):
                swapped("T", j)
        forward_layer(m, l)

    def head(kind_name):
        if kind_name == "M":
            for k in (1, 2, 3):
                net.arrived(("count", k), count_in.at[k], to_z(PLANES - k))
        for j in range(PLANES):
            swapped(kind_name, j)
        head_gradients(m, head_part[kind_name])

    head_part = dict(M=slice(0, MAIN), U=slice(MAIN, HEAD))
    w[s, shard(my_z, my_c), :] = own[role]
    hp[s, my_z] = own_h[ROWS:PACK, :]
    hv[s, my_z] = own_v[...]

    @pl.when(on_class)
    def _():
        wh[shard(my_z, my_c), head_lanes(s)] = own_h[0:ROWS, :]


    def added(a, b):
        return a + b

    def half_rows(which):
        return pl.ds(pl.multiple_of(HALF * which, 16), HALF)

    def half_lanes(which):
        return pl.ds(pl.multiple_of(LANES * which, LANES), LANES)

    def core_send(l, zp):
        theirs = shard(zp, 1 - my_c)
        if l in head_part:
            when = on_class if l == "U" else None
            net.send(("rc", l, zp), gh.at[theirs, head_part[l]], rch.at[zp, :, head_part[l]], to_c, when)
        else:
            net.send(("rc", l, zp), g.at[l, theirs, :], rc.at[l, zp], to_c)

    first, second = pl.ds(0, 2), pl.ds(2, 2)

    def tower_cores(l):
        for zp in range(PLANES):
            net.arrived(("rc", l, zp), rc.at[l, zp], to_c)
            rc[l, zp] = added(rc[l, zp], g[l, shard(zp, my_c), :])
            if zp == 1:
                net.send(("r1a", l), rc.at[l, first, :, half_lanes(1 - my_x)], r1a.at[l], to_x)
        net.send(("r1b", l), rc.at[l, second, half_rows(1 - my_y), :], r1b.at[l], to_y)

    def tower_plane(l):
        net.arrived(("r1a", l), r1a.at[l], to_x)
        for zp in (0, 1):
            rc[l, zp, :, half_lanes(my_x)] = added(rc[l, zp, :, half_lanes(my_x)], r1a[l, zp])
        net.send(("r2a", l), rc.at[l, first, half_rows(1 - my_y), half_lanes(my_x)], r2.at[l, first], to_y)
        net.arrived(("r1b", l), r1b.at[l], to_y)
        for zp in (2, 3):
            rc[l, zp, half_rows(my_y), :] = added(rc[l, zp, half_rows(my_y), :], r1b[l, zp - 2])
        net.send(("r2b", l), rc.at[l, second, half_rows(my_y), half_lanes(1 - my_x)], r2.at[l, second], to_x)

    def to_planes(name, src, dst):
        for zp in range(PLANES):
            k = (zp + PLANES - my_z) % PLANES
            net.send(name, src.at[zp], dst.at[my_z], (s, 2 * zp + my_c), my_z != zp, span=PLANES, offset=k)

    def tower_planes(l):
        net.arrived(("r2a", l), r2.at[l, first], to_y)
        net.arrived(("r2b", l), r2.at[l, second], to_x)
        for zp in range(PLANES):
            quarter[l, zp] = added(rc[l, zp, half_rows(my_y), half_lanes(my_x)], r2[l, zp])
        to_planes(("rz", l), quarter.at[l], rz.at[l])

    def from_planes(name, mine, others):
        for k in (1, 2, 3):
            net.arrived(name, others.at[plane(PLANES - k)], to_z(PLANES - k), span=PLANES, offset=k)
        same = mine[my_z].astype(F32) + others[plane(2)].astype(F32)
        return same, others[plane(1)].astype(F32) + others[plane(3)].astype(F32)

    def tower_sum(l):
        same, other = from_planes(("rz", l), quarter.at[l], rz.at[l])
        done[l, role] = same.astype(BF16)
        done[l, 1 - role] = other.astype(BF16)
        to_l = (l, dp)
        net.send("layer", done.at[l], layer_in.at[s], to_l, s != l, span=SECTIONS, offset=s)

        @pl.when(s == l)
        def _():
            out_towers[role, half_rows(my_y), half_lanes(my_x)] = same
            out_towers[1 - role, half_rows(my_y), half_lanes(my_x)] = other

    def tower_store():
        for sec, peer in ((sx, to_x), (sy, to_y), (sg, to_g)):
            net.arrived("layer", layer_in.at[sec], peer, span=SECTIONS, offset=sec)
            for i in range(2):
                out_towers[i, half_rows(sec // 2), half_lanes(sec % 2)] = layer_in[sec, i].astype(F32)
        give(out_towers, to_towers)

    def head_refs(kind):
        return dict(
            M=(sm, r1m, r2m, sum_m, rzm), U=(su, r1u, r2u, sum_u, rzu), V=(sv, r1v, r2v, sum_v, rzv)
        )[kind]

    def both_cores(zp, rows, lanes):
        at = pl.multiple_of(ROWS * (2 * zp + my_c) + rows[0], 16)
        mine = gh[pl.ds(at, rows[1]), lanes]
        return rch[zp, rows[0] : rows[0] + rows[1], lanes].astype(F32) + mine.astype(F32)

    def head_cores(kind_name, zp):
        landed = rch.at[zp, :, head_part[kind_name]]
        if kind_name == "M":
            net.arrived(("rc", "M", zp), landed, to_c)

            def store(kind):
                for sec in range(SECTIONS):
                    v = both_cores(zp, (0, ROWS), slice(sec * LANES, (sec + 1) * LANES))
                    v = v if kind == "M" else folded(v)
                    head_refs(kind)[0][sec // 2, sec % 2, zp] = v.astype(BF16)

            for kind in kinds("M"):
                pl.when(due(kind))(functools.partial(store, kind))
            head_first_send("M", zp)
            return
        net.arrived(("rc", "U", zp), landed, to_c, on_class)

        @pl.when(on_class)
        def _():
            for q in range(2):
                lanes = slice((SECTIONS + q) * LANES, (SECTIONS + q + 1) * LANES)
                left, right = swap_halves(both_cores(zp, (0, HALF), lanes), both_cores(zp, (HALF, HALF), lanes))
                su[q, 0, zp] = left.astype(BF16)
                su[q, 1, zp] = right.astype(BF16)

        block = su.at[:, :, zp]
        net.send(("ru", zp), block, block, to_pair, on_class)

    def head_relayed(kind_name, zp):
        net.arrived(("ru", zp), su.at[:, :, zp], to_pair, on_boxes)
        head_first_send(kind_name, zp)

    def head_first_send(kind_name, zp):
        for kind in kinds(kind_name):
            into, landing = head_refs(kind)[:2]
            if zp % 2 == 0:
                net.send(("h1", kind, zp), into.at[:, 1 - my_x, zp], landing.at[zp], to_x, due(kind))
            else:
                net.send(("h1", kind, zp), into.at[1 - my_y, :, zp], landing.at[zp], to_y, due(kind))

    def head_plane(kind_name, zp):
        for kind in kinds(kind_name):
            into, landing, landing2 = head_refs(kind)[:3]
            net.arrived(("h1", kind, zp), landing.at[zp], to_x if zp % 2 == 0 else to_y, due(kind))

            @pl.when(due(kind))
            def _():
                for i in range(2):
                    at = (i, my_x, zp) if zp % 2 == 0 else (my_y, i, zp)
                    into[at] = added(into[at], landing[zp, i])

            if zp % 2 == 0:
                net.send(("h2", kind, zp), into.at[1 - my_y, my_x, zp], landing2.at[zp], to_y, due(kind))
            else:
                net.send(("h2", kind, zp), into.at[my_y, 1 - my_x, zp], landing2.at[zp], to_x, due(kind))

    def head_planes(kind_name, zp):
        k = (zp + PLANES - my_z) % PLANES
        for kind in kinds(kind_name):
            into, _, landing2, total, others = head_refs(kind)
            net.arrived(("h2", kind, zp), landing2.at[zp], to_y if zp % 2 == 0 else to_x, due(kind))

            @pl.when(due(kind))
            def _():
                total[zp] = added(into[my_y, my_x, zp], landing2[zp])

            away = jnp.logical_and(due(kind), my_z != zp)
            to_zp = (s, 2 * zp + my_c)
            net.send(("hz", kind), total.at[zp], others.at[my_z], to_zp, away, span=PLANES, offset=k)

    def head_store(kind_name):
        for kind in kinds(kind_name):
            total, others = head_refs(kind)[3:]
            here = due(kind)
            for k in (1, 2, 3):
                when = here if k == 2 else jnp.logical_not(here)
                source = others.at[plane(PLANES - k)]
                net.arrived(("hz", kind), source, to_z(PLANES - k), when, span=PLANES, offset=k)

            def store(v):
                if kind == "M":
                    out_heads[0, 0:ROWS] = v
                elif kind == "U":
                    out_heads[0, ROWS:PACK] = v
                else:
                    for i, part in enumerate(unfolded(v)):
                        out_heads[1, i * FOLD_ROWS : (i + 1) * FOLD_ROWS] = part

            @pl.when(here)
            def _():
                store(total[my_z].astype(F32) + others[plane(2)].astype(F32))

            @pl.when(jnp.logical_not(here))
            def _():
                store(others[plane(1)].astype(F32) + others[plane(3)].astype(F32))

        if kind_name == "U":
            out_heads[1, ROWS:PACK] = jnp.zeros((HALF, LANES), F32)
        rows = pl.ds(0, ROWS) if kind_name == "M" else pl.ds(ROWS, HALF)
        give(out_heads.at[:, rows], to_heads.at[:, rows])

    def bias_cores():
        net.arrived("bias c", bias_in.at[0], to_c)
        bias_z[0] = grad_bias[...] + bias_in[0]
        net.send("bias x", bias_z.at[0], bias_in.at[1], to_x)

    def bias_plane():
        net.arrived("bias x", bias_in.at[1], to_x)
        bias_z[1] = bias_z[0] + bias_in[1]
        net.send("bias y", bias_z.at[1], bias_in.at[2], to_y)

    def bias_planes():
        net.arrived("bias y", bias_in.at[2], to_y)
        bias_z[2] = bias_z[1] + bias_in[2]
        for k in (1, 2, 3):
            net.send(("bias z", k), bias_z.at[2], bias_in.at[2 + k], to_z(k))

    def bias_store():
        for k in (1, 2, 3):
            net.arrived(("bias z", k), bias_in.at[2 + k], to_z(PLANES - k))
        out_bias[role] = bias_z[2] + bias_in[4]
        out_bias[1 - role] = bias_in[3] + bias_in[5]
        give(out_bias, to_bias)

    results = []

    def give(src, dst):
        copy = pltpu.make_async_copy(src, dst, out_sem.at[len(results)])
        copy.start()
        results.append(copy)

    def features_sum():
        net.arrived("dx", dx_in, to_pair)
        tile_out[...] = (da[...] + dx_in[...].astype(F32)).astype(BF16)
        for name, peer, sec in in_plane:
            net.send(("b", name), tile_out.at[rows_of(sec), :], features_in.at[s], peer)

    def features_store():
        for name, peer, sec in in_plane:
            net.arrived(("b", name), features_in.at[sec], peer)
            out_features[sec] = features_in[sec]
        out_features[s] = tile_out[rows_of(s), :]
        give(out_features, to_features)

    def head_gradient(kind_name, r):
        if kind_name == "M":
            head_kernel_gradient(m, head_part["M"], r)
        else:
            pl.when(on_class)(lambda: head_kernel_gradient(m, head_part["U"], r))
        for zp in ((0,), (1,), (2, 3))[r]:
            core_send(kind_name, zp)

    def head_input():
        pl.when(on_class)(lambda: head_input_gradient(m, slice(0, HEAD)))
        pl.when(on_boxes)(lambda: head_input_gradient(m, slice(0, MAIN)))

    def layer_gradient(l):
        for r in range(3):
            layer_kernel_gradient(m, l, r)
        for zp in range(PLANES):
            core_send(l, zp)

    def layer_input(l):
        for t in range(2):
            v = input_gradient(m, l, t)
            if l:
                layer_upstream(m, l - 1, t, v)
            elif t == 0:
                da[...] = v
            else:
                dx[...] = v.astype(BF16)
        if l == 0:
            net.send("dx", dx, dx_in, to_pair)
        if l == 1:
            net.send("bias c", grad_bias, bias_in.at[0], to_c)

    def either(of_head, of_tower):
        return lambda *which: of_head(*which) if which[0] in head_part else of_tower(*which)

    steps = dict(
        d=gather_relayed, r=head_relayed, z=planes_send, f=features_send, e=features_tile, y=prepare, a=gather_mine, b=gather_pass, c=gather_last,
        F=forward, H=head, W=head_gradient, X=head_input, w=layer_gradient, x=layer_input,
        k=either(head_cores, tower_cores), p=either(head_plane, tower_plane), q=either(head_planes, tower_planes),
        s=either(head_store, tower_sum), t=tower_store, D=features_sum, E=features_store,
        B=lambda which: dict(k=bias_cores, p=bias_plane, q=bias_planes, s=bias_store)[which](),
    )
    for step in SCHEDULE:
        steps[step[0]](*(int(v) if v.isdigit() else v for v in step[1:]))
    for copy in results:
        copy.wait()
    net.finish()


def lay(vector):
    width = vector.shape[0]
    per = width // SECTIONS
    row = jnp.concatenate([vector.reshape(1, width), jnp.zeros((1, HEAD - width), F32)], axis=1)
    row = jnp.broadcast_to(row, (8, HEAD))
    lane = lax.broadcasted_iota(jnp.int32, (8, LANES), 1)
    main, tails = [], []
    for s in range(SECTIONS):
        turned = pltpu.roll(row, (HEAD - s * per) % HEAD, 1)
        main.append(jnp.where(lane < per, turned[:, 0:LANES], 0.0))
        tails.append(jnp.where(lane < per - LANES, turned[:, LANES : 2 * LANES], 0.0))
    folded = [tails[2 * q] + pltpu.roll(tails[2 * q + 1], TAIL, 1) for q in range(2)]
    return jnp.concatenate(main + folded, axis=1)[0:1, :]


def unlay(row, width):
    per = width // SECTIONS
    row = jnp.broadcast_to(row, (8, HEAD))
    lane = lax.broadcasted_iota(jnp.int32, (8, LANES), 1)
    total = jnp.zeros((8, HEAD), F32)
    for s in range(SECTIONS):
        tail = row[:, MAIN + (s // 2) * LANES : MAIN + (s // 2 + 1) * LANES]
        tail = pltpu.roll(tail, TAIL, 1) if s % 2 else tail
        parts = [jnp.where(lane < per, row[:, s * LANES : (s + 1) * LANES], 0.0), jnp.where(lane < per - LANES, tail, 0.0)]
        total += pltpu.roll(jnp.concatenate(parts + [jnp.zeros((8, HEAD - 2 * LANES), F32)], axis=1), s * per, 1)
    return total[0:1, 0:width].reshape(width)


def finish_kernel(
    features, towers, heads, sums,
    out_features, out_class, out_bias_class, out_boxes, out_bias_boxes, out_head_class, out_head_class_bias,
    out_head_boxes, out_head_boxes_bias,
):
    out_features[...] = features[...]
    for i, (tower, bias, head, head_bias) in enumerate(
        (
            (out_class, out_bias_class, out_head_class, out_head_class_bias),
            (out_boxes, out_bias_boxes, out_head_boxes, out_head_boxes_bias),
        )
    ):
        tower[0] = towers[i]
        bias[...] = sums[i, 0:LAYERS, 0:CH]
        width = head.shape[0]
        main, rest = min(width, LANES), max(0, width - LANES)
        head[0:main, :] = heads[i, 0:ROWS, :].T[0:main, :]
        if rest:
            low = heads[i, ROWS:PACK, :]
            both = jnp.concatenate([low, pltpu.roll(low, TAIL, 1)], axis=0)
            head[LANES:width, :] = both.T[0:rest, :]
        head_bias[...] = unlay(sums[i, LAYERS : LAYERS + 1, :], head_bias.shape[0])


def fast(features, tower_class, bias_class, tower_boxes, bias_boxes, head_class, head_class_bias, head_boxes,
         head_boxes_bias, anchor_state, class_labels, box_targets, valid_rows):
    class_width, boxes_width = head_class_bias.shape[0], head_boxes_bias.shape[0]
    spread, targets, mask_lab, mask_tgt, label = constants(class_width, boxes_width)
    tiles = features.shape[0]
    vmem = pl.BlockSpec(memory_space=pltpu.VMEM)
    v = lambda shape, dtype: pltpu.VMEM(shape, dtype)
    out = lambda shape, dtype: jax.ShapeDtypeStruct(shape, dtype)
    anywhere = pl.BlockSpec(memory_space=pl.ANY)
    raw = pl.pallas_call(
        head_kernel,
        out_shape=(
            out((tiles, 64, CH), BF16),
            out((2, ROWS, CH), F32),
            out((2, PACK, LANES), F32),
            out((2, 8, HEAD), F32),
        ),
        in_specs=[anywhere] * 18,
        out_specs=(anywhere,) * 4,
        scratch_shapes=[
            v((tiles, 64, CH), BF16),
            v((2, ROWS, CH), F32),
            v((2, PACK, LANES), F32),
            v((2, 8, HEAD), F32),
            pltpu.SemaphoreType.DMA((5,)),
            v(bias_class.shape, F32),
            v(bias_boxes.shape, F32),
            v(head_class_bias.shape, F32),
            v(head_boxes_bias.shape, F32),
            pltpu.SMEM(valid_rows.shape, jnp.int32),
            v(label.shape, F32),
            v(tower_class.shape, F32),
            v(tower_boxes.shape, F32),
            v(head_class.shape[::-1], F32),
            v(head_boxes.shape[::-1], F32),
            v((tiles, 64, CH), BF16),
            v(anchor_state.shape, jnp.int32),
            v(class_labels.shape, jnp.int32),
            v(box_targets.shape, F32),
            v(spread.shape[1:], BF16),
            v(targets.shape, BF16),
            v(mask_lab.shape, BF16),
            v(mask_tgt.shape, BF16),
            v((8, HEAD), F32),
            pltpu.SemaphoreType.DMA((18,)),
            v((2, ROWS, CH), BF16),
            v((PACK, LANES), BF16),
            v((FOLD_ROWS, LANES), BF16),
            v((LAYERS, DEEP, CH), BF16),
            v((DEEP, HEAD), BF16),
            v((SECTIONS, PLANES, HALF, LANES), BF16),
            v((SECTIONS, PLANES, FOLD_ROWS, LANES), BF16),
            v((LAYERS, DEEP, CH), BF16),
            v((DEEP, HEAD), BF16),
            v((LAYERS, PLANES, ROWS, CH), BF16),
            v((PLANES, ROWS, HEAD), BF16),
            v((2, 2, PLANES, ROWS, LANES), BF16),
            v((2, 2, PLANES, HALF, LANES), BF16),
            v((2, 2, PLANES, FOLD_ROWS, LANES), BF16),
            v((LAYERS, 2, ROWS, LANES), BF16),
            v((LAYERS, 2, HALF, CH), BF16),
            v((PLANES, 2, ROWS, LANES), BF16),
            v((PLANES, 2, HALF, LANES), BF16),
            v((PLANES, 2, FOLD_ROWS, LANES), BF16),
            v((LAYERS, PLANES, HALF, LANES), BF16),
            v((PLANES, ROWS, LANES), BF16),
            v((PLANES, HALF, LANES), BF16),
            v((PLANES, FOLD_ROWS, LANES), BF16),
            v((LAYERS, PLANES, HALF, LANES), BF16),
            v((PLANES, ROWS, LANES), BF16),
            v((PLANES, HALF, LANES), BF16),
            v((PLANES, FOLD_ROWS, LANES), BF16),
            v((LAYERS, PLANES, HALF, LANES), BF16),
            v((PLANES, ROWS, LANES), BF16),
            v((PLANES, HALF, LANES), BF16),
            v((PLANES, FOLD_ROWS, LANES), BF16),
            v((LAYERS, 2, HALF, LANES), BF16),
            v((SECTIONS, 2, HALF, LANES), BF16),
            v((2, PX + 2 * TILE, 3 * CH), BF16),
            v((LAYERS, 2, PX + 2 * TILE, 3 * CH), BF16),
            v((2, PX + 2 * TILE, HEAD), BF16),
            v((LAYERS, CH, 2 * PX), BF16),
            v((3, CH, 2 * PX), BF16),
            v((LAYERS, 2 * PX, CH), F32),
            v((ROWS, 2 * LANES), F32),
            v((2 * PX, HEAD), F32),
            v((2 * PX, MAIN), F32),
            v((PX, CH), F32),
            v((2, PX, CH), BF16),
            v((TILE, LAB + TGT), F32),
            v((TILE, LAB + TGT), F32),
            v((8, LANES), F32),
            v((8, LANES), F32),
            v((4, 8, LANES), F32),
            v((8, HEAD), F32),
            v((6, 8, HEAD), F32),
            v((3, 8, HEAD), F32),
            v((PX, CH), BF16),
            v((PX, CH), BF16),
            v((PX, CH), BF16),
            v((SECTIONS, 64, CH), BF16),
            pltpu.SemaphoreType.DMA((SEMAPHORES,)),
            pltpu.SemaphoreType.DMA((SEMAPHORES,)),
        ],
        compiler_params=pltpu.CompilerParams(
            collective_id=0, has_side_effects=True, vmem_limit_bytes=62 * 2**20
        ),
    )(
        features.reshape(tiles, 64, CH), tower_class, tower_boxes, head_class.T, head_boxes.T, bias_class, bias_boxes,
        head_class_bias, head_boxes_bias, anchor_state, class_labels, box_targets, valid_rows, label,
        spread, targets, mask_lab, mask_tgt,
    )
    results = pl.pallas_call(
        finish_kernel,
        out_shape=(
            out((tiles, 64, CH), BF16),
            out(tower_class.shape, F32),
            out(bias_class.shape, F32),
            out(tower_boxes.shape, F32),
            out(bias_boxes.shape, F32),
            out(head_class.shape[::-1], F32),
            out(head_class_bias.shape, F32),
            out(head_boxes.shape[::-1], F32),
            out(head_boxes_bias.shape, F32),
        ),
        in_specs=[vmem] * 4,
        out_specs=(vmem,) * 9,
    )(*raw)
    of_features, of_class, of_bias_class, of_boxes, of_bias_boxes, of_head_class, *rest = results
    of_head_class_bias, of_head_boxes, of_head_boxes_bias = rest
    return (
        of_features.reshape(features.shape), of_class, of_bias_class, of_boxes, of_bias_boxes,
        of_head_class.T, of_head_class_bias, of_head_boxes.T, of_head_boxes_bias,
    )


def shifted(block, axis, distance):
    devices = range(lax.axis_size(axis))
    route = [(i - distance, i) for i in devices if i - distance in devices]
    return lax.ppermute(block, axis, route)


def anchor_masks(anchor_state, valid_rows):
    tile_count = anchor_state.shape[0]
    anchor_kind = anchor_state.reshape(tile_count, TILE, TILE, A)
    row_index = lax.broadcasted_iota(jnp.int32, (tile_count, TILE, 1, 1), 1)
    inside = row_index < valid_rows.reshape(tile_count, 1, 1, 1)
    positive = jnp.logical_and(anchor_kind == 1, inside).astype(jnp.float32)
    counted = jnp.logical_and(anchor_kind != 2, inside).astype(jnp.float32)
    return (positive, counted)


def head_loss(logits, box_values, positive, counted, class_labels, box_targets, normalizer):
    tile_count = logits.shape[0]
    scores = logits.reshape(tile_count, TILE, TILE, A, K)
    labels = class_labels.reshape(tile_count, TILE, TILE, A, 1)
    classes = lax.broadcasted_iota(jnp.int32, (1, 1, 1, 1, K), 4)
    target = (labels == classes).astype(jnp.float32) * positive[..., None]
    chance = jax.nn.sigmoid(scores)
    entropy = jax.nn.softplus(scores) - target * scores
    agreement = chance * target + (1.0 - chance) * (1.0 - target)
    balance = 0.25 * target + 0.75 * (1.0 - target)
    focal_terms = balance * (1.0 - agreement) ** 2 * entropy
    focal_sum = jnp.sum(focal_terms * counted[..., None])
    offsets = box_values.reshape(tile_count, TILE, TILE, A, 4) - box_targets.reshape(
        tile_count, TILE, TILE, A, 4
    )
    spread = jnp.abs(offsets)
    huber_terms = jnp.where(
        spread < huber_beta, 0.5 * offsets * offsets / huber_beta, spread - 0.5 * huber_beta
    )
    box_sum = jnp.sum(huber_terms * positive[..., None])
    return (focal_sum + box_sum) / normalizer


def unfold(values):
    tile_count, tile_side, channels = (values.shape[0], values.shape[1], values.shape[3])
    padded = jnp.pad(values, ((0, 0), (1, 1), (1, 1), (0, 0)))
    pieces = [
        padded[:, row_shift : row_shift + tile_side, col_shift : col_shift + tile_side, :]
        for row_shift in range(3)
        for col_shift in range(3)
    ]
    return jnp.concatenate(pieces, axis=-1).reshape(
        tile_count * tile_side * tile_side, 9 * channels
    )


def fold_back(columns, tile_count, tile_side, channels):
    shaped = columns.reshape(tile_count, tile_side, tile_side, 9 * channels)
    padded = jnp.zeros((tile_count, tile_side + 2, tile_side + 2, channels), jnp.float32)
    for tap_index in range(9):
        row_shift = tap_index // 3
        col_shift = tap_index % 3
        padded = padded.at[
            :, row_shift : row_shift + tile_side, col_shift : col_shift + tile_side, :
        ].add(shaped[..., tap_index * channels : (tap_index + 1) * channels])
    return padded[:, 1 : tile_side + 1, 1 : tile_side + 1, :]


def weight_grad(columns, upstream):
    return jnp.einsum("pk,pc->kc", columns, upstream, preferred_element_type=jnp.float32)


def input_cols(upstream, weight):
    return jnp.einsum("pc,kc->pk", upstream, weight, preferred_element_type=jnp.float32)


def pick(buffer, slot_index):
    return lax.dynamic_index_in_dim(buffer, slot_index, 0, keepdims=False)


def store(buffer, update, slot_index, active):
    return lax.dynamic_update_index_in_dim(
        buffer, jnp.where(active, update, pick(buffer, slot_index)), slot_index, 0
    )


def per_device(
    features,
    tower_class,
    bias_class,
    tower_boxes,
    bias_boxes,
    head_class,
    head_class_bias,
    head_boxes,
    head_boxes_bias,
    anchor_state,
    class_labels,
    box_targets,
    valid_rows,
):
    section_count = lax.axis_size("section")
    section_index = lax.axis_index("section")
    final_section = section_count - 1
    is_first = section_index == 0
    is_final = section_index == final_section
    tile_dev = features.shape[0]
    per_micro = tile_dev // MICRO
    whole = lax.all_gather(features, "section", axis=1, tiled=True)
    tile_side = whole.shape[1]
    channels = whole.shape[3]
    pixels = per_micro * tile_side * tile_side
    act_shape = (per_micro, tile_side, tile_side, channels)
    positive, counted = anchor_masks(anchor_state, valid_rows)
    found = lax.psum(jnp.sum(positive), "dp")
    normalizer = jnp.maximum(found, 1.0)
    gathered = (
        lax.all_gather(tower_class.astype(jnp.bfloat16), "dp", axis=1, tiled=True),
        lax.all_gather(tower_boxes.astype(jnp.bfloat16), "dp", axis=1, tiled=True),
        lax.all_gather(head_class.astype(jnp.bfloat16), "dp", axis=0, tiled=True),
        lax.all_gather(head_boxes.astype(jnp.bfloat16), "dp", axis=0, tiled=True),
    )
    weight_class = gathered[0][0]
    weight_boxes = gathered[1][0]
    head_weight_class, head_weight_boxes = (
        lax.all_gather(gathered[2], "section", axis=1, tiled=True),
        lax.all_gather(gathered[3], "section", axis=1, tiled=True),
    )
    layer_bias_class = lax.dynamic_index_in_dim(bias_class, section_index, 0, keepdims=False)
    layer_bias_boxes = lax.dynamic_index_in_dim(bias_boxes, section_index, 0, keepdims=False)
    class_width = head_weight_class.shape[1]
    boxes_width = head_weight_boxes.shape[1]
    patch_width = head_weight_class.shape[0]

    def head_pass(stored_class, stored_boxes, slot_index):
        cols_class = unfold(stored_class)
        cols_boxes = unfold(stored_boxes)
        logits = (
            jnp.dot(cols_class, head_weight_class, preferred_element_type=jnp.float32)
            + head_class_bias
        )
        box_values = (
            jnp.dot(cols_boxes, head_weight_boxes, preferred_element_type=jnp.float32)
            + head_boxes_bias
        )
        start = slot_index * per_micro
        pos_here = lax.dynamic_slice_in_dim(positive, start, per_micro, 0)
        counted_here = lax.dynamic_slice_in_dim(counted, start, per_micro, 0)
        labels_here = lax.dynamic_slice_in_dim(class_labels, start, per_micro, 0)
        targets_here = lax.dynamic_slice_in_dim(box_targets, start, per_micro, 0)

        def local_loss(logit_part, box_part):
            return head_loss(
                logit_part.reshape(per_micro, tile_side, tile_side, class_width),
                box_part.reshape(per_micro, tile_side, tile_side, boxes_width),
                pos_here,
                counted_here,
                labels_here,
                targets_here,
                normalizer,
            )

        total_loss, pullback = jax.vjp(local_loss, logits, box_values)
        grad_logits, grad_box = pullback(jnp.ones_like(total_loss))
        grad_logits = grad_logits.astype(jnp.bfloat16)
        grad_box = grad_box.astype(jnp.bfloat16)
        back_class = fold_back(
            input_cols(grad_logits, head_weight_class), per_micro, tile_side, channels
        )
        back_boxes = fold_back(
            input_cols(grad_box, head_weight_boxes), per_micro, tile_side, channels
        )
        return (
            weight_grad(cols_class, grad_logits),
            weight_grad(cols_boxes, grad_box),
            jnp.sum(grad_logits.astype(jnp.float32), 0),
            jnp.sum(grad_box.astype(jnp.float32), 0),
            back_class,
            back_boxes,
        )

    def head_spare(stored_class, stored_boxes, slot_index):
        return (
            jnp.zeros((patch_width, class_width), jnp.float32),
            jnp.zeros((patch_width, boxes_width), jnp.float32),
            jnp.zeros((class_width,), jnp.float32),
            jnp.zeros((boxes_width,), jnp.float32),
            jnp.zeros(act_shape, jnp.float32),
            jnp.zeros(act_shape, jnp.float32),
        )

    kept_class = jnp.zeros((MICRO,) + act_shape, jnp.bfloat16)
    kept_boxes = jnp.zeros((MICRO,) + act_shape, jnp.bfloat16)
    kept_pre_class = jnp.zeros((MICRO, pixels, channels), jnp.float32)
    kept_pre_boxes = jnp.zeros((MICRO, pixels, channels), jnp.float32)
    head_back_class = jnp.zeros((MICRO,) + act_shape, jnp.float32)
    head_back_boxes = jnp.zeros((MICRO,) + act_shape, jnp.float32)
    grad_head_class = jnp.zeros((patch_width, class_width), jnp.float32)
    grad_head_boxes = jnp.zeros((patch_width, boxes_width), jnp.float32)
    grad_hbias_class = jnp.zeros((class_width,), jnp.float32)
    grad_hbias_boxes = jnp.zeros((boxes_width,), jnp.float32)
    total_moments = MICRO + section_count - 1
    empty_act = jnp.zeros(act_shape, jnp.bfloat16)
    received = (empty_act, empty_act)
    for moment in range(total_moments):
        micro_index = moment - section_index
        active = jnp.logical_and(micro_index >= 0, micro_index < MICRO)
        slot_index = jnp.clip(micro_index, 0, MICRO - 1)
        if moment < MICRO:
            entering = whole[moment * per_micro : (moment + 1) * per_micro]
        else:
            entering = empty_act
        input_class = jnp.where(is_first, entering, received[0])
        input_boxes = jnp.where(is_first, entering, received[1])
        kept_class = store(kept_class, input_class, slot_index, active)
        kept_boxes = store(kept_boxes, input_boxes, slot_index, active)
        pre_class = (
            jnp.dot(unfold(input_class), weight_class, preferred_element_type=jnp.float32)
            + layer_bias_class
        )
        pre_boxes = (
            jnp.dot(unfold(input_boxes), weight_boxes, preferred_element_type=jnp.float32)
            + layer_bias_boxes
        )
        kept_pre_class = store(kept_pre_class, pre_class, slot_index, active)
        kept_pre_boxes = store(kept_pre_boxes, pre_boxes, slot_index, active)
        act_class = jax.nn.gelu(pre_class).astype(jnp.bfloat16).reshape(act_shape)
        act_boxes = jax.nn.gelu(pre_boxes).astype(jnp.bfloat16).reshape(act_shape)
        results = lax.cond(
            jnp.logical_and(is_final, active),
            head_pass,
            head_spare,
            act_class,
            act_boxes,
            slot_index,
        )
        grad_head_class = grad_head_class + results[0]
        grad_head_boxes = grad_head_boxes + results[1]
        grad_hbias_class = grad_hbias_class + results[2]
        grad_hbias_boxes = grad_hbias_boxes + results[3]
        head_back_class = store(head_back_class, results[4], slot_index, active)
        head_back_boxes = store(head_back_boxes, results[5], slot_index, active)
        if moment < total_moments - 1:
            received = shifted((act_class, act_boxes), "section", 1)
    grad_layer_class = jnp.zeros((patch_width, channels), jnp.float32)
    grad_layer_boxes = jnp.zeros((patch_width, channels), jnp.float32)
    grad_lbias_class = jnp.zeros((channels,), jnp.float32)
    grad_lbias_boxes = jnp.zeros((channels,), jnp.float32)
    input_back = jnp.zeros((MICRO,) + act_shape, jnp.float32)
    returned = (empty_act, empty_act)
    for moment in range(total_moments):
        micro_index = moment - (final_section - section_index)
        active = jnp.logical_and(micro_index >= 0, micro_index < MICRO)
        slot_index = jnp.clip(micro_index, 0, MICRO - 1)
        upstream_class = jnp.where(
            is_final, pick(head_back_class, slot_index), returned[0].astype(jnp.float32)
        ).reshape(pixels, channels)
        upstream_boxes = jnp.where(
            is_final, pick(head_back_boxes, slot_index), returned[1].astype(jnp.float32)
        ).reshape(pixels, channels)
        cols_class = unfold(pick(kept_class, slot_index))
        cols_boxes = unfold(pick(kept_boxes, slot_index))
        pre_class = pick(kept_pre_class, slot_index)
        pre_boxes = pick(kept_pre_boxes, slot_index)
        gelu_class = jax.vjp(jax.nn.gelu, pre_class)[1](upstream_class)[0]
        gelu_boxes = jax.vjp(jax.nn.gelu, pre_boxes)[1](upstream_boxes)[0]
        grad_pre_class = jnp.where(active, gelu_class, 0.0).astype(jnp.bfloat16)
        grad_pre_boxes = jnp.where(active, gelu_boxes, 0.0).astype(jnp.bfloat16)
        grad_layer_class = grad_layer_class + weight_grad(cols_class, grad_pre_class)
        grad_layer_boxes = grad_layer_boxes + weight_grad(cols_boxes, grad_pre_boxes)
        grad_lbias_class = grad_lbias_class + jnp.sum(grad_pre_class.astype(jnp.float32), 0)
        grad_lbias_boxes = grad_lbias_boxes + jnp.sum(grad_pre_boxes.astype(jnp.float32), 0)
        back_class = fold_back(
            input_cols(grad_pre_class, weight_class), per_micro, tile_side, channels
        )
        back_boxes = fold_back(
            input_cols(grad_pre_boxes, weight_boxes), per_micro, tile_side, channels
        )
        input_back = store(
            input_back, back_class + back_boxes, slot_index, jnp.logical_and(active, is_first)
        )
        if moment < total_moments - 1:
            returned = shifted(
                (back_class.astype(jnp.bfloat16), back_boxes.astype(jnp.bfloat16)), "section", -1
            )
    spread_back = jnp.where(
        is_first, input_back.reshape(tile_dev, tile_side, tile_side, channels), 0.0
    )
    grad_features = lax.psum_scatter(
        spread_back.astype(jnp.bfloat16), "section", scatter_dimension=1, tiled=True
    )
    summed = (
        lax.psum_scatter(grad_layer_class, "dp", scatter_dimension=0, tiled=True),
        lax.psum_scatter(grad_layer_boxes, "dp", scatter_dimension=0, tiled=True),
        lax.psum_scatter(grad_head_class, "dp", scatter_dimension=0, tiled=True),
        lax.psum_scatter(grad_head_boxes, "dp", scatter_dimension=0, tiled=True),
    )
    final_head_class, final_head_boxes = (
        lax.psum_scatter(
            summed[2].astype(jnp.bfloat16), "section", scatter_dimension=1, tiled=True
        ).astype(jnp.float32),
        lax.psum_scatter(
            summed[3].astype(jnp.bfloat16), "section", scatter_dimension=1, tiled=True
        ).astype(jnp.float32),
    )
    rows_class = lax.dynamic_update_index_in_dim(
        jnp.zeros((LAYERS, channels), jnp.float32), grad_lbias_class, section_index, 0
    )
    rows_boxes = lax.dynamic_update_index_in_dim(
        jnp.zeros((LAYERS, channels), jnp.float32), grad_lbias_boxes, section_index, 0
    )
    bias_sums = lax.psum(
        (rows_class, rows_boxes, grad_hbias_class, grad_hbias_boxes), ("section", "dp")
    )
    return (
        grad_features,
        summed[0][None],
        bias_sums[0],
        summed[1][None],
        bias_sums[1],
        final_head_class,
        bias_sums[2],
        final_head_boxes,
        bias_sums[3],
    )


def solution(mesh):
    fits = mesh.shape["section"] == SECTIONS == LAYERS and mesh.shape["dp"] == PLANES * CORES
    placed = (
        P("dp", "section", None, None),
        P("section", "dp", None),
        P(),
        P("section", "dp", None),
        P(),
        P("dp", "section"),
        P(),
        P("dp", "section"),
        P(),
        P("dp", None, None),
        P("dp", None, None),
        P("dp", None, None),
        P("dp"),
    )
    return jax.shard_map(
        fast if fits else per_device,
        mesh=mesh,
        in_specs=placed,
        out_specs=(
            P("dp", "section", None, None),
            P("section", "dp", None),
            P(),
            P("section", "dp", None),
            P(),
            P("dp", "section"),
            P(),
            P("dp", "section"),
            P(),
        ),
        check_vma=False,
    )
```

```python
import functools
import math
from types import SimpleNamespace

import jax
import jax.numpy as jnp
import numpy as np
from jax import lax
from jax.experimental import pallas as pl
from jax.experimental.pallas import tpu as pltpu
from jax.sharding import PartitionSpec as P

K = 80
A = 9
LAYERS = 4
TILE = 16
MICRO = 4


huber_beta = 1.0 / 9.0

F32 = jnp.float32
BF16 = jnp.bfloat16
MESH = pl.DeviceIdType.MESH
GELU_C = math.sqrt(2.0 / math.pi)

SECTIONS = 4
PLANES = 4
CORES = 2
CH = 256
PX = TILE * TILE
ROWS = 288
HALF = ROWS // 2
PACK = ROWS + HALF
LANES = 128
TAIL = 64
MAIN = SECTIONS * LANES
HEAD = MAIN + SECTIONS * TAIL
LAB = 256
TGT = 640
DEEP = 9 * CH
FOLD = 3
FOLD_ROWS = ROWS // FOLD
FOLD_LANES = 32


def head_layout(width):
    per = width // SECTIONS
    columns = np.full((HEAD,), -1)
    for s in range(SECTIONS):
        main = min(per, LANES)
        columns[s * LANES : s * LANES + main] = s * per + np.arange(main)
        rest = per - main
        at = SECTIONS * LANES + s * TAIL
        columns[at : at + rest] = s * per + main + np.arange(rest)
    return columns


def constants(class_width, boxes_width):
    classes, boxes = head_layout(class_width), head_layout(boxes_width)
    spread = np.zeros((2, LAB, HEAD), np.float32)
    targets = np.zeros((TGT, MAIN), np.float32)
    for j in range(TILE):
        for col in range(HEAD):
            if classes[col] >= 0:
                spread[0, j * A + classes[col] // K, col] = 1
            if boxes[col] >= 0:
                spread[1, j * A + boxes[col] // 4, col] = 1
                targets[j * boxes_width + boxes[col], col] = 1
    pixel = np.arange(PX)[:, None] % TILE
    mask_lab = (np.arange(LAB)[None, :] // A == pixel) & (np.arange(LAB)[None, :] < TILE * A)
    mask_tgt = (np.arange(TGT)[None, :] // boxes_width == pixel) & (np.arange(TGT)[None, :] < TILE * boxes_width)
    label = np.where(classes >= 0, classes % K, -9).astype(np.float32)[None, :] + 2.0
    bf = lambda v: jnp.asarray(v.astype(np.float32), BF16)
    return bf(spread), bf(targets), bf(mask_lab), bf(mask_tgt), jnp.asarray(np.repeat(label, 8, 0))


def dot(a, b):
    return jnp.dot(a, b, preferred_element_type=F32)


def dot_nt(a, b):
    return lax.dot_general(a, b, (((1,), (1,)), ((), ())), preferred_element_type=F32)


def moved_right(v):
    col = lax.broadcasted_iota(jnp.int32, v.shape, 0) % TILE
    return jnp.where(col == 0, 0.0, pltpu.roll(v, 1, 0))


def moved_left(v):
    col = lax.broadcasted_iota(jnp.int32, v.shape, 0) % TILE
    return jnp.where(col == TILE - 1, 0.0, pltpu.roll(v, PX - 1, 0))


def put_shifted(ref, t, v, order, width):
    blocks = (moved_right(v), v, moved_left(v))[::order]
    for s, block in enumerate(blocks):
        ref[t, TILE : TILE + PX, s * width : (s + 1) * width] = block.astype(BF16)


def shifted_rows(ref, r, lanes=slice(None)):
    return ref[:, TILE * r : TILE * r + PX, lanes].reshape(2 * PX, -1)


def swap_halves(p, q):
    p, q = p.astype(F32), q.astype(F32)
    low = lax.broadcasted_iota(jnp.int32, p.shape, 1) < TAIL
    p_turned, q_turned = pltpu.roll(p, TAIL, 1), pltpu.roll(q, TAIL, 1)
    return jnp.where(low, p, q_turned), jnp.where(low, p_turned, q)


def folded(v):
    parts = [v[i * FOLD_ROWS : (i + 1) * FOLD_ROWS] for i in range(FOLD)]
    return parts[0] + sum(pltpu.roll(part, i * FOLD_LANES, 1) for i, part in enumerate(parts) if i)


def unfolded(v):
    v = v.astype(F32)
    low = lax.broadcasted_iota(jnp.int32, v.shape, 1) < FOLD_LANES
    return [
        jnp.where(low, pltpu.roll(v, LANES - i * FOLD_LANES, 1) if i else v, 0.0) for i in range(FOLD)
    ]


def conv(act3, t, kernel, lanes=slice(None)):
    return sum(
        dot(act3[t, TILE * r : TILE * r + PX, :], kernel[3 * CH * r : 3 * CH * (r + 1), lanes]) for r in range(3)
    )


def forward_layer(m, l):
    for t in range(2):
        z = conv(m.act3, t, m.w.at[l]) + m.bias[l : l + 1, 0:CH]
        square = z * z
        th = jnp.tanh(GELU_C * (z + 0.044715 * z * square))
        half = 0.5 * (1.0 + th)
        a = z * half
        m.slope[l, t * PX : (t + 1) * PX, :] = half + (0.5 * GELU_C) * z * (1.0 - th * th) * (
            1.0 + (3 * 0.044715) * square
        )
        put_shifted(m.act3, t, a, 1, CH)
        if l + 1 < LAYERS:
            m.act_t[l + 1, :, t * PX : (t + 1) * PX] = a.T.astype(BF16)
        else:
            for i, moved in enumerate((moved_right(a), a, moved_left(a))):
                m.last_t[i, :, t * PX : (t + 1) * PX] = moved.T.astype(BF16)


def expand(row, mask):
    lanes = row.shape[-1]
    return jnp.broadcast_to(row[:, None, :], (TILE, TILE, lanes)).reshape(PX, lanes) * mask[...].astype(F32)


def prepare_loss(m):
    for t, lab in enumerate((m.lab, m.lab_in)):
        codes = expand(lab[:, 0:LAB], m.mask_lab).astype(BF16)
        m.code[t * PX : (t + 1) * PX, :] = dot(codes, m.spread[...])

    @pl.when(m.role == 1)
    def _():
        for t, lab in enumerate((m.lab, m.lab_in)):
            values = expand(lab[:, LAB : LAB + TGT], m.mask_tgt)
            m.target[t * PX : (t + 1) * PX, :] = jnp.dot(
                values, m.targets[...].astype(F32), precision=lax.Precision.HIGHEST, preferred_element_type=F32
            )


def head_gradients(m, lanes):
    total = m.count_sum[0:1, :] + m.count_in[1, 0:1, :] + m.count_in[2, 0:1, :] + m.count_in[3, 0:1, :]
    scale = jnp.concatenate([1.0 / jnp.maximum(total, 1.0)] * 2, axis=1)

    def of_class(x, t, at):
        code = m.code[t * PX : (t + 1) * PX, at]
        labeled = code == m.label[0:1, at]
        y = jnp.where(labeled, -x, x)
        e = jnp.exp(-jnp.abs(y))
        more = 1.0 + e
        q = jnp.where(y >= 0, 1.0, e) / more
        softplus = jnp.maximum(y, 0.0) + jnp.log(more)
        slope = q * q * (2.0 * (1.0 - q) * softplus + q)
        return slope * (jnp.where(labeled, -0.25, jnp.where(code > 0.5, 0.75, 0.0)) * scale)

    def of_boxes(x, t, at):
        rows = slice(t * PX, (t + 1) * PX)
        g = jnp.clip((x - m.target[rows, at]) / huber_beta, -1.0, 1.0)
        return jnp.where(m.code[rows, at] > 1.5, g, 0.0) * scale

    def run(gradient):
        blocks = [(t, slice(n, n + 256)) for n in range(lanes.start, lanes.stop, 256) for t in range(2)]
        logits = [conv(m.act3, blocks[0][0], m.wh, blocks[0][1])]
        for i, (t, at) in enumerate(blocks):
            if i + 1 < len(blocks):
                logits.append(conv(m.act3, blocks[i + 1][0], m.wh, blocks[i + 1][1]))
            g = gradient(logits[i] + m.bias[4:5, at], t, at).astype(BF16)
            m.grad_bias[4:5, at] += jnp.sum(g.astype(F32), axis=0, keepdims=True)
            m.gl[t, TILE : TILE + PX, at] = g

    pl.when(m.role == 0)(lambda: run(of_class))
    if lanes.start < MAIN:
        pl.when(m.role == 1)(lambda: run(of_boxes))


def head_kernel_gradient(m, lanes, r):
    for s in range(3):
        at = (3 * r + s) * CH
        m.gh[at : at + CH, lanes] = dot(m.last_t[s], shifted_rows(m.gl, 2 - r, lanes)).astype(BF16)


def head_input_gradient(m, lanes):
    for t in range(2):
        columns = []
        for s in range(3):
            acc = None
            for r in range(3):
                at = (3 * r + s) * CH
                g = m.gl[t, TILE * (2 - r) : TILE * (2 - r) + PX, lanes]
                part = dot_nt(g, m.wh[at : at + CH, lanes])
                acc = part if acc is None else acc + part
            columns.append(acc)
        layer_upstream(m, LAYERS - 1, t, moved_left(columns[0]) + columns[1] + moved_right(columns[2]))


def input_gradient(m, l, t):
    acc = None
    for r in range(3):
        for s in range(3):
            at = (3 * r + s) * CH
            g = m.g3[l, t, TILE * (2 - r) : TILE * (2 - r) + PX, s * CH : (s + 1) * CH]
            part = dot_nt(g, m.w[l, at : at + CH, :])
            acc = part if acc is None else acc + part
    return acc


def layer_upstream(m, l, t, da):
    g = (da * m.slope[l, t * PX : (t + 1) * PX, :]).astype(BF16).astype(F32)
    m.grad_bias[l : l + 1, 0:CH] += jnp.sum(g, axis=0, keepdims=True)
    put_shifted(m.g3.at[l], t, g, -1, CH)


def layer_kernel_gradient(m, l, r):
    part = dot(m.act_t[l], shifted_rows(m.g3.at[l], 2 - r))
    for s in range(3):
        at = (3 * r + s) * CH
        m.g[l, at : at + CH, :] = part[:, s * CH : (s + 1) * CH].astype(BF16)


class Traffic:
    def __init__(self, send_sem, recv_sem):
        self.send_sem, self.recv_sem = send_sem, recv_sem
        self.names, self.used, self.sent = {}, 0, []

    def copy(self, name, src, dst, peer, span=1, offset=0):
        if name not in self.names:
            self.names[name] = self.used
            self.used += span
        i = self.names[name] + offset
        return pltpu.make_async_remote_copy(
            src, dst, self.send_sem.at[i], self.recv_sem.at[i], device_id=peer, device_id_type=MESH
        )

    def send(self, name, src, dst, peer, when=None, **at):
        copy = self.copy(name, src, dst, peer, **at)
        if when is None:
            copy.start()
        else:
            pl.when(when)(copy.start)
        self.sent.append((when, copy))

    def arrived(self, name, dst, peer, when=None, **at):
        copy = self.copy(name, dst, dst, peer, **at)
        if when is None:
            copy.wait_recv()
        else:
            pl.when(when)(copy.wait_recv)

    def finish(self):
        for when, copy in self.sent:
            if when is None:
                copy.wait_send()
            else:
                pl.when(when)(copy.wait_send)


SEMAPHORES = 224
WAYS = {
    "T0": "A", "T1": "B", "T3": "A", "T2": "B", "M0": "B", "M1": "A", "M3": "B", "M2": "A", "U0": "A", "U1": "B", "U3": "A", "U2": "B",
}
SCHEDULE = (
    "zT", "aM0", "aT0", "aU0", "aT1", "bT0", "f", "aT3", "bT1", "bM0", "zU", "aT2", "zM", "bU0", "e", "aU1", "aU3", "bT3", "bT2", "bU3", "aM1", "bU1", "aU2", "aM2", "cU0", "cT0", "y", "cT3", "cM0", "cT1", "cU3", "aM3", "cU1", "cT2", "bM1", "bU2", "F0", "bM2", "cU2", "bM3", "F1", "F2", "cM1", "dU3", "cM3", "cM2", "F3", "HM", "dU2", "dU0", "dU1", "WM0", "WM1", "HU", "X", "kM1", "kM0", "WU0", "w3", "x3", "kU0", "WU1", "k3", "w2", "kU1", "WU2", "x2", "k2", "kU2", "w1", "kU3", "x1", "p3", "Bk", "p2", "k1", "w0", "WM2", "Bp", "q2", "k0", "kM2", "kM3", "x0", "p1", "rU0", "q3", "Bq", "rU1", "rU2", "rU3", "q1", "pU0", "p0", "pM2", "pM0", "pM3", "s2", "q0", "pU3", "Bs", "pU1", "s3", "qU0", "pU2", "s1", "pM1", "D", "qM3", "qM0", "qM2", "s0", "qM1", "E", "qU3", "qU1", "qU2", "sM", "t", "sU",
)


def head_kernel(
    features_any, tower_class_any, tower_boxes_any, head_class_any, head_boxes_any,
    bias_class_any, bias_boxes_any, head_class_bias_any, head_boxes_bias_any, state_any, labels_any, targets_in_any,
    valid_any, label_any, spread_any, targets_any, mask_lab_any, mask_tgt_any,
    to_features, to_towers, to_heads, to_bias,
    out_features, out_towers, out_heads, out_bias, out_sem,
    bias_class, bias_boxes, head_class_bias, head_boxes_bias, valid, label,
    tower_class, tower_boxes, head_class, head_boxes, features, state, labels, targets_in,
    spread, targets, mask_lab, mask_tgt, bias, fetch_sem,
    own, own_h, own_v, w, wh, hp, hv, g, gh, rc, rch, sm, su, sv, r1a, r1b, r1m, r1u, r1v, r2, r2m, r2u, r2v,
    quarter, sum_m, sum_u, sum_v, rz, rzm, rzu, rzv, done, layer_in,
    act3, g3, gl, act_t, last_t, slope, spare, code, target, da,
    x, lab, lab_in, count_mine, count_sum, count_in, grad_bias, bias_in, bias_z, dx, dx_in, tile_out, features_in,
    send_sem, recv_sem,
):
    s, dp = lax.axis_index("section"), lax.axis_index("dp")
    my_y, my_x, my_z, my_c = s // 2, s % 2, dp // 2, dp % 2
    sx, sy, sg = 2 * my_y + (1 - my_x), 2 * (1 - my_y) + my_x, 2 * (1 - my_y) + (1 - my_x)
    to_x, to_y, to_g, to_c = (sx, dp), (sy, dp), (sg, dp), (s, 2 * my_z + 1 - my_c)
    plane = lambda k: (my_z + k) % PLANES
    to_z = lambda k: (s, 2 * plane(k) + my_c)
    to_pair = (s, 2 * (my_z + 1 - 2 * (my_z % 2)) + my_c)
    role = my_z % 2
    on_class, on_boxes = role == 0, role == 1
    net = Traffic(send_sem, recv_sem)
    m = SimpleNamespace(
        w=w, wh=wh, g=g, gh=gh, act3=act3, g3=g3, gl=gl, act_t=act_t, last_t=last_t, slope=slope, code=code,
        target=target, lab=lab, lab_in=lab_in, count_sum=count_sum, count_in=count_in, grad_bias=grad_bias,
        bias=bias, spread=spread, targets=targets, mask_lab=mask_lab, mask_tgt=mask_tgt, label=label, role=role,
    )

    def shard(z, c):
        return pl.ds(pl.multiple_of(ROWS * (2 * z + c), 16), ROWS)

    barrier = pltpu.get_barrier_semaphore()
    peers = (to_x, to_y, to_g, to_c, to_z(1), to_z(2), to_z(3))
    for peer in peers:
        pl.semaphore_signal(barrier, inc=1, device_id=peer, device_id_type=MESH)

    fetched = [
        pltpu.make_async_copy(src, dst, fetch_sem.at[i])
        for i, (src, dst) in enumerate(
            (
                (tower_class_any, tower_class), (tower_boxes_any, tower_boxes), (head_class_any, head_class),
                (head_boxes_any, head_boxes), (features_any, features), (state_any, state), (labels_any, labels),
                (targets_in_any, targets_in), (valid_any, valid), (mask_lab_any, mask_lab),
                (spread_any.at[role], spread), (mask_tgt_any, mask_tgt), (targets_any, targets), (label_any, label),
                (bias_class_any, bias_class), (bias_boxes_any, bias_boxes),
                (head_class_bias_any, head_class_bias), (head_boxes_bias_any, head_boxes_bias),
            )
        )
    ]
    for copy in fetched:
        copy.start()
    for copy in fetched[:4]:
        copy.wait()

    own[0] = tower_class[0].astype(BF16)
    own[1] = tower_boxes[0].astype(BF16)
    own_h[0:ROWS, :] = head_class[0:LANES, :].T.astype(BF16)
    rest, narrow = head_class.shape[0] - LANES, head_boxes.shape[0]
    spare[...] = jnp.zeros((ROWS, 2 * LANES), F32)
    spare[:, 0:rest] = head_class[LANES : LANES + rest, :].T
    spare[:, LANES : LANES + narrow] = head_boxes[...].T
    own_h[ROWS:PACK, :] = (spare[0:HALF, 0:LANES] + pltpu.roll(spare[HALF:ROWS, 0:LANES], TAIL, 1)).astype(BF16)
    own_v[...] = folded(spare[:, LANES : 2 * LANES]).astype(BF16)

    pl.semaphore_wait(barrier, len(peers))

    def kinds(kind_name):
        return ("M", "V") if kind_name == "M" else (kind_name,)

    def due(kind_name):
        return dict(T=None, M=on_class, U=on_boxes, V=on_boxes)[kind_name]

    def head_lanes(sec):
        return pl.ds(pl.multiple_of(LANES * sec, LANES), LANES)

    def place(kind_name, sec, z):
        if kind_name == "T":
            return w.at[sec, shard(z, my_c), :]
        if kind_name == "M":
            return wh.at[shard(z, my_c), head_lanes(sec)]
        if kind_name == "V":
            return hv.at[sec, z]
        return hp.at[sec, z]

    def own_shard(kind_name, which):
        if kind_name == "T":
            return own.at[which]
        if kind_name == "V":
            return own_v
        return own_h.at[pl.ds(0, ROWS) if kind_name == "M" else pl.ds(ROWS, HALF), :]

    def planes_send(kind_name):
        for k in (1, 3, 2):
            other = plane(k) % 2
            for kind in kinds(kind_name):
                when = dict(T=None, M=other == 0, U=other == 1, V=other == 1)[kind]
                net.send(("z", kind, k), own_shard(kind, other), place(kind, s, my_z), to_z(k), when)

    in_plane = (("x", to_x, sx), ("y", to_y, sy), ("g", to_g, sg))

    def rows_of(sec):
        return pl.ds(pl.multiple_of(64 * sec, 64), 64)

    def features_send():
        for copy in fetched[4:9]:
            copy.wait()
        row = lax.broadcasted_iota(jnp.int32, (TILE, TILE * A), 0)
        found = jnp.zeros((TILE, TILE * A), F32)
        for t in range(SECTIONS):
            found += jnp.where(jnp.logical_and(state[t] == 1, row < valid[t]), 1.0, 0.0)
        count_mine[...] = jnp.full((8, LANES), jnp.sum(found), F32)
        inside = row < valid[s]
        kind = state[s]
        lab[...] = jnp.zeros_like(lab)
        lab[:, 0 : TILE * A] = jnp.where(
            inside,
            jnp.where(kind == 1, labels[s].astype(F32) + 2.0, jnp.where(kind == 2, 0.0, 1.0)),
            0.0,
        )
        lab[:, LAB : LAB + targets_in.shape[2]] = targets_in[s]
        for name, peer, sec in in_plane:
            net.send(("f", name), features.at[sec], x.at[0, rows_of(s), :], peer)
        net.send("count c", count_mine, count_in.at[0], to_c)
        net.send("lab", lab, lab_in, to_pair)

    def piece(kind_name, sec, j):
        return place(kind_name, sec, (my_z + PLANES - j) % PLANES)

    def ways(kind_name, j):
        if WAYS[kind_name.replace("V", "M") + str(j)] == "A":
            return (to_x, sx), (to_y, sy)
        return (to_y, sy), (to_x, sx)

    def gather_mine(kind_name, j):
        for kind in kinds(kind_name):
            mine = piece(kind, s, j)
            if j:
                net.arrived(("z", kind, j), mine, to_z(PLANES - j), due(kind))
            for (n, _), name in zip(ways(kind, j), ("g1", "g2")):
                net.send((name, kind, j), mine, mine, n, due(kind))
        if kind_name == "T":
            net.send(("swap", "T", j, 0), mine, mine, to_c)

    def gather_pass(kind_name, j):
        (n1, s1), (n2, s2) = ways(kind_name, j)
        for kind in kinds(kind_name):
            first = piece(kind, s1, j)
            net.arrived(("g1", kind, j), first, n1, due(kind))
            net.send(("g3", kind, j), first, first, n2, due(kind))
        if kind_name == "T":
            net.send(("swap", "T", j, 1), first, first, to_c)

    def gather_last(kind_name, j):
        (n1, s1), (n2, s2) = ways(kind_name, j)
        for i, (name, sec) in enumerate((("g2", s2), ("g3", sg))):
            for kind in kinds(kind_name):
                got = piece(kind, sec, j)
                net.arrived((name, kind, j), got, n2, due(kind))
            if kind_name == "T":
                net.send(("swap", "T", j, 2 + i), got, got, to_c)
        z = (my_z + PLANES - j) % PLANES
        at = pl.multiple_of(ROWS * (2 * z + my_c), 16)
        if kind_name == "M":

            @pl.when(on_boxes)
            def _():
                for sec in range(SECTIONS):
                    for i, part in enumerate(unfolded(hv[sec, z])):
                        rows = pl.ds(at + i * FOLD_ROWS, FOLD_ROWS)
                        wh[rows, sec * LANES : (sec + 1) * LANES] = part.astype(BF16)

            block = wh.at[pl.ds(at, ROWS), 0:MAIN]
            net.send(("swap", "M", j), block, block, to_c)
        if kind_name == "U":

            @pl.when(on_boxes)
            def _():
                for q in range(2):
                    lanes = slice((SECTIONS + q) * LANES, (SECTIONS + q + 1) * LANES)
                    top, bottom = swap_halves(hp[2 * q, z], hp[2 * q + 1, z])
                    wh[pl.ds(at, HALF), lanes] = top.astype(BF16)
                    wh[pl.ds(at + HALF, HALF), lanes] = bottom.astype(BF16)

            block = wh.at[pl.ds(at, ROWS), MAIN:HEAD]
            net.send(("up", j), block, block, to_pair, on_boxes)

    def relayed_plane(j):
        return (my_z + 1 + PLANES - j) % PLANES

    def gather_relayed(kind_name, j):
        block = wh.at[shard(relayed_plane(j), my_c), MAIN:HEAD]
        net.arrived(("up", j), block, to_pair, on_class)
        net.send(("swap", "U", j), block, block, to_c, on_class)

    def swapped(kind_name, j):
        z = (my_z + PLANES - j) % PLANES
        if kind_name == "M":
            net.arrived(("swap", "M", j), wh.at[shard(z, 1 - my_c), 0:MAIN], to_c)
            return
        if kind_name == "U":
            net.arrived(("swap", "U", j), wh.at[shard(relayed_plane(j), 1 - my_c), MAIN:HEAD], to_c, on_class)
            return
        (_, s1), (_, s2) = ways(kind_name, j)
        for i, sec in enumerate((s, s1, s2, sg)):
            net.arrived(("swap", "T", j, i), w.at[sec, shard(z, 1 - my_c), :], to_c)

    def features_tile():
        x[0, rows_of(s), :] = features[s]
        for name, peer, sec in in_plane:
            net.arrived(("f", name), x.at[0, rows_of(sec), :], peer)
        net.send("tile", x.at[0], x.at[1], to_pair)
        net.arrived("count c", count_in.at[0], to_c)
        count_sum[...] = count_mine[...] + count_in[0]
        for k in (1, 2, 3):
            net.send(("count", k), count_sum, count_in.at[k], to_z(k))

    def prepare():
        for ref in (act3, *(g3.at[l] for l in range(LAYERS)), gl):
            for t in range(2):
                ref[t, 0:TILE, :] = jnp.zeros((TILE, ref.shape[2]), BF16)
                ref[t, TILE + PX : 2 * TILE + PX, :] = jnp.zeros((TILE, ref.shape[2]), BF16)
        grad_bias[...] = jnp.zeros_like(grad_bias)
        for copy in fetched[9:]:
            copy.wait()
        bias[0:LAYERS, 0:CH] = jnp.where(role == 0, bias_class[...], bias_boxes[...])
        bias[4:5, :] = jnp.where(role == 0, lay(head_class_bias[...]), lay(head_boxes_bias[...]))
        net.arrived("lab", lab_in, to_pair)
        prepare_loss(m)
        net.arrived("tile", x.at[1], to_pair)
        for t in range(2):
            v = x[t].astype(F32)
            put_shifted(act3, t, v, 1, CH)
            act_t[0, :, t * PX : (t + 1) * PX] = v.T.astype(BF16)

    def forward(l):
        if l == 0:
            for j in range(PLANES):
                swapped("T", j)
        forward_layer(m, l)

    def head(kind_name):
        if kind_name == "M":
            for k in (1, 2, 3):
                net.arrived(("count", k), count_in.at[k], to_z(PLANES - k))
        for j in range(PLANES):
            swapped(kind_name, j)
        head_gradients(m, head_part[kind_name])

    head_part = dict(M=slice(0, MAIN), U=slice(MAIN, HEAD))
    w[s, shard(my_z, my_c), :] = own[role]
    hp[s, my_z] = own_h[ROWS:PACK, :]
    hv[s, my_z] = own_v[...]

    @pl.when(on_class)
    def _():
        wh[shard(my_z, my_c), head_lanes(s)] = own_h[0:ROWS, :]


    def added(a, b):
        return a + b

    def half_rows(which):
        return pl.ds(pl.multiple_of(HALF * which, 16), HALF)

    def half_lanes(which):
        return pl.ds(pl.multiple_of(LANES * which, LANES), LANES)

    def core_send(l, zp):
        theirs = shard(zp, 1 - my_c)
        if l in head_part:
            when = on_class if l == "U" else None
            net.send(("rc", l, zp), gh.at[theirs, head_part[l]], rch.at[zp, :, head_part[l]], to_c, when)
        else:
            net.send(("rc", l, zp), g.at[l, theirs, :], rc.at[l, zp], to_c)

    first, second = pl.ds(0, 2), pl.ds(2, 2)

    def tower_cores(l):
        for zp in range(PLANES):
            net.arrived(("rc", l, zp), rc.at[l, zp], to_c)
            rc[l, zp] = added(rc[l, zp], g[l, shard(zp, my_c), :])
            if zp == 1:
                net.send(("r1a", l), rc.at[l, first, :, half_lanes(1 - my_x)], r1a.at[l], to_x)
        net.send(("r1b", l), rc.at[l, second, half_rows(1 - my_y), :], r1b.at[l], to_y)

    def tower_plane(l):
        net.arrived(("r1a", l), r1a.at[l], to_x)
        for zp in (0, 1):
            rc[l, zp, :, half_lanes(my_x)] = added(rc[l, zp, :, half_lanes(my_x)], r1a[l, zp])
        net.send(("r2a", l), rc.at[l, first, half_rows(1 - my_y), half_lanes(my_x)], r2.at[l, first], to_y)
        net.arrived(("r1b", l), r1b.at[l], to_y)
        for zp in (2, 3):
            rc[l, zp, half_rows(my_y), :] = added(rc[l, zp, half_rows(my_y), :], r1b[l, zp - 2])
        net.send(("r2b", l), rc.at[l, second, half_rows(my_y), half_lanes(1 - my_x)], r2.at[l, second], to_x)

    def to_planes(name, src, dst):
        for zp in range(PLANES):
            k = (zp + PLANES - my_z) % PLANES
            net.send(name, src.at[zp], dst.at[my_z], (s, 2 * zp + my_c), my_z != zp, span=PLANES, offset=k)

    def tower_planes(l):
        net.arrived(("r2a", l), r2.at[l, first], to_y)
        net.arrived(("r2b", l), r2.at[l, second], to_x)
        for zp in range(PLANES):
            quarter[l, zp] = added(rc[l, zp, half_rows(my_y), half_lanes(my_x)], r2[l, zp])
        to_planes(("rz", l), quarter.at[l], rz.at[l])

    def from_planes(name, mine, others):
        for k in (1, 2, 3):
            net.arrived(name, others.at[plane(PLANES - k)], to_z(PLANES - k), span=PLANES, offset=k)
        same = mine[my_z].astype(F32) + others[plane(2)].astype(F32)
        return same, others[plane(1)].astype(F32) + others[plane(3)].astype(F32)

    def tower_sum(l):
        same, other = from_planes(("rz", l), quarter.at[l], rz.at[l])
        done[l, role] = same.astype(BF16)
        done[l, 1 - role] = other.astype(BF16)
        to_l = (l, dp)
        net.send("layer", done.at[l], layer_in.at[s], to_l, s != l, span=SECTIONS, offset=s)

        @pl.when(s == l)
        def _():
            out_towers[role, half_rows(my_y), half_lanes(my_x)] = same
            out_towers[1 - role, half_rows(my_y), half_lanes(my_x)] = other

    def tower_store():
        for sec, peer in ((sx, to_x), (sy, to_y), (sg, to_g)):
            net.arrived("layer", layer_in.at[sec], peer, span=SECTIONS, offset=sec)
            for i in range(2):
                out_towers[i, half_rows(sec // 2), half_lanes(sec % 2)] = layer_in[sec, i].astype(F32)
        give(out_towers, to_towers)

    def head_refs(kind):
        return dict(
            M=(sm, r1m, r2m, sum_m, rzm), U=(su, r1u, r2u, sum_u, rzu), V=(sv, r1v, r2v, sum_v, rzv)
        )[kind]

    def both_cores(zp, rows, lanes):
        at = pl.multiple_of(ROWS * (2 * zp + my_c) + rows[0], 16)
        mine = gh[pl.ds(at, rows[1]), lanes]
        return rch[zp, rows[0] : rows[0] + rows[1], lanes].astype(F32) + mine.astype(F32)

    def head_cores(kind_name, zp):
        landed = rch.at[zp, :, head_part[kind_name]]
        if kind_name == "M":
            net.arrived(("rc", "M", zp), landed, to_c)

            def store(kind):
                for sec in range(SECTIONS):
                    v = both_cores(zp, (0, ROWS), slice(sec * LANES, (sec + 1) * LANES))
                    v = v if kind == "M" else folded(v)
                    head_refs(kind)[0][sec // 2, sec % 2, zp] = v.astype(BF16)

            for kind in kinds("M"):
                pl.when(due(kind))(functools.partial(store, kind))
            head_first_send("M", zp)
            return
        net.arrived(("rc", "U", zp), landed, to_c, on_class)

        @pl.when(on_class)
        def _():
            for q in range(2):
                lanes = slice((SECTIONS + q) * LANES, (SECTIONS + q + 1) * LANES)
                left, right = swap_halves(both_cores(zp, (0, HALF), lanes), both_cores(zp, (HALF, HALF), lanes))
                su[q, 0, zp] = left.astype(BF16)
                su[q, 1, zp] = right.astype(BF16)

        block = su.at[:, :, zp]
        net.send(("ru", zp), block, block, to_pair, on_class)

    def head_relayed(kind_name, zp):
        net.arrived(("ru", zp), su.at[:, :, zp], to_pair, on_boxes)
        head_first_send(kind_name, zp)

    def head_first_send(kind_name, zp):
        for kind in kinds(kind_name):
            into, landing = head_refs(kind)[:2]
            if zp % 2 == 0:
                net.send(("h1", kind, zp), into.at[:, 1 - my_x, zp], landing.at[zp], to_x, due(kind))
            else:
                net.send(("h1", kind, zp), into.at[1 - my_y, :, zp], landing.at[zp], to_y, due(kind))

    def head_plane(kind_name, zp):
        for kind in kinds(kind_name):
            into, landing, landing2 = head_refs(kind)[:3]
            net.arrived(("h1", kind, zp), landing.at[zp], to_x if zp % 2 == 0 else to_y, due(kind))

            @pl.when(due(kind))
            def _():
                for i in range(2):
                    at = (i, my_x, zp) if zp % 2 == 0 else (my_y, i, zp)
                    into[at] = added(into[at], landing[zp, i])

            if zp % 2 == 0:
                net.send(("h2", kind, zp), into.at[1 - my_y, my_x, zp], landing2.at[zp], to_y, due(kind))
            else:
                net.send(("h2", kind, zp), into.at[my_y, 1 - my_x, zp], landing2.at[zp], to_x, due(kind))

    def head_planes(kind_name, zp):
        k = (zp + PLANES - my_z) % PLANES
        for kind in kinds(kind_name):
            into, _, landing2, total, others = head_refs(kind)
            net.arrived(("h2", kind, zp), landing2.at[zp], to_y if zp % 2 == 0 else to_x, due(kind))

            @pl.when(due(kind))
            def _():
                total[zp] = added(into[my_y, my_x, zp], landing2[zp])

            away = jnp.logical_and(due(kind), my_z != zp)
            to_zp = (s, 2 * zp + my_c)
            net.send(("hz", kind), total.at[zp], others.at[my_z], to_zp, away, span=PLANES, offset=k)

    def head_store(kind_name):
        for kind in kinds(kind_name):
            total, others = head_refs(kind)[3:]
            here = due(kind)
            for k in (1, 2, 3):
                when = here if k == 2 else jnp.logical_not(here)
                source = others.at[plane(PLANES - k)]
                net.arrived(("hz", kind), source, to_z(PLANES - k), when, span=PLANES, offset=k)

            def store(v):
                if kind == "M":
                    out_heads[0, 0:ROWS] = v
                elif kind == "U":
                    out_heads[0, ROWS:PACK] = v
                else:
                    for i, part in enumerate(unfolded(v)):
                        out_heads[1, i * FOLD_ROWS : (i + 1) * FOLD_ROWS] = part

            @pl.when(here)
            def _():
                store(total[my_z].astype(F32) + others[plane(2)].astype(F32))

            @pl.when(jnp.logical_not(here))
            def _():
                store(others[plane(1)].astype(F32) + others[plane(3)].astype(F32))

        if kind_name == "U":
            out_heads[1, ROWS:PACK] = jnp.zeros((HALF, LANES), F32)
        rows = pl.ds(0, ROWS) if kind_name == "M" else pl.ds(ROWS, HALF)
        give(out_heads.at[:, rows], to_heads.at[:, rows])

    def bias_cores():
        net.arrived("bias c", bias_in.at[0], to_c)
        bias_z[0] = grad_bias[...] + bias_in[0]
        net.send("bias x", bias_z.at[0], bias_in.at[1], to_x)

    def bias_plane():
        net.arrived("bias x", bias_in.at[1], to_x)
        bias_z[1] = bias_z[0] + bias_in[1]
        net.send("bias y", bias_z.at[1], bias_in.at[2], to_y)

    def bias_planes():
        net.arrived("bias y", bias_in.at[2], to_y)
        bias_z[2] = bias_z[1] + bias_in[2]
        for k in (1, 2, 3):
            net.send(("bias z", k), bias_z.at[2], bias_in.at[2 + k], to_z(k))

    def bias_store():
        for k in (1, 2, 3):
            net.arrived(("bias z", k), bias_in.at[2 + k], to_z(PLANES - k))
        out_bias[role] = bias_z[2] + bias_in[4]
        out_bias[1 - role] = bias_in[3] + bias_in[5]
        give(out_bias, to_bias)

    results = []

    def give(src, dst):
        copy = pltpu.make_async_copy(src, dst, out_sem.at[len(results)])
        copy.start()
        results.append(copy)

    def features_sum():
        net.arrived("dx", dx_in, to_pair)
        tile_out[...] = (da[...] + dx_in[...].astype(F32)).astype(BF16)
        for name, peer, sec in in_plane:
            net.send(("b", name), tile_out.at[rows_of(sec), :], features_in.at[s], peer)

    def features_store():
        for name, peer, sec in in_plane:
            net.arrived(("b", name), features_in.at[sec], peer)
            out_features[sec] = features_in[sec]
        out_features[s] = tile_out[rows_of(s), :]
        give(out_features, to_features)

    def head_gradient(kind_name, r):
        if kind_name == "M":
            head_kernel_gradient(m, head_part["M"], r)
        else:
            pl.when(on_class)(lambda: head_kernel_gradient(m, head_part["U"], r))
        for zp in ((0,), (1,), (2, 3))[r]:
            core_send(kind_name, zp)

    def head_input():
        pl.when(on_class)(lambda: head_input_gradient(m, slice(0, HEAD)))
        pl.when(on_boxes)(lambda: head_input_gradient(m, slice(0, MAIN)))

    def layer_gradient(l):
        for r in range(3):
            layer_kernel_gradient(m, l, r)
        for zp in range(PLANES):
            core_send(l, zp)

    def layer_input(l):
        for t in range(2):
            v = input_gradient(m, l, t)
            if l:
                layer_upstream(m, l - 1, t, v)
            elif t == 0:
                da[...] = v
            else:
                dx[...] = v.astype(BF16)
        if l == 0:
            net.send("dx", dx, dx_in, to_pair)
        if l == 1:
            net.send("bias c", grad_bias, bias_in.at[0], to_c)

    def either(of_head, of_tower):
        return lambda *which: of_head(*which) if which[0] in head_part else of_tower(*which)

    steps = dict(
        d=gather_relayed, r=head_relayed, z=planes_send, f=features_send, e=features_tile, y=prepare, a=gather_mine, b=gather_pass, c=gather_last,
        F=forward, H=head, W=head_gradient, X=head_input, w=layer_gradient, x=layer_input,
        k=either(head_cores, tower_cores), p=either(head_plane, tower_plane), q=either(head_planes, tower_planes),
        s=either(head_store, tower_sum), t=tower_store, D=features_sum, E=features_store,
        B=lambda which: dict(k=bias_cores, p=bias_plane, q=bias_planes, s=bias_store)[which](),
    )
    for step in SCHEDULE:
        steps[step[0]](*(int(v) if v.isdigit() else v for v in step[1:]))
    for copy in results:
        copy.wait()
    net.finish()


def lay(vector):
    width = vector.shape[0]
    per = width // SECTIONS
    row = jnp.concatenate([vector.reshape(1, width), jnp.zeros((1, HEAD - width), F32)], axis=1)
    row = jnp.broadcast_to(row, (8, HEAD))
    lane = lax.broadcasted_iota(jnp.int32, (8, LANES), 1)
    main, tails = [], []
    for s in range(SECTIONS):
        turned = pltpu.roll(row, (HEAD - s * per) % HEAD, 1)
        main.append(jnp.where(lane < per, turned[:, 0:LANES], 0.0))
        tails.append(jnp.where(lane < per - LANES, turned[:, LANES : 2 * LANES], 0.0))
    folded = [tails[2 * q] + pltpu.roll(tails[2 * q + 1], TAIL, 1) for q in range(2)]
    return jnp.concatenate(main + folded, axis=1)[0:1, :]


def unlay(row, width):
    per = width // SECTIONS
    row = jnp.broadcast_to(row, (8, HEAD))
    lane = lax.broadcasted_iota(jnp.int32, (8, LANES), 1)
    total = jnp.zeros((8, HEAD), F32)
    for s in range(SECTIONS):
        tail = row[:, MAIN + (s // 2) * LANES : MAIN + (s // 2 + 1) * LANES]
        tail = pltpu.roll(tail, TAIL, 1) if s % 2 else tail
        parts = [jnp.where(lane < per, row[:, s * LANES : (s + 1) * LANES], 0.0), jnp.where(lane < per - LANES, tail, 0.0)]
        total += pltpu.roll(jnp.concatenate(parts + [jnp.zeros((8, HEAD - 2 * LANES), F32)], axis=1), s * per, 1)
    return total[0:1, 0:width].reshape(width)


def finish_kernel(
    features, towers, heads, sums,
    out_features, out_class, out_bias_class, out_boxes, out_bias_boxes, out_head_class, out_head_class_bias,
    out_head_boxes, out_head_boxes_bias,
):
    out_features[...] = features[...]
    for i, (tower, bias, head, head_bias) in enumerate(
        (
            (out_class, out_bias_class, out_head_class, out_head_class_bias),
            (out_boxes, out_bias_boxes, out_head_boxes, out_head_boxes_bias),
        )
    ):
        tower[0] = towers[i]
        bias[...] = sums[i, 0:LAYERS, 0:CH]
        width = head.shape[0]
        main, rest = min(width, LANES), max(0, width - LANES)
        head[0:main, :] = heads[i, 0:ROWS, :].T[0:main, :]
        if rest:
            low = heads[i, ROWS:PACK, :]
            both = jnp.concatenate([low, pltpu.roll(low, TAIL, 1)], axis=0)
            head[LANES:width, :] = both.T[0:rest, :]
        head_bias[...] = unlay(sums[i, LAYERS : LAYERS + 1, :], head_bias.shape[0])


def fast(features, tower_class, bias_class, tower_boxes, bias_boxes, head_class, head_class_bias, head_boxes,
         head_boxes_bias, anchor_state, class_labels, box_targets, valid_rows):
    class_width, boxes_width = head_class_bias.shape[0], head_boxes_bias.shape[0]
    spread, targets, mask_lab, mask_tgt, label = constants(class_width, boxes_width)
    tiles = features.shape[0]
    vmem = pl.BlockSpec(memory_space=pltpu.VMEM)
    v = lambda shape, dtype: pltpu.VMEM(shape, dtype)
    out = lambda shape, dtype: jax.ShapeDtypeStruct(shape, dtype)
    anywhere = pl.BlockSpec(memory_space=pl.ANY)
    raw = pl.pallas_call(
        head_kernel,
        out_shape=(
            out((tiles, 64, CH), BF16),
            out((2, ROWS, CH), F32),
            out((2, PACK, LANES), F32),
            out((2, 8, HEAD), F32),
        ),
        in_specs=[anywhere] * 18,
        out_specs=(anywhere,) * 4,
        scratch_shapes=[
            v((tiles, 64, CH), BF16),
            v((2, ROWS, CH), F32),
            v((2, PACK, LANES), F32),
            v((2, 8, HEAD), F32),
            pltpu.SemaphoreType.DMA((5,)),
            v(bias_class.shape, F32),
            v(bias_boxes.shape, F32),
            v(head_class_bias.shape, F32),
            v(head_boxes_bias.shape, F32),
            pltpu.SMEM(valid_rows.shape, jnp.int32),
            v(label.shape, F32),
            v(tower_class.shape, F32),
            v(tower_boxes.shape, F32),
            v(head_class.shape[::-1], F32),
            v(head_boxes.shape[::-1], F32),
            v((tiles, 64, CH), BF16),
            v(anchor_state.shape, jnp.int32),
            v(class_labels.shape, jnp.int32),
            v(box_targets.shape, F32),
            v(spread.shape[1:], BF16),
            v(targets.shape, BF16),
            v(mask_lab.shape, BF16),
            v(mask_tgt.shape, BF16),
            v((8, HEAD), F32),
            pltpu.SemaphoreType.DMA((18,)),
            v((2, ROWS, CH), BF16),
            v((PACK, LANES), BF16),
            v((FOLD_ROWS, LANES), BF16),
            v((LAYERS, DEEP, CH), BF16),
            v((DEEP, HEAD), BF16),
            v((SECTIONS, PLANES, HALF, LANES), BF16),
            v((SECTIONS, PLANES, FOLD_ROWS, LANES), BF16),
            v((LAYERS, DEEP, CH), BF16),
            v((DEEP, HEAD), BF16),
            v((LAYERS, PLANES, ROWS, CH), BF16),
            v((PLANES, ROWS, HEAD), BF16),
            v((2, 2, PLANES, ROWS, LANES), BF16),
            v((2, 2, PLANES, HALF, LANES), BF16),
            v((2, 2, PLANES, FOLD_ROWS, LANES), BF16),
            v((LAYERS, 2, ROWS, LANES), BF16),
            v((LAYERS, 2, HALF, CH), BF16),
            v((PLANES, 2, ROWS, LANES), BF16),
            v((PLANES, 2, HALF, LANES), BF16),
            v((PLANES, 2, FOLD_ROWS, LANES), BF16),
            v((LAYERS, PLANES, HALF, LANES), BF16),
            v((PLANES, ROWS, LANES), BF16),
            v((PLANES, HALF, LANES), BF16),
            v((PLANES, FOLD_ROWS, LANES), BF16),
            v((LAYERS, PLANES, HALF, LANES), BF16),
            v((PLANES, ROWS, LANES), BF16),
            v((PLANES, HALF, LANES), BF16),
            v((PLANES, FOLD_ROWS, LANES), BF16),
            v((LAYERS, PLANES, HALF, LANES), BF16),
            v((PLANES, ROWS, LANES), BF16),
            v((PLANES, HALF, LANES), BF16),
            v((PLANES, FOLD_ROWS, LANES), BF16),
            v((LAYERS, 2, HALF, LANES), BF16),
            v((SECTIONS, 2, HALF, LANES), BF16),
            v((2, PX + 2 * TILE, 3 * CH), BF16),
            v((LAYERS, 2, PX + 2 * TILE, 3 * CH), BF16),
            v((2, PX + 2 * TILE, HEAD), BF16),
            v((LAYERS, CH, 2 * PX), BF16),
            v((3, CH, 2 * PX), BF16),
            v((LAYERS, 2 * PX, CH), F32),
            v((ROWS, 2 * LANES), F32),
            v((2 * PX, HEAD), F32),
            v((2 * PX, MAIN), F32),
            v((PX, CH), F32),
            v((2, PX, CH), BF16),
            v((TILE, LAB + TGT), F32),
            v((TILE, LAB + TGT), F32),
            v((8, LANES), F32),
            v((8, LANES), F32),
            v((4, 8, LANES), F32),
            v((8, HEAD), F32),
            v((6, 8, HEAD), F32),
            v((3, 8, HEAD), F32),
            v((PX, CH), BF16),
            v((PX, CH), BF16),
            v((PX, CH), BF16),
            v((SECTIONS, 64, CH), BF16),
            pltpu.SemaphoreType.DMA((SEMAPHORES,)),
            pltpu.SemaphoreType.DMA((SEMAPHORES,)),
        ],
        compiler_params=pltpu.CompilerParams(
            collective_id=0, has_side_effects=True, vmem_limit_bytes=62 * 2**20
        ),
    )(
        features.reshape(tiles, 64, CH), tower_class, tower_boxes, head_class.T, head_boxes.T, bias_class, bias_boxes,
        head_class_bias, head_boxes_bias, anchor_state, class_labels, box_targets, valid_rows, label,
        spread, targets, mask_lab, mask_tgt,
    )
    results = pl.pallas_call(
        finish_kernel,
        out_shape=(
            out((tiles, 64, CH), BF16),
            out(tower_class.shape, F32),
            out(bias_class.shape, F32),
            out(tower_boxes.shape, F32),
            out(bias_boxes.shape, F32),
            out(head_class.shape[::-1], F32),
            out(head_class_bias.shape, F32),
            out(head_boxes.shape[::-1], F32),
            out(head_boxes_bias.shape, F32),
        ),
        in_specs=[vmem] * 4,
        out_specs=(vmem,) * 9,
    )(*raw)
    of_features, of_class, of_bias_class, of_boxes, of_bias_boxes, of_head_class, *rest = results
    of_head_class_bias, of_head_boxes, of_head_boxes_bias = rest
    return (
        of_features.reshape(features.shape), of_class, of_bias_class, of_boxes, of_bias_boxes,
        of_head_class.T, of_head_class_bias, of_head_boxes.T, of_head_boxes_bias,
    )


def shifted(block, axis, distance):
    devices = range(lax.axis_size(axis))
    route = [(i - distance, i) for i in devices if i - distance in devices]
    return lax.ppermute(block, axis, route)


def anchor_masks(anchor_state, valid_rows):
    tile_count = anchor_state.shape[0]
    anchor_kind = anchor_state.reshape(tile_count, TILE, TILE, A)
    row_index = lax.broadcasted_iota(jnp.int32, (tile_count, TILE, 1, 1), 1)
    inside = row_index < valid_rows.reshape(tile_count, 1, 1, 1)
    positive = jnp.logical_and(anchor_kind == 1, inside).astype(jnp.float32)
    counted = jnp.logical_and(anchor_kind != 2, inside).astype(jnp.float32)
    return (positive, counted)


def head_loss(logits, box_values, positive, counted, class_labels, box_targets, normalizer):
    tile_count = logits.shape[0]
    scores = logits.reshape(tile_count, TILE, TILE, A, K)
    labels = class_labels.reshape(tile_count, TILE, TILE, A, 1)
    classes = lax.broadcasted_iota(jnp.int32, (1, 1, 1, 1, K), 4)
    target = (labels == classes).astype(jnp.float32) * positive[..., None]
    chance = jax.nn.sigmoid(scores)
    entropy = jax.nn.softplus(scores) - target * scores
    agreement = chance * target + (1.0 - chance) * (1.0 - target)
    balance = 0.25 * target + 0.75 * (1.0 - target)
    focal_terms = balance * (1.0 - agreement) ** 2 * entropy
    focal_sum = jnp.sum(focal_terms * counted[..., None])
    offsets = box_values.reshape(tile_count, TILE, TILE, A, 4) - box_targets.reshape(
        tile_count, TILE, TILE, A, 4
    )
    spread = jnp.abs(offsets)
    huber_terms = jnp.where(
        spread < huber_beta, 0.5 * offsets * offsets / huber_beta, spread - 0.5 * huber_beta
    )
    box_sum = jnp.sum(huber_terms * positive[..., None])
    return (focal_sum + box_sum) / normalizer


def unfold(values):
    tile_count, tile_side, channels = (values.shape[0], values.shape[1], values.shape[3])
    padded = jnp.pad(values, ((0, 0), (1, 1), (1, 1), (0, 0)))
    pieces = [
        padded[:, row_shift : row_shift + tile_side, col_shift : col_shift + tile_side, :]
        for row_shift in range(3)
        for col_shift in range(3)
    ]
    return jnp.concatenate(pieces, axis=-1).reshape(
        tile_count * tile_side * tile_side, 9 * channels
    )


def fold_back(columns, tile_count, tile_side, channels):
    shaped = columns.reshape(tile_count, tile_side, tile_side, 9 * channels)
    padded = jnp.zeros((tile_count, tile_side + 2, tile_side + 2, channels), jnp.float32)
    for tap_index in range(9):
        row_shift = tap_index // 3
        col_shift = tap_index % 3
        padded = padded.at[
            :, row_shift : row_shift + tile_side, col_shift : col_shift + tile_side, :
        ].add(shaped[..., tap_index * channels : (tap_index + 1) * channels])
    return padded[:, 1 : tile_side + 1, 1 : tile_side + 1, :]


def weight_grad(columns, upstream):
    return jnp.einsum("pk,pc->kc", columns, upstream, preferred_element_type=jnp.float32)


def input_cols(upstream, weight):
    return jnp.einsum("pc,kc->pk", upstream, weight, preferred_element_type=jnp.float32)


def pick(buffer, slot_index):
    return lax.dynamic_index_in_dim(buffer, slot_index, 0, keepdims=False)


def store(buffer, update, slot_index, active):
    return lax.dynamic_update_index_in_dim(
        buffer, jnp.where(active, update, pick(buffer, slot_index)), slot_index, 0
    )


def per_device(
    features,
    tower_class,
    bias_class,
    tower_boxes,
    bias_boxes,
    head_class,
    head_class_bias,
    head_boxes,
    head_boxes_bias,
    anchor_state,
    class_labels,
    box_targets,
    valid_rows,
):
    section_count = lax.axis_size("section")
    section_index = lax.axis_index("section")
    final_section = section_count - 1
    is_first = section_index == 0
    is_final = section_index == final_section
    tile_dev = features.shape[0]
    per_micro = tile_dev // MICRO
    whole = lax.all_gather(features, "section", axis=1, tiled=True)
    tile_side = whole.shape[1]
    channels = whole.shape[3]
    pixels = per_micro * tile_side * tile_side
    act_shape = (per_micro, tile_side, tile_side, channels)
    positive, counted = anchor_masks(anchor_state, valid_rows)
    found = lax.psum(jnp.sum(positive), "dp")
    normalizer = jnp.maximum(found, 1.0)
    gathered = (
        lax.all_gather(tower_class.astype(jnp.bfloat16), "dp", axis=1, tiled=True),
        lax.all_gather(tower_boxes.astype(jnp.bfloat16), "dp", axis=1, tiled=True),
        lax.all_gather(head_class.astype(jnp.bfloat16), "dp", axis=0, tiled=True),
        lax.all_gather(head_boxes.astype(jnp.bfloat16), "dp", axis=0, tiled=True),
    )
    weight_class = gathered[0][0]
    weight_boxes = gathered[1][0]
    head_weight_class, head_weight_boxes = (
        lax.all_gather(gathered[2], "section", axis=1, tiled=True),
        lax.all_gather(gathered[3], "section", axis=1, tiled=True),
    )
    layer_bias_class = lax.dynamic_index_in_dim(bias_class, section_index, 0, keepdims=False)
    layer_bias_boxes = lax.dynamic_index_in_dim(bias_boxes, section_index, 0, keepdims=False)
    class_width = head_weight_class.shape[1]
    boxes_width = head_weight_boxes.shape[1]
    patch_width = head_weight_class.shape[0]

    def head_pass(stored_class, stored_boxes, slot_index):
        cols_class = unfold(stored_class)
        cols_boxes = unfold(stored_boxes)
        logits = (
            jnp.dot(cols_class, head_weight_class, preferred_element_type=jnp.float32)
            + head_class_bias
        )
        box_values = (
            jnp.dot(cols_boxes, head_weight_boxes, preferred_element_type=jnp.float32)
            + head_boxes_bias
        )
        start = slot_index * per_micro
        pos_here = lax.dynamic_slice_in_dim(positive, start, per_micro, 0)
        counted_here = lax.dynamic_slice_in_dim(counted, start, per_micro, 0)
        labels_here = lax.dynamic_slice_in_dim(class_labels, start, per_micro, 0)
        targets_here = lax.dynamic_slice_in_dim(box_targets, start, per_micro, 0)

        def local_loss(logit_part, box_part):
            return head_loss(
                logit_part.reshape(per_micro, tile_side, tile_side, class_width),
                box_part.reshape(per_micro, tile_side, tile_side, boxes_width),
                pos_here,
                counted_here,
                labels_here,
                targets_here,
                normalizer,
            )

        total_loss, pullback = jax.vjp(local_loss, logits, box_values)
        grad_logits, grad_box = pullback(jnp.ones_like(total_loss))
        grad_logits = grad_logits.astype(jnp.bfloat16)
        grad_box = grad_box.astype(jnp.bfloat16)
        back_class = fold_back(
            input_cols(grad_logits, head_weight_class), per_micro, tile_side, channels
        )
        back_boxes = fold_back(
            input_cols(grad_box, head_weight_boxes), per_micro, tile_side, channels
        )
        return (
            weight_grad(cols_class, grad_logits),
            weight_grad(cols_boxes, grad_box),
            jnp.sum(grad_logits.astype(jnp.float32), 0),
            jnp.sum(grad_box.astype(jnp.float32), 0),
            back_class,
            back_boxes,
        )

    def head_spare(stored_class, stored_boxes, slot_index):
        return (
            jnp.zeros((patch_width, class_width), jnp.float32),
            jnp.zeros((patch_width, boxes_width), jnp.float32),
            jnp.zeros((class_width,), jnp.float32),
            jnp.zeros((boxes_width,), jnp.float32),
            jnp.zeros(act_shape, jnp.float32),
            jnp.zeros(act_shape, jnp.float32),
        )

    kept_class = jnp.zeros((MICRO,) + act_shape, jnp.bfloat16)
    kept_boxes = jnp.zeros((MICRO,) + act_shape, jnp.bfloat16)
    kept_pre_class = jnp.zeros((MICRO, pixels, channels), jnp.float32)
    kept_pre_boxes = jnp.zeros((MICRO, pixels, channels), jnp.float32)
    head_back_class = jnp.zeros((MICRO,) + act_shape, jnp.float32)
    head_back_boxes = jnp.zeros((MICRO,) + act_shape, jnp.float32)
    grad_head_class = jnp.zeros((patch_width, class_width), jnp.float32)
    grad_head_boxes = jnp.zeros((patch_width, boxes_width), jnp.float32)
    grad_hbias_class = jnp.zeros((class_width,), jnp.float32)
    grad_hbias_boxes = jnp.zeros((boxes_width,), jnp.float32)
    total_moments = MICRO + section_count - 1
    empty_act = jnp.zeros(act_shape, jnp.bfloat16)
    received = (empty_act, empty_act)
    for moment in range(total_moments):
        micro_index = moment - section_index
        active = jnp.logical_and(micro_index >= 0, micro_index < MICRO)
        slot_index = jnp.clip(micro_index, 0, MICRO - 1)
        if moment < MICRO:
            entering = whole[moment * per_micro : (moment + 1) * per_micro]
        else:
            entering = empty_act
        input_class = jnp.where(is_first, entering, received[0])
        input_boxes = jnp.where(is_first, entering, received[1])
        kept_class = store(kept_class, input_class, slot_index, active)
        kept_boxes = store(kept_boxes, input_boxes, slot_index, active)
        pre_class = (
            jnp.dot(unfold(input_class), weight_class, preferred_element_type=jnp.float32)
            + layer_bias_class
        )
        pre_boxes = (
            jnp.dot(unfold(input_boxes), weight_boxes, preferred_element_type=jnp.float32)
            + layer_bias_boxes
        )
        kept_pre_class = store(kept_pre_class, pre_class, slot_index, active)
        kept_pre_boxes = store(kept_pre_boxes, pre_boxes, slot_index, active)
        act_class = jax.nn.gelu(pre_class).astype(jnp.bfloat16).reshape(act_shape)
        act_boxes = jax.nn.gelu(pre_boxes).astype(jnp.bfloat16).reshape(act_shape)
        results = lax.cond(
            jnp.logical_and(is_final, active),
            head_pass,
            head_spare,
            act_class,
            act_boxes,
            slot_index,
        )
        grad_head_class = grad_head_class + results[0]
        grad_head_boxes = grad_head_boxes + results[1]
        grad_hbias_class = grad_hbias_class + results[2]
        grad_hbias_boxes = grad_hbias_boxes + results[3]
        head_back_class = store(head_back_class, results[4], slot_index, active)
        head_back_boxes = store(head_back_boxes, results[5], slot_index, active)
        if moment < total_moments - 1:
            received = shifted((act_class, act_boxes), "section", 1)
    grad_layer_class = jnp.zeros((patch_width, channels), jnp.float32)
    grad_layer_boxes = jnp.zeros((patch_width, channels), jnp.float32)
    grad_lbias_class = jnp.zeros((channels,), jnp.float32)
    grad_lbias_boxes = jnp.zeros((channels,), jnp.float32)
    input_back = jnp.zeros((MICRO,) + act_shape, jnp.float32)
    returned = (empty_act, empty_act)
    for moment in range(total_moments):
        micro_index = moment - (final_section - section_index)
        active = jnp.logical_and(micro_index >= 0, micro_index < MICRO)
        slot_index = jnp.clip(micro_index, 0, MICRO - 1)
        upstream_class = jnp.where(
            is_final, pick(head_back_class, slot_index), returned[0].astype(jnp.float32)
        ).reshape(pixels, channels)
        upstream_boxes = jnp.where(
            is_final, pick(head_back_boxes, slot_index), returned[1].astype(jnp.float32)
        ).reshape(pixels, channels)
        cols_class = unfold(pick(kept_class, slot_index))
        cols_boxes = unfold(pick(kept_boxes, slot_index))
        pre_class = pick(kept_pre_class, slot_index)
        pre_boxes = pick(kept_pre_boxes, slot_index)
        gelu_class = jax.vjp(jax.nn.gelu, pre_class)[1](upstream_class)[0]
        gelu_boxes = jax.vjp(jax.nn.gelu, pre_boxes)[1](upstream_boxes)[0]
        grad_pre_class = jnp.where(active, gelu_class, 0.0).astype(jnp.bfloat16)
        grad_pre_boxes = jnp.where(active, gelu_boxes, 0.0).astype(jnp.bfloat16)
        grad_layer_class = grad_layer_class + weight_grad(cols_class, grad_pre_class)
        grad_layer_boxes = grad_layer_boxes + weight_grad(cols_boxes, grad_pre_boxes)
        grad_lbias_class = grad_lbias_class + jnp.sum(grad_pre_class.astype(jnp.float32), 0)
        grad_lbias_boxes = grad_lbias_boxes + jnp.sum(grad_pre_boxes.astype(jnp.float32), 0)
        back_class = fold_back(
            input_cols(grad_pre_class, weight_class), per_micro, tile_side, channels
        )
        back_boxes = fold_back(
            input_cols(grad_pre_boxes, weight_boxes), per_micro, tile_side, channels
        )
        input_back = store(
            input_back, back_class + back_boxes, slot_index, jnp.logical_and(active, is_first)
        )
        if moment < total_moments - 1:
            returned = shifted(
                (back_class.astype(jnp.bfloat16), back_boxes.astype(jnp.bfloat16)), "section", -1
            )
    spread_back = jnp.where(
        is_first, input_back.reshape(tile_dev, tile_side, tile_side, channels), 0.0
    )
    grad_features = lax.psum_scatter(
        spread_back.astype(jnp.bfloat16), "section", scatter_dimension=1, tiled=True
    )
    summed = (
        lax.psum_scatter(grad_layer_class, "dp", scatter_dimension=0, tiled=True),
        lax.psum_scatter(grad_layer_boxes, "dp", scatter_dimension=0, tiled=True),
        lax.psum_scatter(grad_head_class, "dp", scatter_dimension=0, tiled=True),
        lax.psum_scatter(grad_head_boxes, "dp", scatter_dimension=0, tiled=True),
    )
    final_head_class, final_head_boxes = (
        lax.psum_scatter(
            summed[2].astype(jnp.bfloat16), "section", scatter_dimension=1, tiled=True
        ).astype(jnp.float32),
        lax.psum_scatter(
            summed[3].astype(jnp.bfloat16), "section", scatter_dimension=1, tiled=True
        ).astype(jnp.float32),
    )
    rows_class = lax.dynamic_update_index_in_dim(
        jnp.zeros((LAYERS, channels), jnp.float32), grad_lbias_class, section_index, 0
    )
    rows_boxes = lax.dynamic_update_index_in_dim(
        jnp.zeros((LAYERS, channels), jnp.float32), grad_lbias_boxes, section_index, 0
    )
    bias_sums = lax.psum(
        (rows_class, rows_boxes, grad_hbias_class, grad_hbias_boxes), ("section", "dp")
    )
    return (
        grad_features,
        summed[0][None],
        bias_sums[0],
        summed[1][None],
        bias_sums[1],
        final_head_class,
        bias_sums[2],
        final_head_boxes,
        bias_sums[3],
    )


def solution(mesh):
    fits = mesh.shape["section"] == SECTIONS == LAYERS and mesh.shape["dp"] == PLANES * CORES
    placed = (
        P("dp", "section", None, None),
        P("section", "dp", None),
        P(),
        P("section", "dp", None),
        P(),
        P("dp", "section"),
        P(),
        P("dp", "section"),
        P(),
        P("dp", None, None),
        P("dp", None, None),
        P("dp", None, None),
        P("dp"),
    )
    return jax.shard_map(
        fast if fits else per_device,
        mesh=mesh,
        in_specs=placed,
        out_specs=(
            P("dp", "section", None, None),
            P("section", "dp", None),
            P(),
            P("section", "dp", None),
            P(),
            P("dp", "section"),
            P(),
            P("dp", "section"),
            P(),
        ),
        check_vma=False,
    )
```
